32 devices in a mesh: rep: 2 (over y), pair: 8 (over z, x), samp: 2 (over core).
Axes of the slice: x: 2, y: 2, z: 4, core: 2. Of those that a mesh axis runs over, the one named last changes fastest.
Arguments:
- dosage: bfloat16 [128, 4096], P(('rep', 'pair', 'samp')), parts along dimension 0, may hold values from 0 to 2
- phenotype: bfloat16 [2, 128], P(None, ('rep', 'pair', 'samp')), parts along dimension 1, may hold values from -6 to 6
- perms: int32 [2, 64], replicated, may hold values from 0 to 63, each once within a row
- pairs: int32 [8, 2], replicated, may hold values from 0 to 7
Outputs:
- stat: bfloat16 [16, 4, 512, 512], P(('rep', 'pair'), None, None, 'samp'), parts along dimension 0
The draws below stay inside these ranges and needn't reach their ends.
There are 2 independent parts, one for each index of `rep`. The reference program is written for one: setup_inputs(seed, part) draws one part's arguments, and reference() takes and returns one part's arrays. A program takes and returns all parts, laid end to end along the dimension named above; an argument that names none is the same for every part. Nothing has to cross between parts.
Inputs may be any that keep to these rules, and one draw needn't show every extreme that they name: `perms`: each row is a permutation of the samples. `pairs`: panel ids; a panel may appear in many blocks.
All inputs are finite; a program needn't handle non-finite values.
Results may differ from the reference program's by a relative error of at most 0.02.
Values may be sent and summed in bfloat16 or wider, within the bound.
No kernel may reach another device: no remote copies, remote signals or barrier semaphores. Data moves between devices by JAX's collectives and lax.ppermute only.
A program may use at most 64 MiB of HBM per device.

```python
import math
import jax
import jax.numpy as jnp
import numpy as np
from jax import lax

PANEL = 512
GENES = 2
PERMS = 2
NB = 8
NPANEL = 8
SNPS = 4096
SAMPLES = 64


def plant(drawn, rng, least, largest):
    dims = drawn.shape
    spot = [jax.random.randint(jax.random.fold_in(rng, axis), (), 0, dims[axis]) for axis in range(len(dims))]
    drawn = drawn.at[tuple(spot)].set(least)
    longest = dims.index(max(dims))
    spot[longest] = (spot[longest] + 1) % dims[longest]
    return drawn.at[tuple(spot)].set(largest)


def shard_levels(own_key, extent, shards, low, largest):
    level = 1.0
    for position, parts in shards:
        heights = jax.random.uniform(jax.random.fold_in(jax.random.fold_in(own_key, 6), position), (parts,), jnp.float32, low / len(shards), largest / len(shards))
        level = level * jnp.repeat(jnp.exp(heights), extent[position] // parts).reshape((-1,) + (1,) * (len(extent) - 1 - position))
    return level


def rank_bounds(number_of, slope):
    loads = [(1 << 20) // math.isqrt(standing ** slope) + 1 for standing in range(1, number_of + 1)]
    width = 1 + sum(loads) // (1 << 30)
    return np.cumsum(np.array([max(1, weight // width) for weight in loads]))


def ranked_ids(stream_key, shape, count, lean):
    listing = rank_bounds(count, lean)
    lot = jax.random.randint(jax.random.fold_in(stream_key, 1), shape, 0, int(listing[count - 1]))
    grade = jnp.searchsorted(jnp.asarray(listing, jnp.int32), lot, side="right")
    return jax.random.permutation(jax.random.fold_in(stream_key, 2), count)[grade].astype(jnp.int32)


def normal_values(rng, extent, scale, bound, cuts=(), dtype=jnp.bfloat16):
    values = jax.random.normal(rng, extent, jnp.float32) * scale
    if len(cuts) > 0:
        values = shard_levels(rng, extent, cuts, -0.22, 0.18) * values
    return jnp.clip(values, min=-bound, max=bound).astype(dtype)


def setup_inputs(seed: int = 0, part: int = 0) -> dict:
    streams_of = jax.random.split(jax.random.key(seed), 5)
    own_keys = jax.random.split(jax.random.fold_in(streams_of[4], part), 5)
    return {
        "dosage": jnp.clip(2.0 * jax.random.uniform(own_keys[0], (SAMPLES, SNPS), jnp.float32) ** shard_levels(own_keys[0], (SAMPLES, SNPS), ((0, 16),), -0.2, 0.2), 0.0, 2.0).astype(jnp.bfloat16),
        "phenotype": normal_values(own_keys[1], (GENES, SAMPLES), 1.0, 6.0, ((1, 16),)),
        "perms": jax.vmap(lambda own: jax.random.permutation(own, SAMPLES))(jax.random.split(streams_of[2], PERMS)).reshape((PERMS, SAMPLES)).astype(jnp.int32),
        "pairs": plant(ranked_ids(streams_of[3], (NB, 2), NPANEL, 2), jax.random.fold_in(streams_of[3], 3), 0, NPANEL - 1).astype(jnp.int32),
    }


def reference(dosage, phenotype, perms, pairs):
    total = dosage.shape[0]
    count = jnp.float32(total)
    pheno = phenotype.astype(jnp.float32)
    yperm = pheno[:, perms].reshape(GENES * PERMS, total)
    grouped = dosage.reshape(total, NPANEL, PANEL)

    def one_block(pair):
        geno_a = lax.dynamic_index_in_dim(grouped, pair[0], 1, keepdims=False).astype(jnp.float32)
        geno_b = lax.dynamic_index_in_dim(grouped, pair[1], 1, keepdims=False).astype(jnp.float32)
        scaled = (yperm[:, :, None] * geno_a[None]).astype(jnp.bfloat16).astype(jnp.float32)
        prod = jnp.einsum('ksi,sj->kij', scaled, geno_b, precision=lax.Precision.HIGHEST)
        ya = lax.optimization_barrier(jnp.sum(scaled, axis=1))
        yb = jnp.einsum('ks,sj->kj', yperm, geno_b, precision=lax.Precision.HIGHEST)
        marg_a = lax.optimization_barrier(jnp.sum(geno_a, axis=0))
        marg_b = lax.optimization_barrier(jnp.sum(geno_b, axis=0))
        ysum = lax.optimization_barrier(jnp.sum(yperm, axis=1))
        value = prod - ya[:, :, None] * marg_b[None, None, :] / count
        value = value - marg_a[None, :, None] * yb[:, None, :] / count
        value = value + marg_a[None, :, None] * marg_b[None, None, :] * ysum[:, None, None] / (count * count)
        return (value / jnp.sqrt(count)).astype(jnp.bfloat16)
    return lax.map(one_block, pairs)
```

```python
import functools
import math

import jax
import jax.numpy as jnp
from jax import lax
from jax.experimental import pallas as pl
from jax.experimental.pallas import tpu as pltpu
from jax.sharding import PartitionSpec as P

PANEL = 512
LANES = 128
TILE = 16


def pack_kernel(pairs_ref, pheno_ref, grid_ref, out_ref):
    genes, s_dev = pheno_ref.shape
    rows = TILE // 2
    pheno = pheno_ref[...].astype(jnp.float32)
    row = lax.broadcasted_iota(jnp.int32, (TILE, LANES), 0)
    lane = lax.broadcasted_iota(jnp.int32, (TILE, LANES), 1)
    block = jnp.zeros((TILE, LANES), jnp.float32)
    for g in range(genes):
        for s in range(s_dev):
            hit = (lane == g) & (lax.rem(row, rows) == s)
            block = jnp.where(hit, pheno[g : g + 1, s : s + 1], block)
    upper = row < rows

    @pl.loop(0, pairs_ref.shape[1], unroll=math.gcd(8, pairs_ref.shape[1]))
    def _(n):
        first = pl.multiple_of(pairs_ref[0, n] * TILE, TILE)
        second = pl.multiple_of(pairs_ref[1, n] * TILE, TILE)
        panel_a = grid_ref[pl.ds(first, TILE), :]
        panel_b = grid_ref[pl.ds(second, TILE), :].astype(jnp.float32)
        out_ref[2 * n, 0:TILE, :] = panel_a
        out_ref[2 * n + 1, 0:TILE, :] = panel_a
        out_ref[2 * n, TILE : 2 * TILE, :] = jnp.where(upper, panel_b, block).astype(out_ref.dtype)
        out_ref[2 * n + 1, TILE : 2 * TILE, :] = jnp.where(upper, block, panel_b).astype(out_ref.dtype)


def stat_kernel(genes, half_ref, perms_ref, got_ref, out_ref):
    sources = got_ref.shape[0]
    rperms, samples = perms_ref.shape
    s_dev = samples // sources
    first_half = half_ref[0] == 0

    def by_samples(tiles, group):
        return tiles[:, group * s_dev : (group + 1) * s_dev, :].reshape(samples, LANES)

    panel_a = got_ref[:, 0:TILE, :].astype(jnp.float32)
    mixed = got_ref[:, TILE : 2 * TILE, :].astype(jnp.float32)
    low, high = mixed[:, : TILE // 2], mixed[:, TILE // 2 :]
    tile_b = jnp.where(first_half, low, high)
    tile_y = jnp.where(first_half, high, low)

    count = jnp.float32(samples)
    geno_b = jnp.concatenate([by_samples(tile_b, q) for q in range(TILE // 2 // s_dev)], axis=1)
    marg_b = jnp.sum(geno_b, axis=0, keepdims=True)
    centred = (geno_b - marg_b / count) * (samples**-0.5)
    b_hi = centred.astype(jnp.bfloat16)
    b_lo = (centred - b_hi.astype(jnp.float32)).astype(jnp.bfloat16)
    b_both = jnp.concatenate([b_hi, b_lo], axis=0)

    pheno = by_samples(tile_y, 0)
    perms = perms_ref[...]
    twice = jnp.concatenate([perms, perms], axis=1)
    sample = lax.broadcasted_iota(jnp.int32, (samples, 2 * samples), 0)
    yrows = []
    for g in range(genes):
        column = pheno[:, g : g + 1]
        for r in range(rperms):
            chosen = jnp.where(sample == twice[r : r + 1, :], column, 0.0)
            yrows.append(jnp.sum(chosen, axis=0, keepdims=True))
    yall = jnp.concatenate(yrows, axis=0)
    tail = jnp.dot(yall.astype(jnp.bfloat16), b_both, preferred_element_type=jnp.float32) / count
    c_hi = tail.astype(jnp.bfloat16)
    c_lo = tail - c_hi.astype(jnp.float32)

    geno_a = jnp.concatenate([by_samples(panel_a, q) for q in range(TILE // s_dev)], axis=1)
    a_rows = jnp.concatenate([geno_a, geno_a], axis=0).T
    a_half = -a_rows.astype(jnp.bfloat16)
    for k in range(len(yrows)):
        scaled = (a_rows * yrows[k]).astype(jnp.bfloat16)
        left = jnp.concatenate([scaled, a_half], axis=1)
        right = jnp.concatenate(
            [
                b_both,
                jnp.broadcast_to(c_hi[k : k + 1, :].astype(jnp.float32), geno_b.shape).astype(jnp.bfloat16),
                jnp.broadcast_to(c_lo[k : k + 1, :], geno_b.shape).astype(jnp.bfloat16),
            ],
            axis=0,
        )
        out_ref[0, k] = jnp.dot(left, right, preferred_element_type=jnp.float32).astype(out_ref.dtype)


def on_device(dosage, phenotype, perms, pairs):
    s_dev, snps = dosage.shape
    genes = phenotype.shape[0]
    devices = lax.axis_size("pair") * lax.axis_size("samp")
    half = PANEL // lax.axis_size("samp")
    grid = dosage.reshape(s_dev, snps // LANES, LANES).transpose(1, 0, 2).reshape(-1, LANES)
    vmem = pl.BlockSpec(memory_space=pltpu.VMEM)
    smem = pl.BlockSpec(memory_space=pltpu.SMEM)
    messages = pl.pallas_call(
        pack_kernel,
        out_shape=jax.ShapeDtypeStruct((devices, 2 * TILE, LANES), dosage.dtype),
        in_specs=[smem, vmem, vmem],
        out_specs=vmem,
        name="pack",
    )(pairs.T, phenotype, grid)
    got = lax.all_to_all(messages, ("pair", "samp"), split_axis=0, concat_axis=0, tiled=True)
    which = lax.axis_index("samp").reshape(1).astype(jnp.int32)
    return pl.pallas_call(
        functools.partial(stat_kernel, genes),
        out_shape=jax.ShapeDtypeStruct((1, genes * perms.shape[0], PANEL, half), jnp.bfloat16),
        in_specs=[smem, vmem, vmem],
        out_specs=vmem,
        compiler_params=pltpu.CompilerParams(vmem_limit_bytes=48 * 1024 * 1024),
        name="stat",
    )(which, perms, got)


def solution(mesh):
    placed = (P(("rep", "pair", "samp"), None), P(None, ("rep", "pair", "samp")), P(), P())
    return jax.shard_map(
        on_device,
        mesh=mesh,
        in_specs=placed,
        out_specs=P(("rep", "pair"), None, None, "samp"),
        check_vma=False,
    )
```

```python
import functools

import jax
import jax.numpy as jnp
from jax import lax
from jax.experimental import pallas as pl
from jax.experimental.pallas import tpu as pltpu
from jax.sharding import PartitionSpec as P

PANEL = 512
LANES = 128
TILE = 16


def offsets(pair_count, samp_count):
    return [(p, s) for p in range(pair_count) for s in range(samp_count)]


def pack_kernel(counts, place_ref, pairs_ref, pheno_ref, grid_ref, *out_refs):
    genes, s_dev = pheno_ref.shape
    rows = TILE // 2
    pheno = pheno_ref[...].astype(jnp.float32)
    row = lax.broadcasted_iota(jnp.int32, (TILE, LANES), 0)
    lane = lax.broadcasted_iota(jnp.int32, (TILE, LANES), 1)
    block = jnp.zeros((TILE, LANES), jnp.float32)
    for g in range(genes):
        for s in range(s_dev):
            hit = (lane == g) & (lax.rem(row, rows) == s)
            block = jnp.where(hit, pheno[g : g + 1, s : s + 1], block)
    for out_ref, (p, s) in zip(out_refs, offsets(*counts)):
        n = lax.rem(place_ref[0] + p, counts[0])
        half = lax.rem(place_ref[1] + s, counts[1])
        first = pl.multiple_of(pairs_ref[0, n] * TILE, TILE)
        second = pl.multiple_of(pairs_ref[1, n] * TILE, TILE)
        panel_b = grid_ref[pl.ds(second, TILE), :].astype(jnp.float32)
        mine = row // rows == half
        out_ref[0:TILE, :] = grid_ref[pl.ds(first, TILE), :]
        out_ref[TILE : 2 * TILE, :] = jnp.where(mine, panel_b, block).astype(out_ref.dtype)


def stat_kernel(counts, genes, place_ref, perms_ref, *refs):
    *message_refs, out_ref, got_ref = refs
    for message_ref, (p, s) in zip(message_refs, offsets(*counts)):
        source_pair = lax.rem(place_ref[0] + (counts[0] - p), counts[0])
        source_samp = lax.rem(place_ref[1] + (counts[1] - s), counts[1])
        got_ref[source_pair * counts[1] + source_samp] = message_ref[...]
    sources = got_ref.shape[0]
    rperms, samples = perms_ref.shape
    s_dev = samples // sources
    first_half = place_ref[1] == 0

    def by_samples(tiles, group):
        return tiles[:, group * s_dev : (group + 1) * s_dev, :].reshape(samples, LANES)

    panel_a = got_ref[:, 0:TILE, :].astype(jnp.float32)
    mixed = got_ref[:, TILE : 2 * TILE, :].astype(jnp.float32)
    low, high = mixed[:, : TILE // 2], mixed[:, TILE // 2 :]
    tile_b = jnp.where(first_half, low, high)
    tile_y = jnp.where(first_half, high, low)

    count = jnp.float32(samples)
    geno_b = jnp.concatenate([by_samples(tile_b, q) for q in range(TILE // 2 // s_dev)], axis=1)
    marg_b = jnp.sum(geno_b, axis=0, keepdims=True)
    centred = (geno_b - marg_b / count) * (samples**-0.5)
    b_hi = centred.astype(jnp.bfloat16)
    b_lo = (centred - b_hi.astype(jnp.float32)).astype(jnp.bfloat16)
    b_both = jnp.concatenate([b_hi, b_lo], axis=0)

    pheno = by_samples(tile_y, 0)
    perms = perms_ref[...]
    twice = jnp.concatenate([perms, perms], axis=1)
    sample = lax.broadcasted_iota(jnp.int32, (samples, 2 * samples), 0)
    yrows = []
    for g in range(genes):
        column = pheno[:, g : g + 1]
        for r in range(rperms):
            chosen = jnp.where(sample == twice[r : r + 1, :], column, 0.0)
            yrows.append(jnp.sum(chosen, axis=0, keepdims=True))
    yall = jnp.concatenate(yrows, axis=0)
    tail = jnp.dot(yall.astype(jnp.bfloat16), b_both, preferred_element_type=jnp.float32) / count
    c_hi = tail.astype(jnp.bfloat16)
    c_lo = tail - c_hi.astype(jnp.float32)

    geno_a = jnp.concatenate([by_samples(panel_a, q) for q in range(TILE // s_dev)], axis=1)
    a_rows = jnp.concatenate([geno_a, geno_a], axis=0).T
    a_half = -a_rows.astype(jnp.bfloat16)
    for k in range(len(yrows)):
        scaled = (a_rows * yrows[k]).astype(jnp.bfloat16)
        left = jnp.concatenate([scaled, a_half], axis=1)
        right = jnp.concatenate(
            [
                b_both,
                jnp.broadcast_to(c_hi[k : k + 1, :].astype(jnp.float32), geno_b.shape).astype(jnp.bfloat16),
                jnp.broadcast_to(c_lo[k : k + 1, :], geno_b.shape).astype(jnp.bfloat16),
            ],
            axis=0,
        )
        out_ref[0, k] = jnp.dot(left, right, preferred_element_type=jnp.float32).astype(out_ref.dtype)


def on_device(dosage, phenotype, perms, pairs):
    s_dev, snps = dosage.shape
    genes = phenotype.shape[0]
    axes = ("pair", "samp")
    counts = tuple(lax.axis_size(axis) for axis in axes)
    devices = counts[0] * counts[1]
    half = PANEL // counts[1]
    grid = dosage.reshape(s_dev, snps // LANES, LANES).transpose(1, 0, 2).reshape(-1, LANES)
    place = jnp.stack([lax.axis_index(axis) for axis in axes]).astype(jnp.int32)
    vmem = pl.BlockSpec(memory_space=pltpu.VMEM)
    smem = pl.BlockSpec(memory_space=pltpu.SMEM)
    message = jax.ShapeDtypeStruct((2 * TILE, LANES), dosage.dtype)
    messages = pl.pallas_call(
        functools.partial(pack_kernel, counts),
        out_shape=[message] * devices,
        in_specs=[smem, smem, vmem, vmem],
        out_specs=[vmem] * devices,
        name="pack",
    )(place, pairs.T, phenotype, grid)
    got = []
    for message, (p, s) in zip(messages, offsets(*counts)):
        route = [
            (i * counts[1] + j, (i + p) % counts[0] * counts[1] + (j + s) % counts[1])
            for i, j in offsets(*counts)
        ]
        got.append(message if p == s == 0 else lax.ppermute(message, axes, route))
    return pl.pallas_call(
        functools.partial(stat_kernel, counts, genes),
        out_shape=jax.ShapeDtypeStruct((1, genes * perms.shape[0], PANEL, half), jnp.bfloat16),
        in_specs=[smem] + [vmem] * (1 + devices),
        out_specs=vmem,
        scratch_shapes=[pltpu.VMEM((devices, 2 * TILE, LANES), dosage.dtype)],
        compiler_params=pltpu.CompilerParams(vmem_limit_bytes=48 * 1024 * 1024),
        name="stat",
    )(place, perms, *got)


def solution(mesh):
    placed = (P(("rep", "pair", "samp"), None), P(None, ("rep", "pair", "samp")), P(), P())
    return jax.shard_map(
        on_device,
        mesh=mesh,
        in_specs=placed,
        out_specs=P(("rep", "pair"), None, None, "samp"),
        check_vma=False,
    )
```

```python
import functools

import jax
import jax.numpy as jnp
from jax import lax
from jax.experimental import pallas as pl
from jax.experimental.pallas import tpu as pltpu
from jax.sharding import PartitionSpec as P

PANEL = 512
LANES = 128
TILE = 16
BLOCK = 2 * TILE


def steps(pair_count):
    far = [1 << bit for bit in range(1, pair_count.bit_length() - 1)]
    return ([1] if pair_count > 1 else []) + far[::-1]


def distance(index, hops):
    return sum(hop for t, hop in enumerate(reversed(hops)) if index >> t & 1)


def wave_rows(genes, samples):
    return -(-genes * -(-samples // LANES) // TILE) * TILE


def pack_kernel(hops, samps, me_ref, pairs_ref, pheno_ref, grid_ref, keep_ref, send_ref, wave_ref):
    genes, s_dev = pheno_ref.shape
    me = me_ref[0]
    pair = lax.div(me, samps)
    half = keep_ref.shape[0]

    rows = wave_ref.shape[0]
    tiles = -(-s_dev * samps * 2 * half // LANES)
    pheno = pheno_ref[...].astype(jnp.float32)
    row = lax.broadcasted_iota(jnp.int32, (rows, LANES), 0)
    lane = lax.broadcasted_iota(jnp.int32, (rows, LANES), 1)
    wave = jnp.zeros((rows, LANES), jnp.float32)
    first_lane = lax.rem(me * s_dev, LANES)
    tile = lax.div(me * s_dev, LANES)
    for g in range(genes):
        for s in range(s_dev):
            hit = (lane == first_lane + s) & (row == g * tiles + tile)
            wave = jnp.where(hit, pheno[g : g + 1, s : s + 1], wave)
    wave_ref[...] = wave.astype(wave_ref.dtype)

    for j in range(2 * half):
        n = lax.bitwise_xor(pair, distance(j, hops))
        first = pl.multiple_of(pairs_ref[0, n] * TILE, TILE)
        second = pl.multiple_of(pairs_ref[1, n] * TILE, TILE)
        panel_a = grid_ref[pl.ds(first, TILE), :]
        panel_b = grid_ref[pl.ds(second, TILE), :]
        if j < half:
            keep_ref[j, 0:TILE, :] = panel_a
            keep_ref[j, TILE:BLOCK, :] = panel_b
        else:
            start = (j - half) * BLOCK
            send_ref[start : start + TILE, :] = panel_a
            send_ref[start + TILE : start + BLOCK, :] = panel_b
    send_ref[half * BLOCK :, :] = wave.astype(send_ref.dtype)


def stat_kernel(hops, samps, genes, me_ref, perms_ref, own_ref, other_ref, out_ref, got_ref):
    me = me_ref[0]
    pair = lax.div(me, samps)
    samp = lax.rem(me, samps)
    sources = got_ref.shape[0]
    pair_count = sources // samps
    for i in range(pair_count):
        source = lax.bitwise_xor(pair, distance(i, hops[::-1])) * samps
        rows = slice(i * BLOCK, (i + 1) * BLOCK)
        got_ref[source + samp] = own_ref[rows, :]
        got_ref[source + (samps - 1 - samp)] = other_ref[rows, :]
    rperms, samples = perms_ref.shape
    s_dev = samples // sources

    def by_samples(tiles, group):
        return tiles[:, group * s_dev : (group + 1) * s_dev, :].reshape(samples, LANES)

    panel_a = got_ref[:, 0:TILE, :].astype(jnp.float32)
    panel_b = got_ref[:, TILE:BLOCK, :].astype(jnp.float32)
    tile_b = jnp.where(samp == 0, panel_b[:, : TILE // 2], panel_b[:, TILE // 2 :])

    count = jnp.float32(samples)
    geno_b = jnp.concatenate([by_samples(tile_b, q) for q in range(TILE // 2 // s_dev)], axis=1)
    marg_b = jnp.sum(geno_b, axis=0, keepdims=True)
    centred = (geno_b - marg_b / count) * (samples**-0.5)
    b_hi = centred.astype(jnp.bfloat16)
    b_lo = (centred - b_hi.astype(jnp.float32)).astype(jnp.bfloat16)
    b_both = jnp.concatenate([b_hi, b_lo], axis=0)

    wave = own_ref[pair_count * BLOCK :, :].astype(jnp.float32)
    wave = wave + other_ref[pair_count * BLOCK :, :].astype(jnp.float32)
    tiles = -(-samples // LANES)
    pheno = [
        jnp.concatenate([wave[g * tiles + t : g * tiles + t + 1] for t in range(tiles)], axis=1)[:, :samples]
        for g in range(genes)
    ]
    pheno = jnp.concatenate(pheno, axis=0).astype(jnp.bfloat16)
    perms = perms_ref[...]
    twice = jnp.concatenate([perms, perms], axis=1)
    sample = lax.broadcasted_iota(jnp.int32, (samples, 2 * samples), 0)
    permuted = []
    for r in range(rperms):
        chosen = jnp.where(sample == twice[r : r + 1, :], 1.0, 0.0).astype(jnp.bfloat16)
        permuted.append(jnp.dot(pheno, chosen, preferred_element_type=jnp.float32))
    yrows = [permuted[r][g : g + 1] for g in range(genes) for r in range(rperms)]
    yall = jnp.concatenate(yrows, axis=0)
    tail = jnp.dot(yall.astype(jnp.bfloat16), b_both, preferred_element_type=jnp.float32) / count
    c_hi = tail.astype(jnp.bfloat16).astype(jnp.float32)
    c_lo = tail - c_hi

    geno_a = jnp.concatenate([by_samples(panel_a, q) for q in range(TILE // s_dev)], axis=1)
    a_rows = jnp.concatenate([geno_a, geno_a], axis=0).T
    a_minus = -a_rows.astype(jnp.bfloat16)
    for k in range(len(yrows)):
        scaled = (a_rows * yrows[k]).astype(jnp.bfloat16)
        left = jnp.concatenate([scaled, a_minus], axis=1)
        tails = [jnp.broadcast_to(c[k : k + 1], geno_b.shape).astype(jnp.bfloat16) for c in (c_hi, c_lo)]
        right = jnp.concatenate([b_both] + tails, axis=0)
        out_ref[0, k] = jnp.dot(left, right, preferred_element_type=jnp.float32).astype(out_ref.dtype)


def on_device(dosage, phenotype, perms, pairs):
    s_dev, snps = dosage.shape
    genes = phenotype.shape[0]
    samples = perms.shape[1]
    axes = ("pair", "samp")
    pair_count, samps = (lax.axis_size(axis) for axis in axes)
    hops = steps(pair_count)
    half = pair_count // 2
    rows = wave_rows(genes, samples)
    me = lax.axis_index(axes).astype(jnp.int32).reshape(1)
    grid = dosage.reshape(s_dev, snps // LANES, LANES).transpose(1, 0, 2).reshape(-1, LANES)
    vmem = pl.BlockSpec(memory_space=pltpu.VMEM)
    smem = pl.BlockSpec(memory_space=pltpu.SMEM)

    def array(*shape):
        return jax.ShapeDtypeStruct(shape, dosage.dtype)

    keep, send, wave = pl.pallas_call(
        functools.partial(pack_kernel, hops, samps),
        out_shape=[array(half, BLOCK, LANES), array(half * BLOCK + rows, LANES), array(rows, LANES)],
        in_specs=[smem, smem, vmem, vmem],
        out_specs=[vmem, vmem, vmem],
        compiler_params=pltpu.CompilerParams(vmem_limit_bytes=8 * 1024 * 1024),
        name="pack",
    )(me, pairs.T, phenotype, grid)

    held = [keep]
    for t, hop in enumerate(hops):
        route = [(i, i ^ hop) for i in range(pair_count)]
        left = pair_count >> (t + 1)
        if t > 0:
            send = jnp.concatenate([h[left:].reshape(-1, LANES) for h in held] + [wave], axis=0)
            held = [h[:left] for h in held]
        got = lax.ppermute(send, "pair", route)
        blocks = got[: half * BLOCK].reshape(len(held), left, BLOCK, LANES)
        held = held + [blocks[i] for i in range(len(held))]
        wave = wave + got[half * BLOCK :]
    own = jnp.concatenate([h.reshape(-1, LANES) for h in held] + [wave], axis=0)
    other = lax.ppermute(own, "samp", [(i, samps - 1 - i) for i in range(samps)])
    return pl.pallas_call(
        functools.partial(stat_kernel, hops, samps, genes),
        out_shape=jax.ShapeDtypeStruct((1, genes * perms.shape[0], PANEL, PANEL // samps), jnp.bfloat16),
        in_specs=[smem, vmem, vmem, vmem],
        out_specs=vmem,
        scratch_shapes=[pltpu.VMEM((pair_count * samps, BLOCK, LANES), dosage.dtype)],
        compiler_params=pltpu.CompilerParams(vmem_limit_bytes=48 * 1024 * 1024),
        name="stat",
    )(me, perms, own, other)


def solution(mesh):
    placed = (P(("rep", "pair", "samp"), None), P(None, ("rep", "pair", "samp")), P(), P())
    return jax.shard_map(
        on_device,
        mesh=mesh,
        in_specs=placed,
        out_specs=P(("rep", "pair"), None, None, "samp"),
        check_vma=False,
    )
```

```python
import functools

import jax
import jax.numpy as jnp
from jax import lax
from jax.experimental import pallas as pl
from jax.experimental.pallas import tpu as pltpu
from jax.sharding import PartitionSpec as P

PANEL = 512
LANES = 128
TILE = 16
BLOCK = 2 * TILE


def offset(pair_count, core, i):
    return pair_count - 2 - 2 * i + core


def wave_rows(genes, samples):
    return -(-genes * -(-samples // LANES) // TILE) * TILE


def pack_kernel(pair_count, samps, me_ref, pairs_ref, pheno_ref, mate_pheno_ref, grid_ref, mate_grid_ref, *out_refs):
    genes, s_dev = pheno_ref.shape
    me = me_ref[0]
    pair = lax.div(me, samps)
    samp = lax.rem(me, samps)

    rows = out_refs[0].shape[0] - samps * BLOCK
    tiles = -(-s_dev * samps * pair_count // LANES)
    row = lax.broadcasted_iota(jnp.int32, (rows, LANES), 0)
    lane = lax.broadcasted_iota(jnp.int32, (rows, LANES), 1)
    wave = jnp.zeros((rows, LANES), jnp.float32)
    for ref, core in ((pheno_ref, samp), (mate_pheno_ref, samps - 1 - samp)):
        pheno = ref[...].astype(jnp.float32)
        spot = (pair * samps + core) * s_dev
        first = lax.rem(spot, LANES)
        tile = lax.div(spot, LANES)
        for g in range(genes):
            for s in range(s_dev):
                hit = (lane == first + s) & (row == g * tiles + tile)
                wave = jnp.where(hit, pheno[g : g + 1, s : s + 1], wave)
    wave = wave.astype(out_refs[0].dtype)

    for i, out_ref in enumerate(out_refs):
        n = lax.bitwise_xor(pair, offset(pair_count, samp, i))
        first = pl.multiple_of(pairs_ref[0, n] * TILE, TILE)
        second = pl.multiple_of(pairs_ref[1, n] * TILE, TILE)
        for core, ref in enumerate((grid_ref, mate_grid_ref)):
            out_ref[core * BLOCK : core * BLOCK + TILE, :] = ref[pl.ds(first, TILE), :]
            out_ref[core * BLOCK + TILE : (core + 1) * BLOCK, :] = ref[pl.ds(second, TILE), :]
        out_ref[samps * BLOCK :, :] = wave


def stat_kernel(samps, genes, me_ref, perms_ref, own_ref, mate_ref, out_ref, got_ref):
    me = me_ref[0]
    pair = lax.div(me, samps)
    samp = lax.rem(me, samps)
    sources = got_ref.shape[0]
    pair_count = sources // samps
    size = samps * BLOCK
    for ref, core in ((own_ref, samp), (mate_ref, samps - 1 - samp)):
        for i in range(pair_count // samps):
            source = lax.bitwise_xor(pair, offset(pair_count, core, i)) * samps
            got_ref[source + core] = ref[i * size : i * size + BLOCK, :]
            got_ref[source + (samps - 1 - core)] = ref[i * size + BLOCK : (i + 1) * size, :]
    end = pair_count // samps * size
    rperms, samples = perms_ref.shape
    s_dev = samples // sources

    def by_samples(tiles, group):
        return tiles[:, group * s_dev : (group + 1) * s_dev, :].reshape(samples, LANES)

    panel_a = got_ref[:, 0:TILE, :].astype(jnp.float32)
    panel_b = got_ref[:, TILE:BLOCK, :].astype(jnp.float32)
    tile_b = jnp.where(samp == 0, panel_b[:, : TILE // 2], panel_b[:, TILE // 2 :])

    count = jnp.float32(samples)
    geno_b = jnp.concatenate([by_samples(tile_b, q) for q in range(TILE // 2 // s_dev)], axis=1)
    marg_b = jnp.sum(geno_b, axis=0, keepdims=True)
    centred = (geno_b - marg_b / count) * (samples**-0.5)
    b_hi = centred.astype(jnp.bfloat16)
    b_lo = (centred - b_hi.astype(jnp.float32)).astype(jnp.bfloat16)
    b_both = jnp.concatenate([b_hi, b_lo], axis=0)

    wave = own_ref[end:, :].astype(jnp.float32)
    wave = wave + mate_ref[end:, :].astype(jnp.float32)
    tiles = -(-samples // LANES)
    pheno = [
        jnp.concatenate([wave[g * tiles + t : g * tiles + t + 1] for t in range(tiles)], axis=1)[:, :samples]
        for g in range(genes)
    ]
    pheno = jnp.concatenate(pheno, axis=0).astype(jnp.bfloat16)
    perms = perms_ref[...]
    twice = jnp.concatenate([perms, perms], axis=1)
    sample = lax.broadcasted_iota(jnp.int32, (samples, 2 * samples), 0)
    permuted = []
    for r in range(rperms):
        chosen = jnp.where(sample == twice[r : r + 1, :], 1.0, 0.0).astype(jnp.bfloat16)
        permuted.append(jnp.dot(pheno, chosen, preferred_element_type=jnp.float32))
    yrows = [permuted[r][g : g + 1] for g in range(genes) for r in range(rperms)]
    yall = jnp.concatenate(yrows, axis=0)
    tail = jnp.dot(yall.astype(jnp.bfloat16), b_both, preferred_element_type=jnp.float32) / count
    c_hi = tail.astype(jnp.bfloat16).astype(jnp.float32)
    c_lo = tail - c_hi

    geno_a = jnp.concatenate([by_samples(panel_a, q) for q in range(TILE // s_dev)], axis=1)
    a_rows = jnp.concatenate([geno_a, geno_a], axis=0).T
    a_minus = -a_rows.astype(jnp.bfloat16)
    for k in range(len(yrows)):
        scaled = (a_rows * yrows[k]).astype(jnp.bfloat16)
        left = jnp.concatenate([scaled, a_minus], axis=1)
        tails = [jnp.broadcast_to(c[k : k + 1], geno_b.shape).astype(jnp.bfloat16) for c in (c_hi, c_lo)]
        right = jnp.concatenate([b_both] + tails, axis=0)
        out_ref[0, k] = jnp.dot(left, right, preferred_element_type=jnp.float32).astype(out_ref.dtype)


def on_device(dosage, phenotype, perms, pairs):
    s_dev, snps = dosage.shape
    genes = phenotype.shape[0]
    samples = perms.shape[1]
    axes = ("pair", "samp")
    pair_count, samps = (lax.axis_size(axis) for axis in axes)
    size = samps * BLOCK
    me = lax.axis_index(axes).astype(jnp.int32).reshape(1)
    swap = [(i, samps - 1 - i) for i in range(samps)]
    mate_dosage = lax.ppermute(dosage, "samp", swap)
    mate_pheno = lax.ppermute(phenotype, "samp", swap)

    def grid(x):
        return x.reshape(s_dev, snps // LANES, LANES).transpose(1, 0, 2).reshape(-1, LANES)

    vmem = pl.BlockSpec(memory_space=pltpu.VMEM)
    smem = pl.BlockSpec(memory_space=pltpu.SMEM)
    message = jax.ShapeDtypeStruct((size + wave_rows(genes, samples), LANES), dosage.dtype)
    messages = pl.pallas_call(
        functools.partial(pack_kernel, pair_count, samps),
        out_shape=[message] * (pair_count // samps),
        in_specs=[smem, smem, vmem, vmem, vmem, vmem],
        out_specs=[vmem] * (pair_count // samps),
        compiler_params=pltpu.CompilerParams(vmem_limit_bytes=8 * 1024 * 1024),
        name="pack",
    )(me, pairs.T, phenotype, mate_pheno, grid(dosage), grid(mate_dosage))

    got = []
    for i, message in enumerate(messages):
        route = [
            (p * samps + c, (p ^ offset(pair_count, c, i)) * samps + c)
            for p in range(pair_count)
            for c in range(samps)
        ]
        got.append(lax.ppermute(message, axes, route))
    own = jnp.concatenate([g[:size] for g in got] + [sum(g[size:] for g in got)], axis=0)
    mate = lax.ppermute(own, "samp", swap)
    return pl.pallas_call(
        functools.partial(stat_kernel, samps, genes),
        out_shape=jax.ShapeDtypeStruct((1, genes * perms.shape[0], PANEL, PANEL // samps), jnp.bfloat16),
        in_specs=[smem, vmem, vmem, vmem],
        out_specs=vmem,
        scratch_shapes=[pltpu.VMEM((pair_count * samps, BLOCK, LANES), dosage.dtype)],
        compiler_params=pltpu.CompilerParams(vmem_limit_bytes=48 * 1024 * 1024),
        name="stat",
    )(me, perms, own, mate)


def solution(mesh):
    placed = (P(("rep", "pair", "samp"), None), P(None, ("rep", "pair", "samp")), P(), P())
    return jax.shard_map(
        on_device,
        mesh=mesh,
        in_specs=placed,
        out_specs=P(("rep", "pair"), None, None, "samp"),
        check_vma=False,
    )
```

```python
import functools

import jax
import jax.numpy as jnp
from jax import lax
from jax.experimental import pallas as pl
from jax.experimental.pallas import tpu as pltpu
from jax.sharding import PartitionSpec as P

PANEL = 512
LANES = 128
TILE = 16
BLOCK = 2 * TILE


def wave_rows(genes, samples):
    return -(-genes * -(-samples // LANES) // TILE) * TILE


def pack_kernel(samples, me_ref, pheno_ref, grid_ref, out_ref):
    genes, s_dev = pheno_ref.shape
    panels = grid_ref.shape[0]
    tiles = -(-samples // LANES)
    shape = (out_ref.shape[0] - panels, LANES)
    row = lax.broadcasted_iota(jnp.int32, shape, 0)
    lane = lax.broadcasted_iota(jnp.int32, shape, 1)
    wave = jnp.zeros(shape, jnp.float32)
    pheno = pheno_ref[...].astype(jnp.float32)
    first = lax.rem(me_ref[0] * s_dev, LANES)
    tile = lax.div(me_ref[0] * s_dev, LANES)
    for g in range(genes):
        for s in range(s_dev):
            hit = (lane == first + s) & (row == g * tiles + tile)
            wave = jnp.where(hit, pheno[g : g + 1, s : s + 1], wave)
    out_ref[:panels] = grid_ref[...]
    out_ref[panels:] = wave.astype(out_ref.dtype)


def stat_kernel(samps, genes, me_ref, pairs_ref, perms_ref, all_ref, out_ref, a_ref, b_ref, wave_ref, sems):
    me = me_ref[0]
    pair = lax.div(me, samps)
    samp = lax.rem(me, samps)
    sources, rows, _ = all_ref.shape
    tail = rows - wave_ref.shape[1]
    copies = []
    for i, ref in enumerate((a_ref, b_ref)):
        first = pl.multiple_of(pairs_ref[i, pair] * TILE, TILE)
        copies.append(pltpu.make_async_copy(all_ref.at[:, pl.ds(first, TILE)], ref, sems.at[i]))
    copies.append(pltpu.make_async_copy(all_ref.at[:, tail:], wave_ref, sems.at[2]))
    for copy in copies:
        copy.start()
    for copy in copies:
        copy.wait()
    rperms, samples = perms_ref.shape
    s_dev = samples // sources

    def by_samples(tiles, group):
        return tiles[:, group * s_dev : (group + 1) * s_dev, :].reshape(samples, LANES)

    panel_a = a_ref[...].astype(jnp.float32)
    panel_b = b_ref[...].astype(jnp.float32)
    tile_b = jnp.where(samp == 0, panel_b[:, : TILE // 2], panel_b[:, TILE // 2 :])

    count = jnp.float32(samples)
    geno_b = jnp.concatenate([by_samples(tile_b, q) for q in range(TILE // 2 // s_dev)], axis=1)
    marg_b = jnp.sum(geno_b, axis=0, keepdims=True)
    centred = (geno_b - marg_b / count) * (samples**-0.5)
    b_hi = centred.astype(jnp.bfloat16)
    b_lo = (centred - b_hi.astype(jnp.float32)).astype(jnp.bfloat16)
    b_both = jnp.concatenate([b_hi, b_lo], axis=0)

    wave = jnp.sum(wave_ref[...].astype(jnp.float32), axis=0)
    tiles = -(-samples // LANES)
    pheno = [
        jnp.concatenate([wave[g * tiles + t : g * tiles + t + 1] for t in range(tiles)], axis=1)[:, :samples]
        for g in range(genes)
    ]
    pheno = jnp.concatenate(pheno, axis=0).astype(jnp.bfloat16)
    perms = perms_ref[...]
    twice = jnp.concatenate([perms, perms], axis=1)
    sample = lax.broadcasted_iota(jnp.int32, (samples, 2 * samples), 0)
    permuted = []
    for r in range(rperms):
        chosen = jnp.where(sample == twice[r : r + 1, :], 1.0, 0.0).astype(jnp.bfloat16)
        permuted.append(jnp.dot(pheno, chosen, preferred_element_type=jnp.float32))
    yrows = [permuted[r][g : g + 1] for g in range(genes) for r in range(rperms)]
    yall = jnp.concatenate(yrows, axis=0)
    tail = jnp.dot(yall.astype(jnp.bfloat16), b_both, preferred_element_type=jnp.float32) / count
    c_hi = tail.astype(jnp.bfloat16).astype(jnp.float32)
    c_lo = tail - c_hi

    geno_a = jnp.concatenate([by_samples(panel_a, q) for q in range(TILE // s_dev)], axis=1)
    a_rows = jnp.concatenate([geno_a, geno_a], axis=0).T
    a_minus = -a_rows.astype(jnp.bfloat16)
    for k in range(len(yrows)):
        scaled = (a_rows * yrows[k]).astype(jnp.bfloat16)
        left = jnp.concatenate([scaled, a_minus], axis=1)
        tails = [jnp.broadcast_to(c[k : k + 1], geno_b.shape).astype(jnp.bfloat16) for c in (c_hi, c_lo)]
        right = jnp.concatenate([b_both] + tails, axis=0)
        out_ref[0, k] = jnp.dot(left, right, preferred_element_type=jnp.float32).astype(out_ref.dtype)


def on_device(dosage, phenotype, perms, pairs):
    s_dev, snps = dosage.shape
    genes = phenotype.shape[0]
    samples = perms.shape[1]
    axes = ("pair", "samp")
    pair_count, samps = (lax.axis_size(axis) for axis in axes)
    me = lax.axis_index(axes).astype(jnp.int32).reshape(1)
    grid = dosage.reshape(s_dev, snps // LANES, LANES).transpose(1, 0, 2).reshape(-1, LANES)
    vmem = pl.BlockSpec(memory_space=pltpu.VMEM)
    smem = pl.BlockSpec(memory_space=pltpu.SMEM)
    rows = wave_rows(genes, samples)
    own = pl.pallas_call(
        functools.partial(pack_kernel, samples),
        out_shape=jax.ShapeDtypeStruct((grid.shape[0] + rows, LANES), dosage.dtype),
        in_specs=[smem, vmem, vmem],
        out_specs=vmem,
        name="pack",
    )(me, phenotype, grid)
    everyone = lax.all_gather(own, axes, axis=0)
    sources = pair_count * samps
    return pl.pallas_call(
        functools.partial(stat_kernel, samps, genes),
        out_shape=jax.ShapeDtypeStruct((1, genes * perms.shape[0], PANEL, PANEL // samps), jnp.bfloat16),
        in_specs=[smem, smem, vmem, pl.BlockSpec(memory_space=pl.ANY)],
        out_specs=vmem,
        scratch_shapes=[
            pltpu.VMEM((sources, TILE, LANES), dosage.dtype),
            pltpu.VMEM((sources, TILE, LANES), dosage.dtype),
            pltpu.VMEM((sources, rows, LANES), dosage.dtype),
            pltpu.SemaphoreType.DMA((3,)),
        ],
        compiler_params=pltpu.CompilerParams(vmem_limit_bytes=48 * 1024 * 1024),
        name="stat",
    )(me, pairs.T, perms, everyone)


def solution(mesh):
    placed = (P(("rep", "pair", "samp"), None), P(None, ("rep", "pair", "samp")), P(), P())
    return jax.shard_map(
        on_device,
        mesh=mesh,
        in_specs=placed,
        out_specs=P(("rep", "pair"), None, None, "samp"),
        check_vma=False,
    )
```

```python
import functools

import jax
import jax.numpy as jnp
from jax import lax
from jax.experimental import pallas as pl
from jax.experimental.pallas import tpu as pltpu
from jax.sharding import PartitionSpec as P

PANEL = 512
LANES = 128
TILE = 16
BLOCK = 2 * TILE


def offset(pair_count, core, i):
    return pair_count - 2 - 2 * i + core


def wave_rows(genes, samples):
    return -(-genes * -(-samples // LANES) // TILE) * TILE


def pack_kernel(pair_count, samps, me_ref, pairs_ref, pheno_ref, mate_pheno_ref, grid_ref, mate_grid_ref, *out_refs):
    genes, s_dev = pheno_ref.shape
    me = me_ref[0]
    pair = lax.div(me, samps)
    samp = lax.rem(me, samps)

    rows = out_refs[0].shape[0] - samps * BLOCK
    tiles = -(-s_dev * samps * pair_count // LANES)
    row = lax.broadcasted_iota(jnp.int32, (rows, LANES), 0)
    lane = lax.broadcasted_iota(jnp.int32, (rows, LANES), 1)
    wave = jnp.zeros((rows, LANES), jnp.float32)
    for ref, core in ((pheno_ref, samp), (mate_pheno_ref, samps - 1 - samp)):
        pheno = ref[...].astype(jnp.float32)
        spot = (pair * samps + core) * s_dev
        first = lax.rem(spot, LANES)
        tile = lax.div(spot, LANES)
        for g in range(genes):
            for s in range(s_dev):
                hit = (lane == first + s) & (row == g * tiles + tile)
                wave = jnp.where(hit, pheno[g : g + 1, s : s + 1], wave)
    wave = wave.astype(out_refs[0].dtype)

    for i, out_ref in enumerate(out_refs):
        n = lax.bitwise_xor(pair, offset(pair_count, samp, i))
        first = pl.multiple_of(pairs_ref[0, n] * TILE, TILE)
        second = pl.multiple_of(pairs_ref[1, n] * TILE, TILE)
        for core, ref in enumerate((grid_ref, mate_grid_ref)):
            out_ref[core * BLOCK : core * BLOCK + TILE, :] = ref[pl.ds(first, TILE), :]
            out_ref[core * BLOCK + TILE : (core + 1) * BLOCK, :] = ref[pl.ds(second, TILE), :]
        out_ref[samps * BLOCK :, :] = wave


def stat_kernel(samps, genes, me_ref, perms_ref, own_ref, mate_ref, out_ref, got_ref):
    me = me_ref[0]
    pair = lax.div(me, samps)
    samp = lax.rem(me, samps)
    sources = got_ref.shape[0]
    pair_count = sources // samps
    size = samps * BLOCK
    for ref, core in ((own_ref, samp), (mate_ref, samps - 1 - samp)):
        for i in range(pair_count // samps):
            source = lax.bitwise_xor(pair, offset(pair_count, core, i)) * samps
            got_ref[source + core] = ref[i * size : i * size + BLOCK, :]
            got_ref[source + (samps - 1 - core)] = ref[i * size + BLOCK : (i + 1) * size, :]
    end = pair_count // samps * size
    rperms, samples = perms_ref.shape
    s_dev = samples // sources

    def by_samples(tiles, group):
        return tiles[:, group * s_dev : (group + 1) * s_dev, :].reshape(samples, LANES)

    panel_a = got_ref[:, 0:TILE, :].astype(jnp.float32)
    panel_b = got_ref[:, TILE:BLOCK, :].astype(jnp.float32)
    tile_b = jnp.where(samp == 0, panel_b[:, : TILE // 2], panel_b[:, TILE // 2 :])

    count = jnp.float32(samples)
    geno_b = jnp.concatenate([by_samples(tile_b, q) for q in range(TILE // 2 // s_dev)], axis=1)
    marg_b = jnp.sum(geno_b, axis=0, keepdims=True)
    centred = (geno_b - marg_b / count) * (samples**-0.5)
    b_hi = centred.astype(jnp.bfloat16)
    b_lo = (centred - b_hi.astype(jnp.float32)).astype(jnp.bfloat16)
    b_both = jnp.concatenate([b_hi, b_lo], axis=0)

    wave = own_ref[end:, :].astype(jnp.float32)
    wave = wave + mate_ref[end:, :].astype(jnp.float32)
    tiles = -(-samples // LANES)
    pheno = [
        jnp.concatenate([wave[g * tiles + t : g * tiles + t + 1] for t in range(tiles)], axis=1)[:, :samples]
        for g in range(genes)
    ]
    pheno = jnp.concatenate(pheno, axis=0).astype(jnp.bfloat16)
    perms = perms_ref[...]
    twice = jnp.concatenate([perms, perms], axis=1)
    sample = lax.broadcasted_iota(jnp.int32, (samples, 2 * samples), 0)
    permuted = []
    for r in range(rperms):
        chosen = jnp.where(sample == twice[r : r + 1, :], 1.0, 0.0).astype(jnp.bfloat16)
        permuted.append(jnp.dot(pheno, chosen, preferred_element_type=jnp.float32))
    yrows = [permuted[r][g : g + 1] for g in range(genes) for r in range(rperms)]
    yall = jnp.concatenate(yrows, axis=0)
    tail = jnp.dot(yall.astype(jnp.bfloat16), b_both, preferred_element_type=jnp.float32) / count
    c_hi = tail.astype(jnp.bfloat16).astype(jnp.float32)
    c_lo = tail - c_hi

    geno_a = jnp.concatenate([by_samples(panel_a, q) for q in range(TILE // s_dev)], axis=1)
    a_rows = jnp.concatenate([geno_a, geno_a], axis=0).T
    a_minus = -a_rows.astype(jnp.bfloat16)
    for k in range(len(yrows)):
        scaled = (a_rows * yrows[k]).astype(jnp.bfloat16)
        left = jnp.concatenate([scaled, a_minus], axis=1)
        tails = [jnp.broadcast_to(c[k : k + 1], geno_b.shape).astype(jnp.bfloat16) for c in (c_hi, c_lo)]
        right = jnp.concatenate([b_both] + tails, axis=0)
        out_ref[0, k] = jnp.dot(left, right, preferred_element_type=jnp.float32).astype(out_ref.dtype)


def on_device(dosage, phenotype, perms, pairs):
    s_dev, snps = dosage.shape
    genes = phenotype.shape[0]
    samples = perms.shape[1]
    axes = ("pair", "samp")
    pair_count, samps = (lax.axis_size(axis) for axis in axes)
    size = samps * BLOCK
    me = lax.axis_index(axes).astype(jnp.int32).reshape(1)
    swap = [(i, samps - 1 - i) for i in range(samps)]
    mate_dosage = lax.ppermute(dosage, "samp", swap)
    mate_pheno = lax.ppermute(phenotype, "samp", swap)

    def grid(x):
        return x.reshape(s_dev, snps // LANES, LANES).transpose(1, 0, 2).reshape(-1, LANES)

    vmem = pl.BlockSpec(memory_space=pltpu.VMEM)
    smem = pl.BlockSpec(memory_space=pltpu.SMEM)
    message = jax.ShapeDtypeStruct((size + wave_rows(genes, samples), LANES), dosage.dtype)
    messages = pl.pallas_call(
        functools.partial(pack_kernel, pair_count, samps),
        out_shape=[message] * (pair_count // samps),
        in_specs=[smem, smem, vmem, vmem, vmem, vmem],
        out_specs=[vmem] * (pair_count // samps),
        name="pack",
    )(me, pairs.T, phenotype, mate_pheno, grid(dosage), grid(mate_dosage))

    got = []
    for i, message in enumerate(messages):
        route = [
            (p * samps + c, (p ^ offset(pair_count, c, i)) * samps + c)
            for p in range(pair_count)
            for c in range(samps)
        ]
        got.append(lax.ppermute(message, axes, route))
    own = jnp.concatenate([g[:size] for g in got] + [sum(g[size:] for g in got)], axis=0)
    mate = lax.ppermute(own, "samp", swap)
    return pl.pallas_call(
        functools.partial(stat_kernel, samps, genes),
        out_shape=jax.ShapeDtypeStruct((1, genes * perms.shape[0], PANEL, PANEL // samps), jnp.bfloat16),
        in_specs=[smem, vmem, vmem, vmem],
        out_specs=vmem,
        scratch_shapes=[pltpu.VMEM((pair_count * samps, BLOCK, LANES), dosage.dtype)],
        compiler_params=pltpu.CompilerParams(vmem_limit_bytes=48 * 1024 * 1024),
        name="stat",
    )(me, perms, own, mate)


def solution(mesh):
    placed = (P(("rep", "pair", "samp"), None), P(None, ("rep", "pair", "samp")), P(), P())
    return jax.shard_map(
        on_device,
        mesh=mesh,
        in_specs=placed,
        out_specs=P(("rep", "pair"), None, None, "samp"),
        check_vma=False,
    )
```

```python
import functools

import jax
import jax.numpy as jnp
from jax import lax
from jax.experimental import pallas as pl
from jax.experimental.pallas import tpu as pltpu
from jax.sharding import PartitionSpec as P

PANEL = 512
LANES = 128
TILE = 16
BLOCK = 2 * TILE
AXES = ("pair", "samp")


def offsets(pair_count, core):
    return [2 * i + core for i in range(pair_count // 2 - 1, 0, -1)] + [1, 0]


def wave_rows(genes, samples):
    return -(-genes * -(-samples // LANES) // 8) * 8


def pack_kernel(pair_count, samps, pairs_hbm, pheno_hbm, grid_hbm, keep_ref, give_ref, wave_ref, pairs_ref, pheno_ref, grid_ref, sems):
    copies = [
        pltpu.make_async_copy(source, target, sems.at[i])
        for i, (source, target) in enumerate(((pairs_hbm, pairs_ref), (grid_hbm, grid_ref), (pheno_hbm, pheno_ref)))
    ]
    for copy in copies:
        copy.start()
    pair, samp = lax.axis_index("pair"), lax.axis_index("samp")
    genes, s_dev = pheno_ref.shape
    rows = wave_ref.shape[0]
    tiles = -(-s_dev * samps * pair_count // LANES)
    row = lax.broadcasted_iota(jnp.int32, (rows, LANES), 0)
    lane = lax.broadcasted_iota(jnp.int32, (rows, LANES), 1)
    spot = (pair * samps + samp) * s_dev
    first, tile = lax.rem(spot, LANES), lax.div(spot, LANES)
    for copy in copies:
        copy.wait()

    pheno = pheno_ref[...].astype(jnp.float32)
    wave = jnp.zeros((rows, LANES), jnp.float32)
    for g in range(genes):
        for s in range(s_dev):
            hit = (lane == first + s) & (row == g * tiles + tile)
            wave = jnp.where(hit, pheno[g : g + 1, s : s + 1], wave)
    wave = wave.astype(wave_ref.dtype)
    wave_ref[...] = wave

    own_side, far_side = offsets(pair_count, 0), offsets(pair_count, 1)
    for i, (even, odd) in enumerate(zip(own_side, far_side)):
        for ref, core in ((keep_ref, samp), (give_ref, samps - 1 - samp)):
            n = lax.bitwise_xor(pair, even + (odd - even) * core)
            for j in range(2):
                start = pl.multiple_of(pairs_ref[j, n] * TILE, TILE)
                place = i * BLOCK + j * TILE
                ref[place : place + TILE, :] = grid_ref[pl.ds(start, TILE), :]
    give_ref[len(own_side) * BLOCK :, :] = wave


def stat_kernel(
    pair_count, samps, perms_ref, keep_ref, give_ref, own_ref, mate_ref, near_ref, wave_ref, out_hbm, got_ref, out_ref, sems
):
    pair, samp = lax.axis_index("pair"), lax.axis_index("samp")
    other = samps - 1 - samp
    far = pair_count // 2 - 1

    def place(offset, core, block):
        got_ref[lax.bitwise_xor(pair, offset) * samps + core] = block

    for ref, core in ((own_ref, samp), (mate_ref, other)):
        for i in range(far):
            offset = 2 * (far - i) + core
            start = 2 * i * BLOCK
            place(offset, core, ref[start : start + BLOCK, :])
            place(offset, samps - 1 - core, ref[start + BLOCK : start + 2 * BLOCK, :])
    place(1, samp, near_ref[:BLOCK, :])
    place(1, other, near_ref[BLOCK : 2 * BLOCK, :])
    itself = (far + 1) * BLOCK
    place(0, samp, keep_ref[itself : itself + BLOCK, :])
    place(0, other, give_ref[itself : itself + BLOCK, :])

    sources = got_ref.shape[0]
    rperms, samples = perms_ref.shape
    s_dev = samples // sources

    def by_samples(tiles, group):
        return tiles[:, group * s_dev : (group + 1) * s_dev, :].reshape(samples, LANES)

    panel_a = got_ref[:, 0:TILE, :].astype(jnp.float32)
    panel_b = got_ref[:, TILE:BLOCK, :].astype(jnp.float32)
    tile_b = jnp.where(samp == 0, panel_b[:, : TILE // 2], panel_b[:, TILE // 2 :])

    count = jnp.float32(samples)
    geno_b = jnp.concatenate([by_samples(tile_b, q) for q in range(TILE // 2 // s_dev)], axis=1)
    marg_b = jnp.sum(geno_b, axis=0, keepdims=True)
    centred = (geno_b - marg_b / count) * (samples**-0.5)
    b_hi = centred.astype(jnp.bfloat16)
    b_lo = (centred - b_hi.astype(jnp.float32)).astype(jnp.bfloat16)
    b_both = jnp.concatenate([b_hi, b_lo], axis=0)

    wave = wave_ref[...].astype(jnp.float32)
    genes = out_ref.shape[0] // rperms
    tiles = -(-samples // LANES)
    pheno = [
        jnp.concatenate([wave[g * tiles + t : g * tiles + t + 1] for t in range(tiles)], axis=1)[:, :samples]
        for g in range(genes)
    ]
    pheno = jnp.concatenate(pheno, axis=0).astype(jnp.bfloat16)
    perms = perms_ref[...]
    twice = jnp.concatenate([perms, perms], axis=1)
    sample = lax.broadcasted_iota(jnp.int32, (samples, 2 * samples), 0)
    permuted = []
    for r in range(rperms):
        chosen = jnp.where(sample == twice[r : r + 1, :], 1.0, 0.0).astype(jnp.bfloat16)
        permuted.append(jnp.dot(pheno, chosen, preferred_element_type=jnp.float32))
    yrows = [permuted[r][g : g + 1] for g in range(genes) for r in range(rperms)]
    yall = jnp.concatenate(yrows, axis=0)
    tail = jnp.dot(yall.astype(jnp.bfloat16), b_both, preferred_element_type=jnp.float32) / count
    c_hi = tail.astype(jnp.bfloat16).astype(jnp.float32)
    c_lo = tail - c_hi

    geno_a = jnp.concatenate([by_samples(panel_a, q) for q in range(TILE // s_dev)], axis=1)
    a_rows = jnp.concatenate([geno_a, geno_a], axis=0).T
    a_minus = -a_rows.astype(jnp.bfloat16)
    copies = []
    for k in range(len(yrows)):
        scaled = (a_rows * yrows[k]).astype(jnp.bfloat16)
        left = jnp.concatenate([scaled, a_minus], axis=1)
        tails = [jnp.broadcast_to(c[k : k + 1], geno_b.shape).astype(jnp.bfloat16) for c in (c_hi, c_lo)]
        right = jnp.concatenate([b_both] + tails, axis=0)
        out_ref[k] = jnp.dot(left, right, preferred_element_type=jnp.float32).astype(out_ref.dtype)
        copies.append(pltpu.make_async_copy(out_ref.at[k], out_hbm.at[0, k], sems.at[k]))
        copies[-1].start()
    for copy in copies:
        copy.wait()


def on_device(dosage, phenotype, perms, pairs):
    s_dev, snps = dosage.shape
    genes = phenotype.shape[0]
    samples = perms.shape[1]
    pair_count, samps = (lax.axis_size(axis) for axis in AXES)
    rounds = pair_count // 2 + 1
    rows = wave_rows(genes, samples)
    grid = dosage.reshape(s_dev, snps // LANES, LANES).transpose(1, 0, 2).reshape(-1, LANES)
    vmem = pl.BlockSpec(memory_space=pltpu.VMEM)
    hbm = pl.BlockSpec(memory_space=pltpu.HBM)

    def array(*shape):
        return jax.ShapeDtypeStruct(shape, dosage.dtype)

    keep, give, wave = pl.pallas_call(
        functools.partial(pack_kernel, pair_count, samps),
        out_shape=[array(rounds * BLOCK, LANES), array(rounds * BLOCK + rows, LANES), array(rows, LANES)],
        in_specs=[hbm, hbm, hbm],
        out_specs=[vmem, vmem, vmem],
        scratch_shapes=[
            pltpu.SMEM(pairs.shape[::-1], pairs.dtype),
            pltpu.VMEM(phenotype.shape, phenotype.dtype),
            pltpu.VMEM(grid.shape, grid.dtype),
            pltpu.SemaphoreType.DMA((3,)),
        ],
        compiler_params=pltpu.CompilerParams(vmem_limit_bytes=8 * 1024 * 1024),
        name="pack",
    )(pairs.T, phenotype, grid)

    swap = [(i, samps - 1 - i) for i in range(samps)]
    got = lax.ppermute(give, "samp", swap)
    wave = wave + got[rounds * BLOCK :]
    arrived = []
    for i in range(rounds - 1):
        blocks = slice(i * BLOCK, (i + 1) * BLOCK)
        message = jnp.concatenate([keep[blocks], got[blocks], wave], axis=0)
        route = [
            (p * samps + c, (p ^ offsets(pair_count, c)[i]) * samps + c)
            for p in range(pair_count)
            for c in range(samps)
        ]
        arrived.append(lax.ppermute(message, AXES, route))
    *far, near = arrived
    own = jnp.concatenate([a[: 2 * BLOCK] for a in far] + [sum(a[2 * BLOCK :] for a in far)], axis=0)
    mate = lax.ppermute(own, "samp", swap)
    end = 2 * BLOCK * len(far)
    wave = wave + own[end:] + mate[end:] + near[2 * BLOCK :]
    stats = genes * perms.shape[0]
    half = PANEL // samps
    return pl.pallas_call(
        functools.partial(stat_kernel, pair_count, samps),
        out_shape=jax.ShapeDtypeStruct((1, stats, PANEL, half), jnp.bfloat16),
        in_specs=[vmem] * 7,
        out_specs=hbm,
        scratch_shapes=[
            pltpu.VMEM((pair_count * samps, BLOCK, LANES), dosage.dtype),
            pltpu.VMEM((stats, PANEL, half), jnp.bfloat16),
            pltpu.SemaphoreType.DMA((stats,)),
        ],
        compiler_params=pltpu.CompilerParams(vmem_limit_bytes=48 * 1024 * 1024),
        name="stat",
    )(perms, keep, got, own, mate, near, wave)


def solution(mesh):
    placed = (P(("rep", "pair", "samp"), None), P(None, ("rep", "pair", "samp")), P(), P())
    return jax.shard_map(
        on_device,
        mesh=mesh,
        in_specs=placed,
        out_specs=P(("rep", "pair"), None, None, "samp"),
        check_vma=False,
    )
```

```python
import functools

import jax
import jax.numpy as jnp
from jax import lax
from jax.experimental import pallas as pl
from jax.experimental.pallas import tpu as pltpu
from jax.sharding import PartitionSpec as P

PANEL = 512
LANES = 128
TILE = 16
BLOCK = 2 * TILE
AXES = ("pair", "samp")


def offsets(pair_count, core):
    return [2 * i + core for i in range(pair_count // 2 - 1, 0, -1)] + [1, 0]


def wave_rows(genes, samples):
    return -(-genes * -(-samples // LANES) // 8) * 8


def pack_kernel(pair_count, samps, pairs_hbm, pheno_hbm, grid_hbm, keep_ref, give_ref, wave_ref, pairs_ref, pheno_ref, grid_ref, sems):
    copies = [
        pltpu.make_async_copy(source, target, sems.at[i])
        for i, (source, target) in enumerate(((pairs_hbm, pairs_ref), (grid_hbm, grid_ref), (pheno_hbm, pheno_ref)))
    ]
    for copy in copies:
        copy.start()
    pair, samp = lax.axis_index("pair"), lax.axis_index("samp")
    genes, s_dev = pheno_ref.shape
    rows = wave_ref.shape[0]
    tiles = -(-s_dev * samps * pair_count // LANES)
    row = lax.broadcasted_iota(jnp.int32, (rows, LANES), 0)
    lane = lax.broadcasted_iota(jnp.int32, (rows, LANES), 1)
    spot = (pair * samps + samp) * s_dev
    first, tile = lax.rem(spot, LANES), lax.div(spot, LANES)
    for copy in copies:
        copy.wait()

    pheno = pheno_ref[...].astype(jnp.float32)
    wave = jnp.zeros((rows, LANES), jnp.float32)
    for g in range(genes):
        for s in range(s_dev):
            hit = (lane == first + s) & (row == g * tiles + tile)
            wave = jnp.where(hit, pheno[g : g + 1, s : s + 1], wave)
    wave = wave.astype(wave_ref.dtype)
    wave_ref[...] = wave

    own_side, far_side = offsets(pair_count, 0), offsets(pair_count, 1)
    for i, (even, odd) in enumerate(zip(own_side, far_side)):
        for ref, core in ((keep_ref, samp), (give_ref, samps - 1 - samp)):
            n = lax.bitwise_xor(pair, even + (odd - even) * core)
            for j in range(2):
                start = pl.multiple_of(pairs_ref[j, n] * TILE, TILE)
                place = i * BLOCK + j * TILE
                ref[place : place + TILE, :] = grid_ref[pl.ds(start, TILE), :]
    give_ref[len(own_side) * BLOCK :, :] = wave


def stat_kernel(pair_count, samps, perms_ref, wave_ref, keep_ref, give_ref, near_ref, *refs):
    far = pair_count // 2 - 1
    own_refs, mate_refs = refs[:far], refs[far : 2 * far]
    out_hbm, got_ref, out_ref, sems = refs[2 * far :]
    pair, samp = lax.axis_index("pair"), lax.axis_index("samp")
    other = samps - 1 - samp

    def place(offset, core, block):
        got_ref[lax.bitwise_xor(pair, offset) * samps + core] = block

    for arrived, core in ((own_refs, samp), (mate_refs, other)):
        for i, ref in enumerate(arrived):
            offset = 2 * (far - i) + core
            place(offset, core, ref[:BLOCK, :])
            place(offset, samps - 1 - core, ref[BLOCK : 2 * BLOCK, :])
    place(1, samp, near_ref[:BLOCK, :])
    place(1, other, near_ref[BLOCK : 2 * BLOCK, :])
    itself = (far + 1) * BLOCK
    place(0, samp, keep_ref[itself : itself + BLOCK, :])
    place(0, other, give_ref[itself : itself + BLOCK, :])

    sources = got_ref.shape[0]
    rperms, samples = perms_ref.shape
    s_dev = samples // sources

    def by_samples(tiles, group):
        return tiles[:, group * s_dev : (group + 1) * s_dev, :].reshape(samples, LANES)

    panel_a = got_ref[:, 0:TILE, :].astype(jnp.float32)
    panel_b = got_ref[:, TILE:BLOCK, :].astype(jnp.float32)
    tile_b = jnp.where(samp == 0, panel_b[:, : TILE // 2], panel_b[:, TILE // 2 :])

    count = jnp.float32(samples)
    geno_b = jnp.concatenate([by_samples(tile_b, q) for q in range(TILE // 2 // s_dev)], axis=1)
    marg_b = jnp.sum(geno_b, axis=0, keepdims=True)
    centred = (geno_b - marg_b / count) * (samples**-0.5)
    b_hi = centred.astype(jnp.bfloat16)
    b_lo = (centred - b_hi.astype(jnp.float32)).astype(jnp.bfloat16)
    b_both = jnp.concatenate([b_hi, b_lo], axis=0)

    wave = wave_ref[...].astype(jnp.float32)
    for ref in (*own_refs, *mate_refs, near_ref):
        wave = wave + ref[2 * BLOCK :, :].astype(jnp.float32)
    genes = out_ref.shape[0] // rperms
    tiles = -(-samples // LANES)
    pheno = [
        jnp.concatenate([wave[g * tiles + t : g * tiles + t + 1] for t in range(tiles)], axis=1)[:, :samples]
        for g in range(genes)
    ]
    pheno = jnp.concatenate(pheno, axis=0).astype(jnp.bfloat16)
    perms = perms_ref[...]
    twice = jnp.concatenate([perms, perms], axis=1)
    sample = lax.broadcasted_iota(jnp.int32, (samples, 2 * samples), 0)
    permuted = []
    for r in range(rperms):
        chosen = jnp.where(sample == twice[r : r + 1, :], 1.0, 0.0).astype(jnp.bfloat16)
        permuted.append(jnp.dot(pheno, chosen, preferred_element_type=jnp.float32))
    yrows = [permuted[r][g : g + 1] for g in range(genes) for r in range(rperms)]
    yall = jnp.concatenate(yrows, axis=0)
    tail = jnp.dot(yall.astype(jnp.bfloat16), b_both, preferred_element_type=jnp.float32) / count
    c_hi = tail.astype(jnp.bfloat16).astype(jnp.float32)
    c_lo = tail - c_hi

    geno_a = jnp.concatenate([by_samples(panel_a, q) for q in range(TILE // s_dev)], axis=1)
    a_rows = jnp.concatenate([geno_a, geno_a], axis=0).T
    a_minus = -a_rows.astype(jnp.bfloat16)
    copies = []
    for k in range(len(yrows)):
        scaled = (a_rows * yrows[k]).astype(jnp.bfloat16)
        left = jnp.concatenate([scaled, a_minus], axis=1)
        tails = [jnp.broadcast_to(c[k : k + 1], geno_b.shape).astype(jnp.bfloat16) for c in (c_hi, c_lo)]
        right = jnp.concatenate([b_both] + tails, axis=0)
        out_ref[k] = jnp.dot(left, right, preferred_element_type=jnp.float32).astype(out_ref.dtype)
        copies.append(pltpu.make_async_copy(out_ref.at[k], out_hbm.at[0, k], sems.at[k]))
        copies[-1].start()
    for copy in copies:
        copy.wait()


def on_device(dosage, phenotype, perms, pairs):
    s_dev, snps = dosage.shape
    genes = phenotype.shape[0]
    samples = perms.shape[1]
    pair_count, samps = (lax.axis_size(axis) for axis in AXES)
    rounds = pair_count // 2 + 1
    rows = wave_rows(genes, samples)
    grid = dosage.reshape(s_dev, snps // LANES, LANES).transpose(1, 0, 2).reshape(-1, LANES)
    vmem = pl.BlockSpec(memory_space=pltpu.VMEM)
    hbm = pl.BlockSpec(memory_space=pltpu.HBM)

    def array(*shape):
        return jax.ShapeDtypeStruct(shape, dosage.dtype)

    keep, give, wave = pl.pallas_call(
        functools.partial(pack_kernel, pair_count, samps),
        out_shape=[array(rounds * BLOCK, LANES), array(rounds * BLOCK + rows, LANES), array(rows, LANES)],
        in_specs=[hbm, hbm, hbm],
        out_specs=[vmem, vmem, vmem],
        scratch_shapes=[
            pltpu.SMEM(pairs.shape[::-1], pairs.dtype),
            pltpu.VMEM(phenotype.shape, phenotype.dtype),
            pltpu.VMEM(grid.shape, grid.dtype),
            pltpu.SemaphoreType.DMA((3,)),
        ],
        compiler_params=pltpu.CompilerParams(vmem_limit_bytes=8 * 1024 * 1024),
        name="pack",
    )(*[pltpu.with_memory_space_constraint(x, pltpu.HBM) for x in (pairs.T, phenotype, grid)])

    swap = [(i, samps - 1 - i) for i in range(samps)]
    got = lax.ppermute(give, "samp", swap)
    wave = wave + got[rounds * BLOCK :]
    arrived = []
    for i in range(rounds - 1):
        blocks = slice(i * BLOCK, (i + 1) * BLOCK)
        message = jnp.concatenate([keep[blocks], got[blocks], wave], axis=0)
        route = [
            (p * samps + c, (p ^ offsets(pair_count, c)[i]) * samps + c)
            for p in range(pair_count)
            for c in range(samps)
        ]
        arrived.append(lax.ppermute(message, AXES, route))
    *far, near = arrived
    mates = [lax.ppermute(a, "samp", swap) for a in far]
    stats = genes * perms.shape[0]
    half = PANEL // samps
    return pl.pallas_call(
        functools.partial(stat_kernel, pair_count, samps),
        out_shape=jax.ShapeDtypeStruct((1, stats, PANEL, half), jnp.bfloat16),
        in_specs=[vmem] * (5 + 2 * len(far)),
        out_specs=hbm,
        scratch_shapes=[
            pltpu.VMEM((pair_count * samps, BLOCK, LANES), dosage.dtype),
            pltpu.VMEM((stats, PANEL, half), jnp.bfloat16),
            pltpu.SemaphoreType.DMA((stats,)),
        ],
        compiler_params=pltpu.CompilerParams(vmem_limit_bytes=48 * 1024 * 1024),
        name="stat",
    )(perms, wave, keep, got, near, *far, *mates)


def solution(mesh):
    placed = (P(("rep", "pair", "samp"), None), P(None, ("rep", "pair", "samp")), P(), P())
    return jax.shard_map(
        on_device,
        mesh=mesh,
        in_specs=placed,
        out_specs=P(("rep", "pair"), None, None, "samp"),
        check_vma=False,
    )
```

```python
import functools

import jax
import jax.numpy as jnp
from jax import lax
from jax.experimental import pallas as pl
from jax.experimental.pallas import tpu as pltpu
from jax.sharding import PartitionSpec as P

PANEL = 512
LANES = 128
TILE = 16
BLOCK = 2 * TILE
AXES = ("pair", "samp")


def offsets(pair_count, core):
    return [2 * i + core for i in range(pair_count // 2 - 1, 0, -1)] + [1, 0]


def wave_rows(genes, samples):
    return -(-genes * -(-samples // LANES) // 8) * 8


def pack_kernel(pair_count, samps, pairs_hbm, pheno_hbm, grid_hbm, keep_ref, give_ref, wave_ref, pairs_ref, pheno_ref, grid_ref, sems):
    copies = [
        pltpu.make_async_copy(source, target, sems.at[i])
        for i, (source, target) in enumerate(((pairs_hbm, pairs_ref), (grid_hbm, grid_ref), (pheno_hbm, pheno_ref)))
    ]
    for copy in copies:
        copy.start()
    pair, samp = lax.axis_index("pair"), lax.axis_index("samp")
    genes, s_dev = pheno_ref.shape
    rows = wave_ref.shape[0]
    tiles = -(-s_dev * samps * pair_count // LANES)
    row = lax.broadcasted_iota(jnp.int32, (rows, LANES), 0)
    lane = lax.broadcasted_iota(jnp.int32, (rows, LANES), 1)
    spot = (pair * samps + samp) * s_dev
    first, tile = lax.rem(spot, LANES), lax.div(spot, LANES)
    for copy in copies:
        copy.wait()

    pheno = pheno_ref[...].astype(jnp.float32)
    wave = jnp.zeros((rows, LANES), jnp.float32)
    for g in range(genes):
        for s in range(s_dev):
            hit = (lane == first + s) & (row == g * tiles + tile)
            wave = jnp.where(hit, pheno[g : g + 1, s : s + 1], wave)
    wave = wave.astype(wave_ref.dtype)
    wave_ref[...] = wave

    own_side, far_side = offsets(pair_count, 0), offsets(pair_count, 1)
    for i, (even, odd) in enumerate(zip(own_side, far_side)):
        for ref, core in ((keep_ref, samp), (give_ref, samps - 1 - samp)):
            n = lax.bitwise_xor(pair, even + (odd - even) * core)
            for j in range(2):
                start = pl.multiple_of(pairs_ref[j, n] * TILE, TILE)
                place = i * BLOCK + j * TILE
                ref[place : place + TILE, :] = grid_ref[pl.ds(start, TILE), :]
    give_ref[len(own_side) * BLOCK :, :] = wave


def stat_kernel(pair_count, samps, perms_ref, wave_ref, keep_ref, give_ref, near_ref, *refs):
    far = pair_count // 2 - 1
    own_refs, mate_refs = refs[:far], refs[far : 2 * far]
    out_hbm, got_ref, out_ref, sems = refs[2 * far :]
    pair, samp = lax.axis_index("pair"), lax.axis_index("samp")
    other = samps - 1 - samp

    def place(offset, core, block):
        got_ref[lax.bitwise_xor(pair, offset) * samps + core] = block

    for arrived, core in ((own_refs, samp), (mate_refs, other)):
        for i, ref in enumerate(arrived):
            offset = 2 * (far - i) + core
            place(offset, core, ref[:BLOCK, :])
            place(offset, samps - 1 - core, ref[BLOCK : 2 * BLOCK, :])
    place(1, samp, near_ref[:BLOCK, :])
    place(1, other, near_ref[BLOCK : 2 * BLOCK, :])
    itself = (far + 1) * BLOCK
    place(0, samp, keep_ref[itself : itself + BLOCK, :])
    place(0, other, give_ref[itself : itself + BLOCK, :])

    sources = got_ref.shape[0]
    rperms, samples = perms_ref.shape
    s_dev = samples // sources

    def by_samples(tiles, group):
        return tiles[:, group * s_dev : (group + 1) * s_dev, :].reshape(samples, LANES)

    panel_a = got_ref[:, 0:TILE, :].astype(jnp.float32)
    panel_b = got_ref[:, TILE:BLOCK, :].astype(jnp.float32)
    tile_b = jnp.where(samp == 0, panel_b[:, : TILE // 2], panel_b[:, TILE // 2 :])

    count = jnp.float32(samples)
    geno_b = jnp.concatenate([by_samples(tile_b, q) for q in range(TILE // 2 // s_dev)], axis=1)
    marg_b = jnp.sum(geno_b, axis=0, keepdims=True)
    centred = (geno_b - marg_b / count) * (samples**-0.5)
    b_hi = centred.astype(jnp.bfloat16)
    b_lo = (centred - b_hi.astype(jnp.float32)).astype(jnp.bfloat16)
    b_both = jnp.concatenate([b_hi, b_lo], axis=0)

    wave = wave_ref[...].astype(jnp.float32)
    for ref in (*own_refs, *mate_refs, near_ref):
        wave = wave + ref[2 * BLOCK :, :].astype(jnp.float32)
    genes = out_ref.shape[0] // rperms
    tiles = -(-samples // LANES)
    pheno = [
        jnp.concatenate([wave[g * tiles + t : g * tiles + t + 1] for t in range(tiles)], axis=1)[:, :samples]
        for g in range(genes)
    ]
    pheno = jnp.concatenate(pheno, axis=0).astype(jnp.bfloat16)
    perms = perms_ref[...]
    twice = jnp.concatenate([perms, perms], axis=1)
    sample = lax.broadcasted_iota(jnp.int32, (samples, 2 * samples), 0)
    permuted = []
    for r in range(rperms):
        chosen = jnp.where(sample == twice[r : r + 1, :], 1.0, 0.0).astype(jnp.bfloat16)
        permuted.append(jnp.dot(pheno, chosen, preferred_element_type=jnp.float32))
    yrows = [permuted[r][g : g + 1] for g in range(genes) for r in range(rperms)]
    yall = jnp.concatenate(yrows, axis=0)
    tail = jnp.dot(yall.astype(jnp.bfloat16), b_both, preferred_element_type=jnp.float32) / count
    c_hi = tail.astype(jnp.bfloat16).astype(jnp.float32)
    c_lo = tail - c_hi

    geno_a = jnp.concatenate([by_samples(panel_a, q) for q in range(TILE // s_dev)], axis=1)
    a_rows = jnp.concatenate([geno_a, geno_a], axis=0).T
    a_minus = -a_rows.astype(jnp.bfloat16)
    copies = []
    for k in range(len(yrows)):
        scaled = (a_rows * yrows[k]).astype(jnp.bfloat16)
        left = jnp.concatenate([scaled, a_minus], axis=1)
        tails = [jnp.broadcast_to(c[k : k + 1], geno_b.shape).astype(jnp.bfloat16) for c in (c_hi, c_lo)]
        right = jnp.concatenate([b_both] + tails, axis=0)
        out_ref[k] = jnp.dot(left, right, preferred_element_type=jnp.float32).astype(out_ref.dtype)
        copies.append(pltpu.make_async_copy(out_ref.at[k], out_hbm.at[0, k], sems.at[k]))
        copies[-1].start()
    for copy in copies:
        copy.wait()


def on_device(dosage, phenotype, perms, pairs):
    s_dev, snps = dosage.shape
    genes = phenotype.shape[0]
    samples = perms.shape[1]
    pair_count, samps = (lax.axis_size(axis) for axis in AXES)
    rounds = pair_count // 2 + 1
    rows = wave_rows(genes, samples)
    grid = dosage.reshape(s_dev, snps // LANES, LANES).transpose(1, 0, 2).reshape(-1, LANES)
    vmem = pl.BlockSpec(memory_space=pltpu.VMEM)
    hbm = pl.BlockSpec(memory_space=pltpu.HBM)

    def array(*shape):
        return jax.ShapeDtypeStruct(shape, dosage.dtype)

    keep, give, wave = pl.pallas_call(
        functools.partial(pack_kernel, pair_count, samps),
        out_shape=[array(rounds * BLOCK, LANES), array(rounds * BLOCK + rows, LANES), array(rows, LANES)],
        in_specs=[hbm, hbm, hbm],
        out_specs=[vmem, vmem, vmem],
        scratch_shapes=[
            pltpu.SMEM(pairs.shape[::-1], pairs.dtype),
            pltpu.VMEM(phenotype.shape, phenotype.dtype),
            pltpu.VMEM(grid.shape, grid.dtype),
            pltpu.SemaphoreType.DMA((3,)),
        ],
        compiler_params=pltpu.CompilerParams(vmem_limit_bytes=8 * 1024 * 1024),
        name="pack",
    )(*[pltpu.with_memory_space_constraint(x, pltpu.HBM) for x in (pairs.T, phenotype, grid)])

    swap = [(i, samps - 1 - i) for i in range(samps)]
    got = lax.ppermute(give, "samp", swap)
    wave = wave + got[rounds * BLOCK :]
    messages = []
    for i in range(rounds - 1):
        blocks = slice(i * BLOCK, (i + 1) * BLOCK)
        messages.append(jnp.concatenate([keep[blocks], got[blocks], wave], axis=0))
    *far_messages, near_message = messages

    def exchange(i, side=None):
        bit = 1 << (pair_count // 2 - 1 - i).bit_length()
        return [
            (p * samps + c, (p ^ offsets(pair_count, c)[i]) * samps + c)
            for p in range(pair_count)
            for c in range(samps)
            if side in (None, (p & bit > 0))
        ]

    count = len(far_messages)
    down = [lax.ppermute(far_messages[i], AXES, exchange(i, 1)) for i in range(count - 1)]
    last = lax.ppermute(far_messages[-1], AXES, exchange(count - 1))
    near = lax.ppermute(near_message, "pair", [(p, p ^ 1) for p in range(pair_count)])
    *far_messages, _, _ = lax.optimization_barrier((*far_messages, *down))
    up = [lax.ppermute(far_messages[i], AXES, exchange(i, 0)) for i in range(count - 1)]
    far = [d + u for d, u in zip(down, up)] + [last]
    mates = [lax.ppermute(a, "samp", swap) for a in far]
    stats = genes * perms.shape[0]
    half = PANEL // samps
    return pl.pallas_call(
        functools.partial(stat_kernel, pair_count, samps),
        out_shape=jax.ShapeDtypeStruct((1, stats, PANEL, half), jnp.bfloat16),
        in_specs=[vmem] * (5 + 2 * len(far)),
        out_specs=hbm,
        scratch_shapes=[
            pltpu.VMEM((pair_count * samps, BLOCK, LANES), dosage.dtype),
            pltpu.VMEM((stats, PANEL, half), jnp.bfloat16),
            pltpu.SemaphoreType.DMA((stats,)),
        ],
        compiler_params=pltpu.CompilerParams(vmem_limit_bytes=48 * 1024 * 1024),
        name="stat",
    )(perms, wave, keep, got, near, *far, *mates)


def solution(mesh):
    placed = (P(("rep", "pair", "samp"), None), P(None, ("rep", "pair", "samp")), P(), P())
    return jax.shard_map(
        on_device,
        mesh=mesh,
        in_specs=placed,
        out_specs=P(("rep", "pair"), None, None, "samp"),
        check_vma=False,
    )
```

```python
import functools

import jax
import jax.numpy as jnp
from jax import lax
from jax.experimental import pallas as pl
from jax.experimental.pallas import tpu as pltpu
from jax.sharding import PartitionSpec as P

PANEL = 512
LANES = 128
TILE = 16
BLOCK = 2 * TILE
AXES = ("pair", "samp")


def offsets(pair_count, core):
    shared = pair_count - 2
    rest = [e for e in range(1, pair_count) if e != shared]
    mine = rest[: len(rest) // 2] if core == 0 else rest[len(rest) // 2 :]
    if core == 0:
        mine = mine[1:] + mine[:1]
    return mine[1:] + mine[:1] + [shared, 0]


def shifted(pair, offset, pair_count, sign=1):
    high = (pair // 2 + sign * (offset // 2) + pair_count // 2) % (pair_count // 2)
    return high * 2 + (pair + offset) % 2


def wave_rows(genes, samples):
    return -(-genes * -(-samples // LANES) // 8) * 8


def pack_kernel(pair_count, samps, pairs_hbm, pheno_hbm, grid_hbm, keep_ref, give_ref, wave_ref, pairs_ref, pheno_ref, grid_ref, sems):
    copies = [
        pltpu.make_async_copy(source, target, sems.at[i])
        for i, (source, target) in enumerate(((pairs_hbm, pairs_ref), (grid_hbm, grid_ref), (pheno_hbm, pheno_ref)))
    ]
    for copy in copies:
        copy.start()
    pair, samp = lax.axis_index("pair"), lax.axis_index("samp")
    genes, s_dev = pheno_ref.shape
    rows = wave_ref.shape[0]
    tiles = -(-s_dev * samps * pair_count // LANES)
    row = lax.broadcasted_iota(jnp.int32, (rows, LANES), 0)
    lane = lax.broadcasted_iota(jnp.int32, (rows, LANES), 1)
    spot = (pair * samps + samp) * s_dev
    first, tile = lax.rem(spot, LANES), lax.div(spot, LANES)
    for copy in copies:
        copy.wait()

    pheno = pheno_ref[...].astype(jnp.float32)
    wave = jnp.zeros((rows, LANES), jnp.float32)
    for g in range(genes):
        for s in range(s_dev):
            hit = (lane == first + s) & (row == g * tiles + tile)
            wave = jnp.where(hit, pheno[g : g + 1, s : s + 1], wave)
    wave = wave.astype(wave_ref.dtype)
    wave_ref[...] = wave

    own_side, far_side = offsets(pair_count, 0), offsets(pair_count, 1)
    for i, (even, odd) in enumerate(zip(own_side, far_side)):
        for ref, core in ((keep_ref, samp), (give_ref, samps - 1 - samp)):
            n = shifted(pair, jnp.where(core == 0, even, odd), pair_count)
            for j in range(2):
                start = pl.multiple_of(pairs_ref[j, n] * TILE, TILE)
                place = i * BLOCK + j * TILE
                ref[place : place + TILE, :] = grid_ref[pl.ds(start, TILE), :]
    give_ref[len(own_side) * BLOCK :, :] = wave


def stat_kernel(pair_count, samps, perms_ref, wave_ref, keep_ref, give_ref, near_ref, *refs):
    far = pair_count // 2 - 1
    own_refs, mate_refs = refs[:far], refs[far : 2 * far]
    out_hbm, got_ref, out_ref, sems = refs[2 * far :]
    pair, samp = lax.axis_index("pair"), lax.axis_index("samp")
    other = samps - 1 - samp

    def place(offset, core, block):
        got_ref[shifted(pair, offset, pair_count, -1) * samps + core] = block

    even, odd = offsets(pair_count, 0), offsets(pair_count, 1)
    for arrived, core in ((own_refs, samp), (mate_refs, other)):
        for i, ref in enumerate(arrived):
            offset = jnp.where(core == 0, even[i], odd[i])
            place(offset, core, ref[:BLOCK, :])
            place(offset, samps - 1 - core, ref[BLOCK : 2 * BLOCK, :])
    place(even[far], samp, near_ref[:BLOCK, :])
    place(even[far], other, near_ref[BLOCK : 2 * BLOCK, :])
    itself = (far + 1) * BLOCK
    place(0, samp, keep_ref[itself : itself + BLOCK, :])
    place(0, other, give_ref[itself : itself + BLOCK, :])

    sources = got_ref.shape[0]
    rperms, samples = perms_ref.shape
    s_dev = samples // sources

    def by_samples(tiles, group):
        return tiles[:, group * s_dev : (group + 1) * s_dev, :].reshape(samples, LANES)

    panel_a = got_ref[:, 0:TILE, :].astype(jnp.float32)
    panel_b = got_ref[:, TILE:BLOCK, :].astype(jnp.float32)
    tile_b = jnp.where(samp == 0, panel_b[:, : TILE // 2], panel_b[:, TILE // 2 :])

    count = jnp.float32(samples)
    geno_b = jnp.concatenate([by_samples(tile_b, q) for q in range(TILE // 2 // s_dev)], axis=1)
    marg_b = jnp.sum(geno_b, axis=0, keepdims=True)
    centred = (geno_b - marg_b / count) * (samples**-0.5)
    b_hi = centred.astype(jnp.bfloat16)
    b_lo = (centred - b_hi.astype(jnp.float32)).astype(jnp.bfloat16)
    b_both = jnp.concatenate([b_hi, b_lo], axis=0)

    wave = wave_ref[...].astype(jnp.float32)
    for ref in (*own_refs, *mate_refs, near_ref):
        wave = wave + ref[2 * BLOCK :, :].astype(jnp.float32)
    genes = out_ref.shape[0] // rperms
    tiles = -(-samples // LANES)
    pheno = [
        jnp.concatenate([wave[g * tiles + t : g * tiles + t + 1] for t in range(tiles)], axis=1)[:, :samples]
        for g in range(genes)
    ]
    pheno = jnp.concatenate(pheno, axis=0).astype(jnp.bfloat16)
    perms = perms_ref[...]
    twice = jnp.concatenate([perms, perms], axis=1)
    sample = lax.broadcasted_iota(jnp.int32, (samples, 2 * samples), 0)
    permuted = []
    for r in range(rperms):
        chosen = jnp.where(sample == twice[r : r + 1, :], 1.0, 0.0).astype(jnp.bfloat16)
        permuted.append(jnp.dot(pheno, chosen, preferred_element_type=jnp.float32))
    yrows = [permuted[r][g : g + 1] for g in range(genes) for r in range(rperms)]
    yall = jnp.concatenate(yrows, axis=0)
    tail = jnp.dot(yall.astype(jnp.bfloat16), b_both, preferred_element_type=jnp.float32) / count
    c_hi = tail.astype(jnp.bfloat16).astype(jnp.float32)
    c_lo = tail - c_hi

    rows = []
    for q in range(TILE // s_dev):
        geno_a = by_samples(panel_a, q)
        rows.append(jnp.concatenate([geno_a, geno_a], axis=0).astype(jnp.bfloat16).T)
    copies = []
    for k, yrow in enumerate(yrows):
        yrow = yrow.astype(jnp.bfloat16)
        tails = [jnp.broadcast_to(c[k : k + 1], geno_b.shape).astype(jnp.bfloat16) for c in (c_hi, c_lo)]
        right = jnp.concatenate([b_both] + tails, axis=0)
        for q, part in enumerate(rows):
            left = jnp.concatenate([part * yrow, -part], axis=1)
            piece = slice(q * LANES, (q + 1) * LANES)
            out_ref[k, piece, :] = jnp.dot(left, right, preferred_element_type=jnp.float32).astype(out_ref.dtype)
            copies.append(pltpu.make_async_copy(out_ref.at[k, piece], out_hbm.at[0, k, piece], sems.at[k, q]))
            copies[-1].start()
    for copy in copies:
        copy.wait()


def on_device(dosage, phenotype, perms, pairs):
    s_dev, snps = dosage.shape
    genes = phenotype.shape[0]
    samples = perms.shape[1]
    pair_count, samps = (lax.axis_size(axis) for axis in AXES)
    rounds = pair_count // 2 + 1
    rows = wave_rows(genes, samples)
    grid = dosage.reshape(s_dev, snps // LANES, LANES).transpose(1, 0, 2).reshape(-1, LANES)
    vmem = pl.BlockSpec(memory_space=pltpu.VMEM)
    hbm = pl.BlockSpec(memory_space=pltpu.HBM)

    def array(*shape):
        return jax.ShapeDtypeStruct(shape, dosage.dtype)

    keep, give, wave = pl.pallas_call(
        functools.partial(pack_kernel, pair_count, samps),
        out_shape=[array(rounds * BLOCK, LANES), array(rounds * BLOCK + rows, LANES), array(rows, LANES)],
        in_specs=[hbm, hbm, hbm],
        out_specs=[vmem, vmem, vmem],
        scratch_shapes=[
            pltpu.SMEM(pairs.shape[::-1], pairs.dtype),
            pltpu.VMEM(phenotype.shape, phenotype.dtype),
            pltpu.VMEM(grid.shape, grid.dtype),
            pltpu.SemaphoreType.DMA((3,)),
        ],
        compiler_params=pltpu.CompilerParams(vmem_limit_bytes=8 * 1024 * 1024),
        name="pack",
    )(*[pltpu.with_memory_space_constraint(x, pltpu.HBM) for x in (pairs.T, phenotype, grid)])

    swap = [(i, samps - 1 - i) for i in range(samps)]
    got = lax.ppermute(give, "samp", swap)
    wave = wave + got[rounds * BLOCK :]
    arrived = []
    for i in range(rounds - 1):
        blocks = slice(i * BLOCK, (i + 1) * BLOCK)
        message = jnp.concatenate([keep[blocks], got[blocks], wave], axis=0)
        route = [
            (p * samps + c, shifted(p, offsets(pair_count, c)[i], pair_count) * samps + c)
            for p in range(pair_count)
            for c in range(samps)
        ]
        arrived.append(lax.ppermute(message, AXES, route))
    *far, near = arrived
    mates = [lax.ppermute(a, "samp", swap) for a in far]
    stats = genes * perms.shape[0]
    half = PANEL // samps
    return pl.pallas_call(
        functools.partial(stat_kernel, pair_count, samps),
        out_shape=jax.ShapeDtypeStruct((1, stats, PANEL, half), jnp.bfloat16),
        in_specs=[vmem] * (5 + 2 * len(far)),
        out_specs=hbm,
        scratch_shapes=[
            pltpu.VMEM((pair_count * samps, BLOCK, LANES), dosage.dtype),
            pltpu.VMEM((stats, PANEL, half), jnp.bfloat16),
            pltpu.SemaphoreType.DMA((stats, PANEL // LANES)),
        ],
        compiler_params=pltpu.CompilerParams(vmem_limit_bytes=48 * 1024 * 1024),
        name="stat",
    )(perms, wave, keep, got, near, *far, *mates)


def solution(mesh):
    placed = (P(("rep", "pair", "samp"), None), P(None, ("rep", "pair", "samp")), P(), P())
    return jax.shard_map(
        on_device,
        mesh=mesh,
        in_specs=placed,
        out_specs=P(("rep", "pair"), None, None, "samp"),
        check_vma=False,
    )
```

```python
import functools

import jax
import jax.numpy as jnp
from jax import lax
from jax.experimental import pallas as pl
from jax.experimental.pallas import tpu as pltpu
from jax.sharding import PartitionSpec as P

PANEL = 512
LANES = 128
TILE = 16
BLOCK = 2 * TILE
AXES = ("pair", "samp")


def offsets(pair_count, core):
    shared = pair_count - 2
    rest = [e for e in range(1, pair_count) if e != shared]
    mine = rest[: len(rest) // 2] if core == 0 else rest[len(rest) // 2 :]
    if core == 0:
        mine = mine[1:] + mine[:1]
    return mine[1:] + mine[:1] + [shared, 0]


def shifted(pair, offset, pair_count, sign=1):
    high = (pair // 2 + sign * (offset // 2) + pair_count // 2) % (pair_count // 2)
    return high * 2 + (pair + offset) % 2


def wave_rows(stats, samples):
    return -(-stats * 2 * samples // LANES // 8) * 8


def pack_kernel(
    pair_count, samps, pairs_hbm, pheno_hbm, perms_hbm, grid_hbm, keep_ref, give_ref, wave_ref, pairs_ref, pheno_ref, perms_ref, grid_ref, sems
):
    fetched = ((pairs_hbm, pairs_ref), (grid_hbm, grid_ref), (pheno_hbm, pheno_ref), (perms_hbm, perms_ref))
    copies = [pltpu.make_async_copy(source, target, sems.at[i]) for i, (source, target) in enumerate(fetched)]
    for copy in copies:
        copy.start()
    pair, samp = lax.axis_index("pair"), lax.axis_index("samp")
    genes, s_dev = pheno_ref.shape
    rperms, samples = perms_ref.shape
    spot = (pair * samps + samp) * s_dev
    for copy in copies:
        copy.wait()

    pheno = pheno_ref[...].astype(jnp.float32)
    perms = perms_ref[...] - spot
    perms = jnp.concatenate([perms, perms], axis=1)
    rows = []
    for g in range(genes):
        drawn = jnp.zeros(perms.shape, jnp.float32)
        for s in range(s_dev):
            drawn = jnp.where(perms == s, pheno[g : g + 1, s : s + 1], drawn)
        rows += [drawn[r : r + 1, t : t + LANES] for r in range(rperms) for t in range(0, 2 * samples, LANES)]
    if wave_ref.shape[0] > len(rows):
        rows.append(jnp.zeros((wave_ref.shape[0] - len(rows), LANES), jnp.float32))
    wave = jnp.concatenate(rows, axis=0).astype(wave_ref.dtype)
    wave_ref[...] = wave

    own_side, far_side = offsets(pair_count, 0), offsets(pair_count, 1)
    for i, (even, odd) in enumerate(zip(own_side, far_side)):
        for ref, core in ((keep_ref, samp), (give_ref, samps - 1 - samp)):
            n = shifted(pair, jnp.where(core == 0, even, odd), pair_count)
            for j in range(2):
                start = pl.multiple_of(pairs_ref[j, n] * TILE, TILE)
                place = i * BLOCK + j * TILE
                ref[place : place + TILE, :] = grid_ref[pl.ds(start, TILE), :]
    give_ref[len(own_side) * BLOCK :, :] = wave


def stat_kernel(pair_count, samps, wave_ref, keep_ref, give_ref, near_ref, *refs):
    far = pair_count // 2 - 1
    own_refs, mate_refs = refs[:far], refs[far : 2 * far]
    out_hbm, got_ref, out_ref, sems = refs[2 * far :]
    pair, samp = lax.axis_index("pair"), lax.axis_index("samp")
    other = samps - 1 - samp

    def place(offset, core, block):
        got_ref[shifted(pair, offset, pair_count, -1) * samps + core] = block

    even, odd = offsets(pair_count, 0), offsets(pair_count, 1)
    for arrived, core in ((own_refs, samp), (mate_refs, other)):
        for i, ref in enumerate(arrived):
            offset = jnp.where(core == 0, even[i], odd[i])
            place(offset, core, ref[:BLOCK, :])
            place(offset, samps - 1 - core, ref[BLOCK : 2 * BLOCK, :])
    place(even[far], samp, near_ref[:BLOCK, :])
    place(even[far], other, near_ref[BLOCK : 2 * BLOCK, :])
    itself = (far + 1) * BLOCK
    place(0, samp, keep_ref[itself : itself + BLOCK, :])
    place(0, other, give_ref[itself : itself + BLOCK, :])

    sources = got_ref.shape[0]
    s_dev = TILE * LANES // PANEL
    samples = sources * s_dev

    def by_samples(tiles, group):
        return tiles[:, group * s_dev : (group + 1) * s_dev, :].reshape(samples, LANES)

    panel_a = got_ref[:, 0:TILE, :].astype(jnp.float32)
    panel_b = got_ref[:, TILE:BLOCK, :].astype(jnp.float32)
    tile_b = jnp.where(samp == 0, panel_b[:, : TILE // 2], panel_b[:, TILE // 2 :])

    count = jnp.float32(samples)
    geno_b = jnp.concatenate([by_samples(tile_b, q) for q in range(TILE // 2 // s_dev)], axis=1)
    marg_b = jnp.sum(geno_b, axis=0, keepdims=True)
    centred = (geno_b - marg_b / count) * (samples**-0.5)
    b_hi = centred.astype(jnp.bfloat16)
    b_lo = (centred - b_hi.astype(jnp.float32)).astype(jnp.bfloat16)
    b_both = jnp.concatenate([b_hi, b_lo], axis=0)

    wave = wave_ref[...].astype(jnp.float32)
    for ref in (*own_refs, *mate_refs, near_ref):
        wave = wave + ref[2 * BLOCK :, :].astype(jnp.float32)
    tiles = 2 * samples // LANES
    yrows = [
        jnp.concatenate([wave[k * tiles + t : k * tiles + t + 1] for t in range(tiles)], axis=1)
        for k in range(out_ref.shape[0])
    ]
    yall = jnp.concatenate(yrows, axis=0)
    tail = jnp.dot(yall.astype(jnp.bfloat16), b_both, preferred_element_type=jnp.float32) / count
    c_hi = tail.astype(jnp.bfloat16).astype(jnp.float32)
    c_lo = tail - c_hi

    rows = []
    for q in range(TILE // s_dev):
        geno_a = by_samples(panel_a, q)
        rows.append(jnp.concatenate([geno_a, geno_a], axis=0).astype(jnp.bfloat16).T)
    copies = []
    for k, yrow in enumerate(yrows):
        yrow = yrow.astype(jnp.bfloat16)
        tails = [jnp.broadcast_to(c[k : k + 1], geno_b.shape).astype(jnp.bfloat16) for c in (c_hi, c_lo)]
        right = jnp.concatenate([b_both] + tails, axis=0)
        for q, part in enumerate(rows):
            left = jnp.concatenate([part * yrow, -part], axis=1)
            piece = slice(q * LANES, (q + 1) * LANES)
            out_ref[k, piece, :] = jnp.dot(left, right, preferred_element_type=jnp.float32).astype(out_ref.dtype)
            copies.append(pltpu.make_async_copy(out_ref.at[k, piece], out_hbm.at[0, k, piece], sems.at[k, q]))
            copies[-1].start()
    for copy in copies:
        copy.wait()


def on_device(dosage, phenotype, perms, pairs):
    s_dev, snps = dosage.shape
    genes = phenotype.shape[0]
    samples = perms.shape[1]
    pair_count, samps = (lax.axis_size(axis) for axis in AXES)
    rounds = pair_count // 2 + 1
    stats = genes * perms.shape[0]
    rows = wave_rows(stats, samples)
    grid = dosage.reshape(s_dev, snps // LANES, LANES).transpose(1, 0, 2).reshape(-1, LANES)
    vmem = pl.BlockSpec(memory_space=pltpu.VMEM)
    hbm = pl.BlockSpec(memory_space=pltpu.HBM)

    def array(*shape):
        return jax.ShapeDtypeStruct(shape, dosage.dtype)

    keep, give, wave = pl.pallas_call(
        functools.partial(pack_kernel, pair_count, samps),
        out_shape=[array(rounds * BLOCK, LANES), array(rounds * BLOCK + rows, LANES), array(rows, LANES)],
        in_specs=[hbm, hbm, hbm, hbm],
        out_specs=[vmem, vmem, vmem],
        scratch_shapes=[
            pltpu.SMEM(pairs.shape[::-1], pairs.dtype),
            pltpu.VMEM(phenotype.shape, phenotype.dtype),
            pltpu.VMEM(perms.shape, perms.dtype),
            pltpu.VMEM(grid.shape, grid.dtype),
            pltpu.SemaphoreType.DMA((4,)),
        ],
        compiler_params=pltpu.CompilerParams(vmem_limit_bytes=8 * 1024 * 1024),
        name="pack",
    )(*[pltpu.with_memory_space_constraint(x, pltpu.HBM) for x in (pairs.T, phenotype, perms, grid)])

    swap = [(i, samps - 1 - i) for i in range(samps)]
    got = lax.ppermute(give, "samp", swap)
    wave = wave + got[rounds * BLOCK :]
    arrived = []
    for i in range(rounds - 1):
        blocks = slice(i * BLOCK, (i + 1) * BLOCK)
        message = jnp.concatenate([keep[blocks], got[blocks], wave], axis=0)
        route = [
            (p * samps + c, shifted(p, offsets(pair_count, c)[i], pair_count) * samps + c)
            for p in range(pair_count)
            for c in range(samps)
        ]
        arrived.append(lax.ppermute(message, AXES, route))
    *far, near = arrived
    mates = [lax.ppermute(a, "samp", swap) for a in far]
    half = PANEL // samps
    return pl.pallas_call(
        functools.partial(stat_kernel, pair_count, samps),
        out_shape=jax.ShapeDtypeStruct((1, stats, PANEL, half), jnp.bfloat16),
        in_specs=[vmem] * (4 + 2 * len(far)),
        out_specs=hbm,
        scratch_shapes=[
            pltpu.VMEM((pair_count * samps, BLOCK, LANES), dosage.dtype),
            pltpu.VMEM((stats, PANEL, half), jnp.bfloat16),
            pltpu.SemaphoreType.DMA((stats, PANEL // LANES)),
        ],
        compiler_params=pltpu.CompilerParams(vmem_limit_bytes=48 * 1024 * 1024),
        name="stat",
    )(wave, keep, got, near, *far, *mates)


def solution(mesh):
    placed = (P(("rep", "pair", "samp"), None), P(None, ("rep", "pair", "samp")), P(), P())
    return jax.shard_map(
        on_device,
        mesh=mesh,
        in_specs=placed,
        out_specs=P(("rep", "pair"), None, None, "samp"),
        check_vma=False,
    )
```

```python
import functools

import jax
import jax.numpy as jnp
from jax import lax
from jax.experimental import pallas as pl
from jax.experimental.pallas import tpu as pltpu
from jax.sharding import PartitionSpec as P

PANEL = 512
LANES = 128
TILE = 16
BLOCK = 2 * TILE
AXES = ("pair", "samp")


def offsets(pair_count, core):
    shared = pair_count - 2
    rest = [e for e in range(1, pair_count) if e != shared]
    mine = rest[: len(rest) // 2] if core == 0 else rest[len(rest) // 2 :]
    if core == 0:
        mine = mine[1:] + mine[:1]
    return mine[1:] + mine[:1] + [shared, 0]


def shifted(pair, offset, pair_count, sign=1):
    high = (pair // 2 + sign * (offset // 2) + pair_count // 2) % (pair_count // 2)
    return high * 2 + (pair + offset) % 2


def wave_rows(stats, samples):
    return -(-stats * 2 * samples // LANES // 8) * 8


def pack_kernel(
    pair_count, samps, pairs_hbm, pheno_hbm, perms_hbm, grid_hbm, keep_ref, give_ref, wave_ref, pairs_ref, pheno_ref, perms_ref, grid_ref, sems
):
    fetched = ((pairs_hbm, pairs_ref), (grid_hbm, grid_ref), (pheno_hbm, pheno_ref), (perms_hbm, perms_ref))
    copies = [pltpu.make_async_copy(source, target, sems.at[i]) for i, (source, target) in enumerate(fetched)]
    for copy in copies:
        copy.start()
    pair, samp = lax.axis_index("pair"), lax.axis_index("samp")
    genes, s_dev = pheno_ref.shape
    rperms, samples = perms_ref.shape
    spot = (pair * samps + samp) * s_dev
    for copy in copies:
        copy.wait()

    pheno = pheno_ref[...].astype(jnp.float32)
    perms = perms_ref[...] - spot
    perms = jnp.concatenate([perms, perms], axis=1)
    rows = []
    for g in range(genes):
        drawn = jnp.zeros(perms.shape, jnp.float32)
        for s in range(s_dev):
            drawn = jnp.where(perms == s, pheno[g : g + 1, s : s + 1], drawn)
        rows += [drawn[r : r + 1, t : t + LANES] for r in range(rperms) for t in range(0, 2 * samples, LANES)]
    if wave_ref.shape[0] > len(rows):
        rows.append(jnp.zeros((wave_ref.shape[0] - len(rows), LANES), jnp.float32))
    wave = jnp.concatenate(rows, axis=0).astype(wave_ref.dtype)
    wave_ref[...] = wave

    own_side, far_side = offsets(pair_count, 0), offsets(pair_count, 1)
    for i, (even, odd) in enumerate(zip(own_side, far_side)):
        for ref, core in ((keep_ref, samp), (give_ref, samps - 1 - samp)):
            n = shifted(pair, jnp.where(core == 0, even, odd), pair_count)
            for j in range(2):
                start = pl.multiple_of(pairs_ref[j, n] * TILE, TILE)
                place = i * BLOCK + j * TILE
                ref[place : place + TILE, :] = grid_ref[pl.ds(start, TILE), :]
    give_ref[len(own_side) * BLOCK :, :] = wave


def stat_kernel(pair_count, samps, wave_ref, keep_ref, give_ref, near_ref, *refs):
    far = pair_count // 2 - 1
    own_refs, mate_refs = refs[:far], refs[far : 2 * far]
    out_hbm, got_ref, out_ref, sems = refs[2 * far :]
    pair, samp = lax.axis_index("pair"), lax.axis_index("samp")
    other = samps - 1 - samp

    def place(offset, core, block):
        got_ref[shifted(pair, offset, pair_count, -1) * samps + core] = block

    even, odd = offsets(pair_count, 0), offsets(pair_count, 1)
    for arrived, core in ((own_refs, samp), (mate_refs, other)):
        for i, ref in enumerate(arrived):
            offset = jnp.where(core == 0, even[i], odd[i])
            place(offset, core, ref[:BLOCK, :])
            place(offset, samps - 1 - core, ref[BLOCK : 2 * BLOCK, :])
    place(even[far], samp, near_ref[:BLOCK, :])
    place(even[far], other, near_ref[BLOCK : 2 * BLOCK, :])
    itself = (far + 1) * BLOCK
    place(0, samp, keep_ref[itself : itself + BLOCK, :])
    place(0, other, give_ref[itself : itself + BLOCK, :])

    sources = got_ref.shape[0]
    s_dev = TILE * LANES // PANEL
    samples = sources * s_dev

    def by_samples(tiles, group):
        return tiles[:, group * s_dev : (group + 1) * s_dev, :].reshape(samples, LANES)

    panel_a = got_ref[:, 0:TILE, :].astype(jnp.float32)
    panel_b = got_ref[:, TILE:BLOCK, :].astype(jnp.float32)
    tile_b = jnp.where(samp == 0, panel_b[:, : TILE // 2], panel_b[:, TILE // 2 :])

    count = jnp.float32(samples)
    geno_b = jnp.concatenate([by_samples(tile_b, q) for q in range(TILE // 2 // s_dev)], axis=1)
    marg_b = jnp.sum(geno_b, axis=0, keepdims=True)
    centred = (geno_b - marg_b / count) * (samples**-0.5)
    b_hi = centred.astype(jnp.bfloat16)
    b_lo = (centred - b_hi.astype(jnp.float32)).astype(jnp.bfloat16)
    b_both = jnp.concatenate([b_hi, b_lo], axis=0)

    wave = wave_ref[...].astype(jnp.float32)
    for ref in (*own_refs, *mate_refs, near_ref):
        wave = wave + ref[2 * BLOCK :, :].astype(jnp.float32)
    tiles = 2 * samples // LANES
    yrows = [
        jnp.concatenate([wave[k * tiles + t : k * tiles + t + 1] for t in range(tiles)], axis=1)
        for k in range(out_ref.shape[0])
    ]
    yall = jnp.concatenate(yrows, axis=0)
    tail = jnp.dot(yall.astype(jnp.bfloat16), b_both, preferred_element_type=jnp.float32) / count
    c_hi = tail.astype(jnp.bfloat16).astype(jnp.float32)
    c_lo = tail - c_hi

    rows = []
    for q in range(TILE // s_dev):
        geno_a = by_samples(panel_a, q)
        rows.append(jnp.concatenate([geno_a, geno_a], axis=0).astype(jnp.bfloat16).T)
    rows = jnp.concatenate(rows, axis=0)
    minus = -rows
    copies = []
    for k, yrow in enumerate(yrows):
        tails = [jnp.broadcast_to(c[k : k + 1], geno_b.shape).astype(jnp.bfloat16) for c in (c_hi, c_lo)]
        right = jnp.concatenate([b_both] + tails, axis=0)
        left = jnp.concatenate([rows * yrow.astype(jnp.bfloat16), minus], axis=1)
        out_ref[k] = jnp.dot(left, right, preferred_element_type=jnp.float32).astype(out_ref.dtype)
        copies.append(pltpu.make_async_copy(out_ref.at[k], out_hbm.at[0, k], sems.at[k]))
        copies[-1].start()
    for copy in copies:
        copy.wait()


def on_device(dosage, phenotype, perms, pairs):
    s_dev, snps = dosage.shape
    genes = phenotype.shape[0]
    samples = perms.shape[1]
    pair_count, samps = (lax.axis_size(axis) for axis in AXES)
    rounds = pair_count // 2 + 1
    stats = genes * perms.shape[0]
    rows = wave_rows(stats, samples)
    grid = dosage.reshape(s_dev, snps // LANES, LANES).transpose(1, 0, 2).reshape(-1, LANES)
    vmem = pl.BlockSpec(memory_space=pltpu.VMEM)
    hbm = pl.BlockSpec(memory_space=pltpu.HBM)

    def array(*shape):
        return jax.ShapeDtypeStruct(shape, dosage.dtype)

    keep, give, wave = pl.pallas_call(
        functools.partial(pack_kernel, pair_count, samps),
        out_shape=[array(rounds * BLOCK, LANES), array(rounds * BLOCK + rows, LANES), array(rows, LANES)],
        in_specs=[hbm, hbm, hbm, hbm],
        out_specs=[vmem, vmem, vmem],
        scratch_shapes=[
            pltpu.SMEM(pairs.shape[::-1], pairs.dtype),
            pltpu.VMEM(phenotype.shape, phenotype.dtype),
            pltpu.VMEM(perms.shape, perms.dtype),
            pltpu.VMEM(grid.shape, grid.dtype),
            pltpu.SemaphoreType.DMA((4,)),
        ],
        compiler_params=pltpu.CompilerParams(vmem_limit_bytes=8 * 1024 * 1024),
        name="pack",
    )(*[pltpu.with_memory_space_constraint(x, pltpu.HBM) for x in (pairs.T, phenotype, perms, grid)])

    swap = [(i, samps - 1 - i) for i in range(samps)]
    got = lax.ppermute(give, "samp", swap)
    wave = wave + got[rounds * BLOCK :]
    arrived = []
    for i in range(rounds - 1):
        blocks = slice(i * BLOCK, (i + 1) * BLOCK)
        message = jnp.concatenate([keep[blocks], got[blocks], wave], axis=0)
        route = [
            (p * samps + c, shifted(p, offsets(pair_count, c)[i], pair_count) * samps + c)
            for p in range(pair_count)
            for c in range(samps)
        ]
        arrived.append(lax.ppermute(message, AXES, route))
    *far, near = arrived
    mates = [lax.ppermute(a, "samp", swap) for a in far]
    half = PANEL // samps
    return pl.pallas_call(
        functools.partial(stat_kernel, pair_count, samps),
        out_shape=jax.ShapeDtypeStruct((1, stats, PANEL, half), jnp.bfloat16),
        in_specs=[vmem] * (4 + 2 * len(far)),
        out_specs=hbm,
        scratch_shapes=[
            pltpu.VMEM((pair_count * samps, BLOCK, LANES), dosage.dtype),
            pltpu.VMEM((stats, PANEL, half), jnp.bfloat16),
            pltpu.SemaphoreType.DMA((stats,)),
        ],
        compiler_params=pltpu.CompilerParams(vmem_limit_bytes=48 * 1024 * 1024),
        name="stat",
    )(wave, keep, got, near, *far, *mates)


def solution(mesh):
    placed = (P(("rep", "pair", "samp"), None), P(None, ("rep", "pair", "samp")), P(), P())
    return jax.shard_map(
        on_device,
        mesh=mesh,
        in_specs=placed,
        out_specs=P(("rep", "pair"), None, None, "samp"),
        check_vma=False,
    )
```

```python
import functools

import jax
import jax.numpy as jnp
from jax import lax
from jax.experimental import pallas as pl
from jax.experimental.pallas import tpu as pltpu
from jax.sharding import PartitionSpec as P

PANEL = 512
LANES = 128
TILE = 16
BLOCK = 2 * TILE
AXES = ("pair", "samp")


def offsets(pair_count, core):
    shared = pair_count - 2
    rest = [e for e in range(1, pair_count) if e != shared]
    mine = rest[: len(rest) // 2] if core == 0 else rest[len(rest) // 2 :]
    if core == 0:
        mine = mine[1:] + mine[:1]
    return mine[1:] + mine[:1] + [shared, 0]


def shifted(pair, offset, pair_count, sign=1):
    high = (pair // 2 + sign * (offset // 2) + pair_count // 2) % (pair_count // 2)
    return high * 2 + (pair + offset) % 2


def wave_rows(stats, samples):
    return -(-stats * 2 * samples // LANES // 8) * 8


def pack_kernel(
    pair_count, samps, pairs_hbm, pheno_hbm, perms_hbm, grid_hbm, keep_ref, give_ref, wave_ref, pairs_ref, pheno_ref, perms_ref, grid_ref, sems
):
    fetched = ((pairs_hbm, pairs_ref), (grid_hbm, grid_ref), (pheno_hbm, pheno_ref), (perms_hbm, perms_ref))
    copies = [pltpu.make_async_copy(source, target, sems.at[i]) for i, (source, target) in enumerate(fetched)]
    for copy in copies:
        copy.start()
    pair, samp = lax.axis_index("pair"), lax.axis_index("samp")
    genes, s_dev = pheno_ref.shape
    rperms, samples = perms_ref.shape
    spot = (pair * samps + samp) * s_dev
    for copy in copies:
        copy.wait()

    pheno = pheno_ref[...].astype(jnp.float32)
    perms = perms_ref[...] - spot
    perms = jnp.concatenate([perms, perms], axis=1)
    rows = []
    for g in range(genes):
        drawn = jnp.zeros(perms.shape, jnp.float32)
        for s in range(s_dev):
            drawn = jnp.where(perms == s, pheno[g : g + 1, s : s + 1], drawn)
        rows += [drawn[r : r + 1, t : t + LANES] for r in range(rperms) for t in range(0, 2 * samples, LANES)]
    if wave_ref.shape[0] > len(rows):
        rows.append(jnp.zeros((wave_ref.shape[0] - len(rows), LANES), jnp.float32))
    wave = jnp.concatenate(rows, axis=0).astype(wave_ref.dtype)
    wave_ref[...] = wave

    own_side, far_side = offsets(pair_count, 0), offsets(pair_count, 1)
    for i, (even, odd) in enumerate(zip(own_side, far_side)):
        for ref, core in ((keep_ref, samp), (give_ref, samps - 1 - samp)):
            n = shifted(pair, jnp.where(core == 0, even, odd), pair_count)
            for j in range(2):
                start = pl.multiple_of(pairs_ref[j, n] * TILE, TILE)
                place = i * BLOCK + j * TILE
                ref[place : place + TILE, :] = grid_ref[pl.ds(start, TILE), :]
    give_ref[len(own_side) * BLOCK :, :] = wave


def stat_kernel(pair_count, samps, wave_ref, keep_ref, give_ref, near_ref, *refs):
    far = pair_count // 2 - 1
    own_refs, mate_refs = refs[:far], refs[far : 2 * far]
    out_hbm, got_ref, out_ref, sems = refs[2 * far :]
    pair, samp = lax.axis_index("pair"), lax.axis_index("samp")
    other = samps - 1 - samp

    def place(offset, core, block):
        got_ref[shifted(pair, offset, pair_count, -1) * samps + core] = block

    even, odd = offsets(pair_count, 0), offsets(pair_count, 1)
    for arrived, core in ((own_refs, samp), (mate_refs, other)):
        for i, ref in enumerate(arrived):
            offset = jnp.where(core == 0, even[i], odd[i])
            place(offset, core, ref[:BLOCK, :])
            place(offset, samps - 1 - core, ref[BLOCK : 2 * BLOCK, :])
    place(even[far], samp, near_ref[:BLOCK, :])
    place(even[far], other, near_ref[BLOCK : 2 * BLOCK, :])
    itself = (far + 1) * BLOCK
    place(0, samp, keep_ref[itself : itself + BLOCK, :])
    place(0, other, give_ref[itself : itself + BLOCK, :])

    sources = got_ref.shape[0]
    s_dev = TILE * LANES // PANEL
    samples = sources * s_dev

    def by_samples(tiles, group):
        return tiles[:, group * s_dev : (group + 1) * s_dev, :].reshape(samples, LANES)

    panel_a = got_ref[:, 0:TILE, :].astype(jnp.float32)
    panel_b = got_ref[:, TILE:BLOCK, :].astype(jnp.float32)
    tile_b = jnp.where(samp == 0, panel_b[:, : TILE // 2], panel_b[:, TILE // 2 :])

    count = jnp.float32(samples)
    geno_b = jnp.concatenate([by_samples(tile_b, q) for q in range(TILE // 2 // s_dev)], axis=1)
    marg_b = jnp.sum(geno_b, axis=0, keepdims=True)
    centred = (geno_b - marg_b / count) * (samples**-0.5)
    b_hi = centred.astype(jnp.bfloat16)
    b_lo = (centred - b_hi.astype(jnp.float32)).astype(jnp.bfloat16)
    b_both = jnp.concatenate([b_hi, b_lo], axis=0)

    wave = wave_ref[...].astype(jnp.float32)
    for ref in (*own_refs, *mate_refs, near_ref):
        wave = wave + ref[2 * BLOCK :, :].astype(jnp.float32)
    tiles = 2 * samples // LANES
    yrows = [
        jnp.concatenate([wave[k * tiles + t : k * tiles + t + 1] for t in range(tiles)], axis=1)
        for k in range(out_ref.shape[0])
    ]
    yall = jnp.concatenate(yrows, axis=0)
    tail = jnp.dot(yall.astype(jnp.bfloat16), b_both, preferred_element_type=jnp.float32) / count
    c_hi = tail.astype(jnp.bfloat16).astype(jnp.float32)
    c_lo = tail - c_hi

    rows = []
    for q in range(TILE // s_dev):
        geno_a = by_samples(panel_a, q)
        rows.append(jnp.concatenate([geno_a, geno_a], axis=0).astype(jnp.bfloat16).T)
    rows = jnp.concatenate(rows, axis=0)
    minus = -rows
    copies = []
    for k, yrow in enumerate(yrows):
        tails = [jnp.broadcast_to(c[k : k + 1], geno_b.shape).astype(jnp.bfloat16) for c in (c_hi, c_lo)]
        right = jnp.concatenate([b_both] + tails, axis=0)
        left = jnp.concatenate([rows * yrow.astype(jnp.bfloat16), minus], axis=1)
        out_ref[k] = jnp.dot(left, right, preferred_element_type=jnp.float32).astype(out_ref.dtype)
        for part in range(2):
            piece = slice(part * PANEL // 2, (part + 1) * PANEL // 2)
            copies.append(pltpu.make_async_copy(out_ref.at[k, piece], out_hbm.at[0, k, piece], sems.at[k, part]))
            copies[-1].start(priority=part)
    for copy in copies:
        copy.wait()


def on_device(dosage, phenotype, perms, pairs):
    s_dev, snps = dosage.shape
    genes = phenotype.shape[0]
    samples = perms.shape[1]
    pair_count, samps = (lax.axis_size(axis) for axis in AXES)
    rounds = pair_count // 2 + 1
    stats = genes * perms.shape[0]
    rows = wave_rows(stats, samples)
    grid = dosage.reshape(s_dev, snps // LANES, LANES).transpose(1, 0, 2).reshape(-1, LANES)
    vmem = pl.BlockSpec(memory_space=pltpu.VMEM)
    hbm = pl.BlockSpec(memory_space=pltpu.HBM)

    def array(*shape):
        return jax.ShapeDtypeStruct(shape, dosage.dtype)

    keep, give, wave = pl.pallas_call(
        functools.partial(pack_kernel, pair_count, samps),
        out_shape=[array(rounds * BLOCK, LANES), array(rounds * BLOCK + rows, LANES), array(rows, LANES)],
        in_specs=[hbm, hbm, hbm, hbm],
        out_specs=[vmem, vmem, vmem],
        scratch_shapes=[
            pltpu.SMEM(pairs.shape[::-1], pairs.dtype),
            pltpu.VMEM(phenotype.shape, phenotype.dtype),
            pltpu.VMEM(perms.shape, perms.dtype),
            pltpu.VMEM(grid.shape, grid.dtype),
            pltpu.SemaphoreType.DMA((4,)),
        ],
        compiler_params=pltpu.CompilerParams(vmem_limit_bytes=8 * 1024 * 1024),
        name="pack",
    )(*[pltpu.with_memory_space_constraint(x, pltpu.HBM) for x in (pairs.T, phenotype, perms, grid)])

    swap = [(i, samps - 1 - i) for i in range(samps)]
    got = lax.ppermute(give, "samp", swap)
    wave = wave + got[rounds * BLOCK :]
    arrived = []
    for i in range(rounds - 1):
        blocks = slice(i * BLOCK, (i + 1) * BLOCK)
        message = jnp.concatenate([keep[blocks], got[blocks], wave], axis=0)
        route = [
            (p * samps + c, shifted(p, offsets(pair_count, c)[i], pair_count) * samps + c)
            for p in range(pair_count)
            for c in range(samps)
        ]
        arrived.append(lax.ppermute(message, AXES, route))
    *far, near = arrived
    mates = [lax.ppermute(a, "samp", swap) for a in far]
    half = PANEL // samps
    return pl.pallas_call(
        functools.partial(stat_kernel, pair_count, samps),
        out_shape=jax.ShapeDtypeStruct((1, stats, PANEL, half), jnp.bfloat16),
        in_specs=[vmem] * (4 + 2 * len(far)),
        out_specs=hbm,
        scratch_shapes=[
            pltpu.VMEM((pair_count * samps, BLOCK, LANES), dosage.dtype),
            pltpu.VMEM((stats, PANEL, half), jnp.bfloat16),
            pltpu.SemaphoreType.DMA((stats, 2)),
        ],
        compiler_params=pltpu.CompilerParams(vmem_limit_bytes=48 * 1024 * 1024),
        name="stat",
    )(wave, keep, got, near, *far, *mates)


def solution(mesh):
    placed = (P(("rep", "pair", "samp"), None), P(None, ("rep", "pair", "samp")), P(), P())
    return jax.shard_map(
        on_device,
        mesh=mesh,
        in_specs=placed,
        out_specs=P(("rep", "pair"), None, None, "samp"),
        check_vma=False,
    )
```

```python
import functools

import jax
import jax.numpy as jnp
from jax import lax
from jax.experimental import pallas as pl
from jax.experimental.pallas import tpu as pltpu
from jax.sharding import PartitionSpec as P

PANEL = 512
LANES = 128
TILE = 16
BLOCK = 2 * TILE
AXES = ("pair", "samp")


def offsets(pair_count, core):
    shared = pair_count - 2
    rest = [e for e in range(1, pair_count) if e != shared]
    mine = rest[: len(rest) // 2] if core == 0 else rest[len(rest) // 2 :]
    if core == 0:
        mine = mine[1:] + mine[:1]
    return mine[1:] + mine[:1] + [shared, 0]


def shifted(pair, offset, pair_count, sign=1):
    turn = pair_count // 2
    high = (pair >> 1) + sign * (offset >> 1)
    high = high - turn * (high >= turn) + turn * (high < 0)
    return high * 2 + ((pair ^ offset) & 1)


def wave_rows(stats, samples):
    return -(-stats * 2 * samples // LANES // 8) * 8


def pack_kernel(
    pair_count, samps, pairs_hbm, pheno_hbm, perms_hbm, grid_hbm, keep_ref, give_ref, wave_ref, pairs_ref, pheno_ref, perms_ref, grid_ref, sems
):
    fetched = ((pairs_hbm, pairs_ref), (grid_hbm, grid_ref), (pheno_hbm, pheno_ref), (perms_hbm, perms_ref))
    copies = [pltpu.make_async_copy(source, target, sems.at[i]) for i, (source, target) in enumerate(fetched)]
    for copy in copies:
        copy.start()
    pair, samp = lax.axis_index("pair"), lax.axis_index("samp")
    genes, s_dev = pheno_ref.shape
    rperms, samples = perms_ref.shape
    spot = (pair * samps + samp) * s_dev
    for copy in copies[:2]:
        copy.wait()

    own_side, far_side = offsets(pair_count, 0), offsets(pair_count, 1)
    for i, (even, odd) in enumerate(zip(own_side, far_side)):
        for ref, core in ((keep_ref, samp), (give_ref, samps - 1 - samp)):
            n = shifted(pair, jnp.where(core == 0, even, odd), pair_count)
            for j in range(2):
                start = pl.multiple_of(pairs_ref[j, n] * TILE, TILE)
                place = i * BLOCK + j * TILE
                ref[place : place + TILE, :] = grid_ref[pl.ds(start, TILE), :]

    for copy in copies[2:]:
        copy.wait()
    pheno = pheno_ref[...].astype(jnp.float32)
    perms = perms_ref[...] - spot
    perms = jnp.concatenate([perms, perms], axis=1)
    rows = []
    for g in range(genes):
        drawn = jnp.zeros(perms.shape, jnp.float32)
        for s in range(s_dev):
            drawn = jnp.where(perms == s, pheno[g : g + 1, s : s + 1], drawn)
        rows += [drawn[r : r + 1, t : t + LANES] for r in range(rperms) for t in range(0, 2 * samples, LANES)]
    if wave_ref.shape[0] > len(rows):
        rows.append(jnp.zeros((wave_ref.shape[0] - len(rows), LANES), jnp.float32))
    wave = jnp.concatenate(rows, axis=0).astype(wave_ref.dtype)
    wave_ref[...] = wave
    give_ref[len(own_side) * BLOCK :, :] = wave


def stat_kernel(pair_count, samps, wave_ref, keep_ref, give_ref, near_ref, *refs):
    far = pair_count // 2 - 1
    own_refs, mate_refs = refs[:far], refs[far : 2 * far]
    out_hbm, got_ref, out_ref, sems = refs[2 * far :]
    pair, samp = lax.axis_index("pair"), lax.axis_index("samp")
    other = samps - 1 - samp

    def place(offset, core, block):
        got_ref[shifted(pair, offset, pair_count, -1) * samps + core] = block

    even, odd = offsets(pair_count, 0), offsets(pair_count, 1)
    for arrived, core in ((own_refs, samp), (mate_refs, other)):
        for i, ref in enumerate(arrived):
            offset = jnp.where(core == 0, even[i], odd[i])
            place(offset, core, ref[:BLOCK, :])
            place(offset, samps - 1 - core, ref[BLOCK : 2 * BLOCK, :])
    place(even[far], samp, near_ref[:BLOCK, :])
    place(even[far], other, near_ref[BLOCK : 2 * BLOCK, :])
    itself = (far + 1) * BLOCK
    place(0, samp, keep_ref[itself : itself + BLOCK, :])
    place(0, other, give_ref[itself : itself + BLOCK, :])

    sources = got_ref.shape[0]
    s_dev = TILE * LANES // PANEL
    samples = sources * s_dev

    def by_samples(tiles):
        groups = tiles.shape[1] // s_dev
        if groups * s_dev != 8 or groups != 2:
            return [tiles[:, g * s_dev : (g + 1) * s_dev, :].reshape(samples, LANES) for g in range(groups)]
        couples = tiles.reshape(sources // 2, 2, 8, LANES)
        one, two = couples[:, 0], couples[:, 1]
        upper = lax.broadcasted_iota(jnp.int32, one.shape, 1) < s_dev
        first = jnp.where(upper, one, pltpu.roll(two, s_dev, 1))
        second = jnp.where(upper, pltpu.roll(one, s_dev, 1), two)
        return [x.reshape(samples, LANES) for x in (first, second)]

    panel_a = got_ref[:, 0:TILE, :].astype(jnp.float32)
    panel_b = got_ref[:, TILE:BLOCK, :].astype(jnp.float32)
    tile_b = jnp.where(samp == 0, panel_b[:, : TILE // 2], panel_b[:, TILE // 2 :])

    count = jnp.float32(samples)
    geno_b = jnp.concatenate(by_samples(tile_b), axis=1)
    marg_b = jnp.sum(geno_b, axis=0, keepdims=True)
    centred = (geno_b - marg_b / count) * (samples**-0.5)
    b_hi = centred.astype(jnp.bfloat16)
    b_lo = (centred - b_hi.astype(jnp.float32)).astype(jnp.bfloat16)
    b_both = jnp.concatenate([b_hi, b_lo], axis=0)

    wave = wave_ref[...].astype(jnp.float32)
    for ref in (*own_refs, *mate_refs, near_ref):
        wave = wave + ref[2 * BLOCK :, :].astype(jnp.float32)
    tiles = 2 * samples // LANES
    yrows = [
        jnp.concatenate([wave[k * tiles + t : k * tiles + t + 1] for t in range(tiles)], axis=1)
        for k in range(out_ref.shape[0])
    ]
    yall = jnp.concatenate(yrows, axis=0)
    tail = jnp.dot(yall.astype(jnp.bfloat16), b_both, preferred_element_type=jnp.float32) / count
    c_hi = tail.astype(jnp.bfloat16).astype(jnp.float32)
    c_lo = tail - c_hi

    rows = []
    for geno_a in by_samples(panel_a[:, : TILE // 2]) + by_samples(panel_a[:, TILE // 2 :]):
        rows.append(jnp.concatenate([geno_a, geno_a], axis=0).astype(jnp.bfloat16).T)
    rows = jnp.concatenate(rows, axis=0)
    minus = -rows
    copies = []
    for k, yrow in enumerate(yrows):
        tails = [jnp.broadcast_to(c[k : k + 1], (TILE, c.shape[1])).astype(jnp.bfloat16) for c in (c_hi, c_lo)]
        right = jnp.concatenate([b_both] + [t for t in tails for _ in range(samples // TILE)], axis=0)
        left = jnp.concatenate([rows * yrow.astype(jnp.bfloat16), minus], axis=1)
        out_ref[k] = jnp.dot(left, right, preferred_element_type=jnp.float32).astype(out_ref.dtype)
        copies.append(pltpu.make_async_copy(out_ref.at[k], out_hbm.at[0, k], sems.at[k]))
        copies[-1].start()
    for copy in copies:
        copy.wait()


def on_device(dosage, phenotype, perms, pairs):
    s_dev, snps = dosage.shape
    genes = phenotype.shape[0]
    samples = perms.shape[1]
    pair_count, samps = (lax.axis_size(axis) for axis in AXES)
    rounds = pair_count // 2 + 1
    stats = genes * perms.shape[0]
    rows = wave_rows(stats, samples)
    grid = dosage.reshape(s_dev, snps // LANES, LANES).transpose(1, 0, 2).reshape(-1, LANES)
    vmem = pl.BlockSpec(memory_space=pltpu.VMEM)
    hbm = pl.BlockSpec(memory_space=pltpu.HBM)

    def array(*shape):
        return jax.ShapeDtypeStruct(shape, dosage.dtype)

    keep, give, wave = pl.pallas_call(
        functools.partial(pack_kernel, pair_count, samps),
        out_shape=[array(rounds * BLOCK, LANES), array(rounds * BLOCK + rows, LANES), array(rows, LANES)],
        in_specs=[hbm, hbm, hbm, hbm],
        out_specs=[vmem, vmem, vmem],
        scratch_shapes=[
            pltpu.SMEM(pairs.shape[::-1], pairs.dtype),
            pltpu.VMEM(phenotype.shape, phenotype.dtype),
            pltpu.VMEM(perms.shape, perms.dtype),
            pltpu.VMEM(grid.shape, grid.dtype),
            pltpu.SemaphoreType.DMA((4,)),
        ],
        compiler_params=pltpu.CompilerParams(vmem_limit_bytes=8 * 1024 * 1024),
        name="pack",
    )(*[pltpu.with_memory_space_constraint(x, pltpu.HBM) for x in (pairs.T, phenotype, perms, grid)])

    swap = [(i, samps - 1 - i) for i in range(samps)]
    got = lax.ppermute(give, "samp", swap)
    wave = wave + got[rounds * BLOCK :]
    arrived = []
    for i in range(rounds - 1):
        blocks = slice(i * BLOCK, (i + 1) * BLOCK)
        message = jnp.concatenate([keep[blocks], got[blocks], wave], axis=0)
        route = [
            (p * samps + c, shifted(p, offsets(pair_count, c)[i], pair_count) * samps + c)
            for p in range(pair_count)
            for c in range(samps)
        ]
        arrived.append(lax.ppermute(message, AXES, route))
    *far, near = arrived
    mates = [lax.ppermute(a, "samp", swap) for a in far]
    half = PANEL // samps
    return pl.pallas_call(
        functools.partial(stat_kernel, pair_count, samps),
        out_shape=jax.ShapeDtypeStruct((1, stats, PANEL, half), jnp.bfloat16),
        in_specs=[vmem] * (4 + 2 * len(far)),
        out_specs=hbm,
        scratch_shapes=[
            pltpu.VMEM((pair_count * samps, BLOCK, LANES), dosage.dtype),
            pltpu.VMEM((stats, PANEL, half), jnp.bfloat16),
            pltpu.SemaphoreType.DMA((stats,)),
        ],
        compiler_params=pltpu.CompilerParams(vmem_limit_bytes=48 * 1024 * 1024),
        name="stat",
    )(wave, keep, got, near, *far, *mates)


def solution(mesh):
    placed = (P(("rep", "pair", "samp"), None), P(None, ("rep", "pair", "samp")), P(), P())
    return jax.shard_map(
        on_device,
        mesh=mesh,
        in_specs=placed,
        out_specs=P(("rep", "pair"), None, None, "samp"),
        check_vma=False,
    )
```

```python
import functools

import jax
import jax.numpy as jnp
from jax import lax
from jax.experimental import pallas as pl
from jax.experimental.pallas import tpu as pltpu
from jax.sharding import PartitionSpec as P

PANEL = 512
LANES = 128
TILE = 16
BLOCK = 2 * TILE
AXES = ("pair", "samp")


def offsets(pair_count, core):
    shared = pair_count - 2
    rest = [e for e in range(1, pair_count) if e != shared]
    mine = rest[: len(rest) // 2] if core == 0 else rest[len(rest) // 2 :]
    if core == 0:
        mine = mine[1:] + mine[:1]
    return mine + [shared, 0]


def shifted(pair, offset, pair_count, sign=1):
    turn = pair_count // 2
    high = (pair >> 1) + sign * (offset >> 1)
    high = high - turn * (high >= turn) + turn * (high < 0)
    return high * 2 + ((pair ^ offset) & 1)


def wave_rows(stats, samples):
    return -(-stats * 2 * samples // LANES // 8) * 8


def spread(pheno, perms, first, rows):
    genes, s_dev = pheno.shape
    samples = perms.shape[1]
    pheno = pheno.astype(jnp.float32)
    perms = perms - first
    perms = jnp.concatenate([perms, perms], axis=1)
    tiles = []
    for g in range(genes):
        drawn = jnp.zeros(perms.shape, jnp.float32)
        for s in range(s_dev):
            drawn = jnp.where(perms == s, pheno[g : g + 1, s : s + 1], drawn)
        tiles += [drawn[r : r + 1, t : t + LANES] for r in range(perms.shape[0]) for t in range(0, 2 * samples, LANES)]
    if rows > len(tiles):
        tiles.append(jnp.zeros((rows - len(tiles), LANES), jnp.float32))
    return jnp.concatenate(tiles, axis=0)


def pick_kernel(
    pair_count, samps, pairs_hbm, grid_hbm, pheno_hbm, perms_hbm, keep_ref, pick_ref, wave_ref, perms_ref, pairs_ref, grid_ref, pheno_ref, sems
):
    fetched = ((pairs_hbm, pairs_ref), (grid_hbm, grid_ref), (pheno_hbm, pheno_ref), (perms_hbm, perms_ref))
    copies = [pltpu.make_async_copy(source, target, sems.at[i]) for i, (source, target) in enumerate(fetched)]
    for copy in copies:
        copy.start()
    pair, samp = lax.axis_index("pair"), lax.axis_index("samp")
    shape = (TILE, pick_ref.shape[1])
    ahead = lax.broadcasted_iota(jnp.int32, shape, 1) - lax.broadcasted_iota(jnp.int32, shape, 0)
    for copy in copies:
        copy.wait()
    wave = spread(pheno_ref[...], perms_ref[...], (pair * samps + samp) * pheno_ref.shape[1], wave_ref.shape[0])
    wave_ref[...] = wave.astype(wave_ref.dtype)
    for i, (even, odd) in enumerate(zip(offsets(pair_count, 0), offsets(pair_count, 1))):
        n = shifted(pair, jnp.where(samp == 0, even, odd), pair_count)
        for j in range(2):
            start = pl.multiple_of(pairs_ref[j, n] * TILE, TILE)
            rows = slice(i * BLOCK + j * TILE, i * BLOCK + (j + 1) * TILE)
            keep_ref[rows, :] = grid_ref[pl.ds(start, TILE), :]
            pick_ref[rows, :] = jnp.where(ahead == start, 1.0, 0.0).astype(pick_ref.dtype)


def join_kernel(pair_count, samps, keep_ref, pick_ref, wave_ref, perms_ref, grid_ref, pheno_ref, mate_ref, both_ref, *out_refs):
    pair, samp = lax.axis_index("pair"), lax.axis_index("samp")
    first = (pair * samps + samps - 1 - samp) * pheno_ref.shape[1]
    wave = spread(pheno_ref[...], perms_ref[...], first, wave_ref.shape[0])
    wave = (wave_ref[...].astype(jnp.float32) + wave).astype(wave_ref.dtype)
    both_ref[...] = wave
    picked = jnp.dot(pick_ref[...], grid_ref[...], preferred_element_type=jnp.float32).astype(mate_ref.dtype)
    for i, ref in enumerate(out_refs):
        rows = slice(i * BLOCK, (i + 1) * BLOCK)
        ref[:BLOCK, :] = keep_ref[rows, :]
        ref[BLOCK : 2 * BLOCK, :] = picked[rows]
        ref[2 * BLOCK :, :] = wave
    mate_ref[...] = picked[len(out_refs) * BLOCK :]


def stat_kernel(pair_count, samps, wave_ref, keep_ref, mate_self_ref, near_ref, *refs):
    far = pair_count // 2 - 1
    own_refs, mate_refs = refs[:far], refs[far : 2 * far]
    out_hbm, got_ref, out_ref, sems = refs[2 * far :]
    pair, samp = lax.axis_index("pair"), lax.axis_index("samp")
    other = samps - 1 - samp

    def place(offset, core, block):
        got_ref[shifted(pair, offset, pair_count, -1) * samps + core] = block

    even, odd = offsets(pair_count, 0), offsets(pair_count, 1)
    for arrived, core in ((own_refs, samp), (mate_refs, other)):
        for i, ref in enumerate(arrived):
            offset = jnp.where(core == 0, even[i], odd[i])
            place(offset, core, ref[:BLOCK, :])
            place(offset, samps - 1 - core, ref[BLOCK : 2 * BLOCK, :])
    place(even[far], samp, near_ref[:BLOCK, :])
    place(even[far], other, near_ref[BLOCK : 2 * BLOCK, :])
    itself = (far + 1) * BLOCK
    place(0, samp, keep_ref[itself : itself + BLOCK, :])
    place(0, other, mate_self_ref[...])

    sources = got_ref.shape[0]
    s_dev = TILE * LANES // PANEL
    samples = sources * s_dev

    def by_samples(tiles):
        groups = tiles.shape[1] // s_dev
        if groups * s_dev != 8 or groups != 2:
            return [tiles[:, g * s_dev : (g + 1) * s_dev, :].reshape(samples, LANES) for g in range(groups)]
        couples = tiles.reshape(sources // 2, 2, 8, LANES)
        one, two = couples[:, 0], couples[:, 1]
        upper = lax.broadcasted_iota(jnp.int32, one.shape, 1) < s_dev
        first = jnp.where(upper, one, pltpu.roll(two, s_dev, 1))
        second = jnp.where(upper, pltpu.roll(one, s_dev, 1), two)
        return [x.reshape(samples, LANES) for x in (first, second)]

    panel_a = got_ref[:, 0:TILE, :].astype(jnp.float32)
    panel_b = got_ref[:, TILE:BLOCK, :].astype(jnp.float32)
    tile_b = jnp.where(samp == 0, panel_b[:, : TILE // 2], panel_b[:, TILE // 2 :])

    count = jnp.float32(samples)
    geno_b = jnp.concatenate(by_samples(tile_b), axis=1)
    marg_b = jnp.sum(geno_b, axis=0, keepdims=True)
    centred = (geno_b - marg_b / count) * (samples**-0.5)
    b_hi = centred.astype(jnp.bfloat16)
    b_lo = (centred - b_hi.astype(jnp.float32)).astype(jnp.bfloat16)
    b_both = jnp.concatenate([b_hi, b_lo], axis=0)

    wave = wave_ref[...].astype(jnp.float32)
    for ref in (*own_refs, *mate_refs, near_ref):
        wave = wave + ref[2 * BLOCK :, :].astype(jnp.float32)
    tiles = 2 * samples // LANES
    yrows = [
        jnp.concatenate([wave[k * tiles + t : k * tiles + t + 1] for t in range(tiles)], axis=1)
        for k in range(out_ref.shape[0])
    ]
    yall = jnp.concatenate(yrows, axis=0)
    tail = jnp.dot(yall.astype(jnp.bfloat16), b_both, preferred_element_type=jnp.float32) / count
    c_hi = tail.astype(jnp.bfloat16).astype(jnp.float32)
    c_lo = tail - c_hi

    rows = []
    for geno_a in by_samples(panel_a[:, : TILE // 2]) + by_samples(panel_a[:, TILE // 2 :]):
        rows.append(jnp.concatenate([geno_a, geno_a], axis=0).astype(jnp.bfloat16).T)
    rows = jnp.concatenate(rows, axis=0)
    minus = -rows
    copies = []
    for k, yrow in enumerate(yrows):
        tails = [jnp.broadcast_to(c[k : k + 1], (TILE, c.shape[1])).astype(jnp.bfloat16) for c in (c_hi, c_lo)]
        right = jnp.concatenate([b_both] + [t for t in tails for _ in range(samples // TILE)], axis=0)
        left = jnp.concatenate([rows * yrow.astype(jnp.bfloat16), minus], axis=1)
        out_ref[k] = jnp.dot(left, right, preferred_element_type=jnp.float32).astype(out_ref.dtype)
        copies.append(pltpu.make_async_copy(out_ref.at[k], out_hbm.at[0, k], sems.at[k]))
        copies[-1].start()
    for copy in copies:
        copy.wait()


def on_device(dosage, phenotype, perms, pairs):
    s_dev, snps = dosage.shape
    genes = phenotype.shape[0]
    samples = perms.shape[1]
    pair_count, samps = (lax.axis_size(axis) for axis in AXES)
    rounds = pair_count // 2 + 1
    stats = genes * perms.shape[0]
    rows = wave_rows(stats, samples)
    grid = dosage.reshape(s_dev, snps // LANES, LANES).transpose(1, 0, 2).reshape(-1, LANES)
    vmem = pl.BlockSpec(memory_space=pltpu.VMEM)
    hbm = pl.BlockSpec(memory_space=pltpu.HBM)

    def array(*shape):
        return jax.ShapeDtypeStruct(shape, dosage.dtype)

    swap = [(i, samps - 1 - i) for i in range(samps)]
    mate_dosage = lax.ppermute(dosage, "samp", swap)
    mate_pheno = lax.ppermute(phenotype, "samp", swap)
    params = pltpu.CompilerParams(vmem_limit_bytes=24 * 1024 * 1024)
    blocks = rounds * BLOCK
    keep, pick, wave, perms_near = pl.pallas_call(
        functools.partial(pick_kernel, pair_count, samps),
        out_shape=[
            array(blocks, LANES),
            array(blocks, grid.shape[0]),
            array(rows, LANES),
            jax.ShapeDtypeStruct(perms.shape, perms.dtype),
        ],
        in_specs=[hbm] * 4,
        out_specs=[vmem] * 4,
        scratch_shapes=[
            pltpu.SMEM(pairs.shape[::-1], pairs.dtype),
            pltpu.VMEM(grid.shape, grid.dtype),
            pltpu.VMEM(phenotype.shape, phenotype.dtype),
            pltpu.SemaphoreType.DMA((4,)),
        ],
        compiler_params=params,
        cost_estimate=pl.CostEstimate(flops=0, bytes_accessed=4 * blocks * LANES * 2, transcendentals=0),
        name="pick",
    )(*[pltpu.with_memory_space_constraint(x, pltpu.HBM) for x in (pairs.T, grid, phenotype, perms)])

    mate_grid = mate_dosage.reshape(s_dev, snps // LANES, LANES).transpose(1, 0, 2).reshape(-1, LANES)
    mate_self, wave, *messages = pl.pallas_call(
        functools.partial(join_kernel, pair_count, samps),
        out_shape=[array(BLOCK, LANES), array(rows, LANES)] + [array(2 * BLOCK + rows, LANES)] * (rounds - 1),
        in_specs=[vmem] * 6,
        out_specs=[vmem] * (rounds + 1),
        compiler_params=params,
        name="join",
    )(keep, pick, wave, perms_near, mate_grid, mate_pheno)

    arrived = []
    for i, message in enumerate(messages):
        route = [
            (p * samps + c, shifted(p, offsets(pair_count, c)[i], pair_count) * samps + c)
            for p in range(pair_count)
            for c in range(samps)
        ]
        arrived.append(lax.ppermute(message, AXES, route))
    *far, near = arrived
    mates = [lax.ppermute(a, "samp", swap) for a in far]
    half = PANEL // samps
    return pl.pallas_call(
        functools.partial(stat_kernel, pair_count, samps),
        out_shape=jax.ShapeDtypeStruct((1, stats, PANEL, half), jnp.bfloat16),
        in_specs=[vmem] * (4 + 2 * len(far)),
        out_specs=hbm,
        scratch_shapes=[
            pltpu.VMEM((pair_count * samps, BLOCK, LANES), dosage.dtype),
            pltpu.VMEM((stats, PANEL, half), jnp.bfloat16),
            pltpu.SemaphoreType.DMA((stats,)),
        ],
        compiler_params=pltpu.CompilerParams(vmem_limit_bytes=48 * 1024 * 1024),
        name="stat",
    )(wave, keep, mate_self, near, *far, *mates)


def solution(mesh):
    placed = (P(("rep", "pair", "samp"), None), P(None, ("rep", "pair", "samp")), P(), P())
    return jax.shard_map(
        on_device,
        mesh=mesh,
        in_specs=placed,
        out_specs=P(("rep", "pair"), None, None, "samp"),
        check_vma=False,
    )
```

```python
import functools

import jax
import jax.numpy as jnp
from jax import lax
from jax.experimental import pallas as pl
from jax.experimental.pallas import tpu as pltpu
from jax.sharding import PartitionSpec as P

PANEL = 512
LANES = 128
TILE = 16
BLOCK = 2 * TILE
AXES = ("pair", "samp")


def offsets(pair_count, core):
    shared = pair_count - 2
    rest = [e for e in range(1, pair_count) if e != shared]
    quarter = (len(rest) + 2) // 4
    middle = rest[quarter : quarter + len(rest) // 2]
    mine = [e for e in rest if e not in middle] if core == 0 else sorted(middle, key=lambda e: e % 2 == 0)
    return mine + [shared, 0]


def shifted(pair, offset, pair_count, sign=1):
    turn = pair_count // 2
    high = (pair >> 1) + sign * (offset >> 1)
    high = high - turn * (high >= turn) + turn * (high < 0)
    return high * 2 + ((pair ^ offset) & 1)


def wave_rows(stats, samples):
    return -(-stats * 2 * samples // LANES // 8) * 8


def spread(pheno, perms, first, rows):
    genes, s_dev = pheno.shape
    samples = perms.shape[1]
    pheno = pheno.astype(jnp.float32)
    perms = perms - first
    perms = jnp.concatenate([perms, perms], axis=1)
    tiles = []
    for g in range(genes):
        drawn = jnp.zeros(perms.shape, jnp.float32)
        for s in range(s_dev):
            drawn = jnp.where(perms == s, pheno[g : g + 1, s : s + 1], drawn)
        tiles += [drawn[r : r + 1, t : t + LANES] for r in range(perms.shape[0]) for t in range(0, 2 * samples, LANES)]
    if rows > len(tiles):
        tiles.append(jnp.zeros((rows - len(tiles), LANES), jnp.float32))
    return jnp.concatenate(tiles, axis=0)


def pick_kernel(
    pair_count, samps, pairs_hbm, grid_hbm, pheno_hbm, perms_hbm, keep_ref, pick_ref, wave_ref, perms_ref, pairs_ref, grid_ref, pheno_ref, sems
):
    fetched = ((pairs_hbm, pairs_ref), (grid_hbm, grid_ref), (pheno_hbm, pheno_ref), (perms_hbm, perms_ref))
    copies = [pltpu.make_async_copy(source, target, sems.at[i]) for i, (source, target) in enumerate(fetched)]
    for copy in copies:
        copy.start()
    pair, samp = lax.axis_index("pair"), lax.axis_index("samp")
    shape = (TILE, pick_ref.shape[1])
    ahead = lax.broadcasted_iota(jnp.int32, shape, 1) - lax.broadcasted_iota(jnp.int32, shape, 0)
    for copy in copies:
        copy.wait()
    wave = spread(pheno_ref[...], perms_ref[...], (pair * samps + samp) * pheno_ref.shape[1], wave_ref.shape[0])
    wave_ref[...] = wave.astype(wave_ref.dtype)
    for i, (even, odd) in enumerate(zip(offsets(pair_count, 0), offsets(pair_count, 1))):
        n = shifted(pair, jnp.where(samp == 0, even, odd), pair_count)
        for j in range(2):
            start = pl.multiple_of(pairs_ref[j, n] * TILE, TILE)
            rows = slice(i * BLOCK + j * TILE, i * BLOCK + (j + 1) * TILE)
            keep_ref[rows, :] = grid_ref[pl.ds(start, TILE), :]
            pick_ref[rows, :] = jnp.where(ahead == start, 1.0, 0.0).astype(pick_ref.dtype)


def join_kernel(pair_count, samps, keep_ref, pick_ref, wave_ref, perms_ref, grid_ref, pheno_ref, mate_ref, both_ref, *out_refs):
    pair, samp = lax.axis_index("pair"), lax.axis_index("samp")
    first = (pair * samps + samps - 1 - samp) * pheno_ref.shape[1]
    wave = spread(pheno_ref[...], perms_ref[...], first, wave_ref.shape[0])
    wave = (wave_ref[...].astype(jnp.float32) + wave).astype(wave_ref.dtype)
    both_ref[...] = wave
    picked = jnp.dot(pick_ref[...], grid_ref[...], preferred_element_type=jnp.float32).astype(mate_ref.dtype)
    for i, ref in enumerate(out_refs):
        rows = slice(i * BLOCK, (i + 1) * BLOCK)
        ref[:BLOCK, :] = keep_ref[rows, :]
        ref[BLOCK : 2 * BLOCK, :] = picked[rows]
        ref[2 * BLOCK :, :] = wave
    mate_ref[...] = picked[len(out_refs) * BLOCK :]


def stat_kernel(pair_count, samps, wave_ref, keep_ref, mate_self_ref, near_ref, *refs):
    far = pair_count // 2 - 1
    own_refs, mate_refs = refs[:far], refs[far : 2 * far]
    out_hbm, got_ref, out_ref, sems = refs[2 * far :]
    pair, samp = lax.axis_index("pair"), lax.axis_index("samp")
    other = samps - 1 - samp

    def place(offset, core, block):
        got_ref[shifted(pair, offset, pair_count, -1) * samps + core] = block

    even, odd = offsets(pair_count, 0), offsets(pair_count, 1)
    for arrived, core in ((own_refs, samp), (mate_refs, other)):
        for i, ref in enumerate(arrived):
            offset = jnp.where(core == 0, even[i], odd[i])
            place(offset, core, ref[:BLOCK, :])
            place(offset, samps - 1 - core, ref[BLOCK : 2 * BLOCK, :])
    place(even[far], samp, near_ref[:BLOCK, :])
    place(even[far], other, near_ref[BLOCK : 2 * BLOCK, :])
    itself = (far + 1) * BLOCK
    place(0, samp, keep_ref[itself : itself + BLOCK, :])
    place(0, other, mate_self_ref[...])

    sources = got_ref.shape[0]
    s_dev = TILE * LANES // PANEL
    samples = sources * s_dev

    def by_samples(tiles):
        groups = tiles.shape[1] // s_dev
        if groups * s_dev != 8 or groups != 2:
            return [tiles[:, g * s_dev : (g + 1) * s_dev, :].reshape(samples, LANES) for g in range(groups)]
        couples = tiles.reshape(sources // 2, 2, 8, LANES)
        one, two = couples[:, 0], couples[:, 1]
        upper = lax.broadcasted_iota(jnp.int32, one.shape, 1) < s_dev
        first = jnp.where(upper, one, pltpu.roll(two, s_dev, 1))
        second = jnp.where(upper, pltpu.roll(one, s_dev, 1), two)
        return [x.reshape(samples, LANES) for x in (first, second)]

    panel_a = got_ref[:, 0:TILE, :].astype(jnp.float32)
    panel_b = got_ref[:, TILE:BLOCK, :].astype(jnp.float32)
    tile_b = jnp.where(samp == 0, panel_b[:, : TILE // 2], panel_b[:, TILE // 2 :])

    count = jnp.float32(samples)
    geno_b = jnp.concatenate(by_samples(tile_b), axis=1)
    marg_b = jnp.sum(geno_b, axis=0, keepdims=True)
    centred = (geno_b - marg_b / count) * (samples**-0.5)
    b_hi = centred.astype(jnp.bfloat16)
    b_lo = (centred - b_hi.astype(jnp.float32)).astype(jnp.bfloat16)
    b_both = jnp.concatenate([b_hi, b_lo], axis=0)

    wave = wave_ref[...].astype(jnp.float32)
    for ref in (*own_refs, *mate_refs, near_ref):
        wave = wave + ref[2 * BLOCK :, :].astype(jnp.float32)
    tiles = 2 * samples // LANES
    yrows = [
        jnp.concatenate([wave[k * tiles + t : k * tiles + t + 1] for t in range(tiles)], axis=1)
        for k in range(out_ref.shape[0])
    ]
    yall = jnp.concatenate(yrows, axis=0)
    tail = jnp.dot(yall.astype(jnp.bfloat16), b_both, preferred_element_type=jnp.float32) / count
    c_hi = tail.astype(jnp.bfloat16).astype(jnp.float32)
    c_lo = tail - c_hi

    rows = []
    for geno_a in by_samples(panel_a[:, : TILE // 2]) + by_samples(panel_a[:, TILE // 2 :]):
        rows.append(jnp.concatenate([geno_a, geno_a], axis=0).astype(jnp.bfloat16).T)
    rows = jnp.concatenate(rows, axis=0)
    minus = -rows
    copies = []
    for k, yrow in enumerate(yrows):
        tails = [jnp.broadcast_to(c[k : k + 1], (TILE, c.shape[1])).astype(jnp.bfloat16) for c in (c_hi, c_lo)]
        right = jnp.concatenate([b_both] + [t for t in tails for _ in range(samples // TILE)], axis=0)
        left = jnp.concatenate([rows * yrow.astype(jnp.bfloat16), minus], axis=1)
        out_ref[k] = jnp.dot(left, right, preferred_element_type=jnp.float32).astype(out_ref.dtype)
        copies.append(pltpu.make_async_copy(out_ref.at[k], out_hbm.at[0, k], sems.at[k]))
        copies[-1].start()
    for copy in copies:
        copy.wait()


def on_device(dosage, phenotype, perms, pairs):
    s_dev, snps = dosage.shape
    genes = phenotype.shape[0]
    samples = perms.shape[1]
    pair_count, samps = (lax.axis_size(axis) for axis in AXES)
    rounds = pair_count // 2 + 1
    stats = genes * perms.shape[0]
    rows = wave_rows(stats, samples)
    grid = dosage.reshape(s_dev, snps // LANES, LANES).transpose(1, 0, 2).reshape(-1, LANES)
    vmem = pl.BlockSpec(memory_space=pltpu.VMEM)
    hbm = pl.BlockSpec(memory_space=pltpu.HBM)

    def array(*shape):
        return jax.ShapeDtypeStruct(shape, dosage.dtype)

    swap = [(i, samps - 1 - i) for i in range(samps)]
    mate_dosage = lax.ppermute(dosage, "samp", swap)
    mate_pheno = lax.ppermute(phenotype, "samp", swap)
    params = pltpu.CompilerParams(vmem_limit_bytes=24 * 1024 * 1024)
    blocks = rounds * BLOCK
    keep, pick, wave, perms_near = pl.pallas_call(
        functools.partial(pick_kernel, pair_count, samps),
        out_shape=[
            array(blocks, LANES),
            array(blocks, grid.shape[0]),
            array(rows, LANES),
            jax.ShapeDtypeStruct(perms.shape, perms.dtype),
        ],
        in_specs=[hbm] * 4,
        out_specs=[vmem] * 4,
        scratch_shapes=[
            pltpu.SMEM(pairs.shape[::-1], pairs.dtype),
            pltpu.VMEM(grid.shape, grid.dtype),
            pltpu.VMEM(phenotype.shape, phenotype.dtype),
            pltpu.SemaphoreType.DMA((4,)),
        ],
        compiler_params=params,
        cost_estimate=pl.CostEstimate(flops=0, bytes_accessed=4 * blocks * LANES * 2, transcendentals=0),
        name="pick",
    )(*[pltpu.with_memory_space_constraint(x, pltpu.HBM) for x in (pairs.T, grid, phenotype, perms)])

    mate_grid = mate_dosage.reshape(s_dev, snps // LANES, LANES).transpose(1, 0, 2).reshape(-1, LANES)
    mate_self, wave, *messages = pl.pallas_call(
        functools.partial(join_kernel, pair_count, samps),
        out_shape=[array(BLOCK, LANES), array(rows, LANES)] + [array(2 * BLOCK + rows, LANES)] * (rounds - 1),
        in_specs=[vmem] * 6,
        out_specs=[vmem] * (rounds + 1),
        compiler_params=params,
        name="join",
    )(keep, pick, wave, perms_near, mate_grid, mate_pheno)

    arrived = []
    for i, message in enumerate(messages):
        route = [
            (p * samps + c, shifted(p, offsets(pair_count, c)[i], pair_count) * samps + c)
            for p in range(pair_count)
            for c in range(samps)
        ]
        arrived.append(lax.ppermute(message, AXES, route))
    *far, near = arrived
    mates = [lax.ppermute(a, "samp", swap) for a in far]
    half = PANEL // samps
    return pl.pallas_call(
        functools.partial(stat_kernel, pair_count, samps),
        out_shape=jax.ShapeDtypeStruct((1, stats, PANEL, half), jnp.bfloat16),
        in_specs=[vmem] * (4 + 2 * len(far)),
        out_specs=hbm,
        scratch_shapes=[
            pltpu.VMEM((pair_count * samps, BLOCK, LANES), dosage.dtype),
            pltpu.VMEM((stats, PANEL, half), jnp.bfloat16),
            pltpu.SemaphoreType.DMA((stats,)),
        ],
        compiler_params=pltpu.CompilerParams(vmem_limit_bytes=48 * 1024 * 1024),
        name="stat",
    )(wave, keep, mate_self, near, *far, *mates)


def solution(mesh):
    placed = (P(("rep", "pair", "samp"), None), P(None, ("rep", "pair", "samp")), P(), P())
    return jax.shard_map(
        on_device,
        mesh=mesh,
        in_specs=placed,
        out_specs=P(("rep", "pair"), None, None, "samp"),
        check_vma=False,
    )
```

```python
import functools

import jax
import jax.numpy as jnp
from jax import lax
from jax.experimental import pallas as pl
from jax.experimental.pallas import tpu as pltpu
from jax.sharding import PartitionSpec as P

PANEL = 512
LANES = 128
TILE = 16
BLOCK = 2 * TILE
AXES = ("pair", "samp")


def offsets(pair_count, core):
    shared = pair_count - 2
    rest = [e for e in range(1, pair_count) if e != shared]
    mine = rest[: len(rest) // 2] if core == 0 else rest[len(rest) // 2 :]
    if core == 0:
        mine = mine[1:] + mine[:1]
    return mine + [shared, 0]


def shifted(pair, offset, pair_count, sign=1):
    turn = pair_count // 2
    high = (pair >> 1) + sign * (offset >> 1)
    high = high - turn * (high >= turn) + turn * (high < 0)
    return high * 2 + ((pair ^ offset) & 1)


def wave_rows(stats, samples):
    return -(-stats * 2 * samples // LANES // 8) * 8


def spread(pheno, perms, first, rows):
    genes, s_dev = pheno.shape
    samples = perms.shape[1]
    pheno = pheno.astype(jnp.float32)
    perms = perms - first
    perms = jnp.concatenate([perms, perms], axis=1)
    tiles = []
    for g in range(genes):
        drawn = jnp.zeros(perms.shape, jnp.float32)
        for s in range(s_dev):
            drawn = jnp.where(perms == s, pheno[g : g + 1, s : s + 1], drawn)
        tiles += [drawn[r : r + 1, t : t + LANES] for r in range(perms.shape[0]) for t in range(0, 2 * samples, LANES)]
    if rows > len(tiles):
        tiles.append(jnp.zeros((rows - len(tiles), LANES), jnp.float32))
    return jnp.concatenate(tiles, axis=0)


def pick_kernel(
    pair_count, samps, pairs_hbm, grid_hbm, pheno_hbm, perms_hbm, keep_ref, pick_ref, wave_ref, perms_ref, pairs_ref, grid_ref, pheno_ref, sems
):
    fetched = ((pairs_hbm, pairs_ref), (grid_hbm, grid_ref), (pheno_hbm, pheno_ref), (perms_hbm, perms_ref))
    copies = [pltpu.make_async_copy(source, target, sems.at[i]) for i, (source, target) in enumerate(fetched)]
    for copy in copies:
        copy.start()
    pair, samp = lax.axis_index("pair"), lax.axis_index("samp")
    shape = (TILE, pick_ref.shape[1])
    ahead = lax.broadcasted_iota(jnp.int32, shape, 1) - lax.broadcasted_iota(jnp.int32, shape, 0)
    for copy in copies:
        copy.wait()
    wave = spread(pheno_ref[...], perms_ref[...], (pair * samps + samp) * pheno_ref.shape[1], wave_ref.shape[0])
    wave_ref[...] = wave.astype(wave_ref.dtype)
    for i, (even, odd) in enumerate(zip(offsets(pair_count, 0), offsets(pair_count, 1))):
        n = shifted(pair, jnp.where(samp == 0, even, odd), pair_count)
        for j in range(2):
            start = pl.multiple_of(pairs_ref[j, n] * TILE, TILE)
            rows = slice(i * BLOCK + j * TILE, i * BLOCK + (j + 1) * TILE)
            keep_ref[rows, :] = grid_ref[pl.ds(start, TILE), :]
            pick_ref[rows, :] = jnp.where(ahead == start, 1.0, 0.0).astype(pick_ref.dtype)


def join_kernel(pair_count, samps, keep_ref, pick_ref, wave_ref, perms_ref, grid_ref, pheno_ref, mate_ref, both_ref, *out_refs):
    pair, samp = lax.axis_index("pair"), lax.axis_index("samp")
    first = (pair * samps + samps - 1 - samp) * pheno_ref.shape[1]
    wave = spread(pheno_ref[...], perms_ref[...], first, wave_ref.shape[0])
    wave = (wave_ref[...].astype(jnp.float32) + wave).astype(wave_ref.dtype)
    both_ref[...] = wave
    picked = jnp.dot(pick_ref[...], grid_ref[...], preferred_element_type=jnp.float32).astype(mate_ref.dtype)
    for i, ref in enumerate(out_refs):
        rows = slice(i * BLOCK, (i + 1) * BLOCK)
        ref[:BLOCK, :] = keep_ref[rows, :]
        ref[BLOCK : 2 * BLOCK, :] = picked[rows]
        ref[2 * BLOCK :, :] = wave
    mate_ref[...] = picked[len(out_refs) * BLOCK :]


def stat_kernel(pair_count, samps, wave_ref, keep_ref, mate_self_ref, near_ref, *refs):
    far = pair_count // 2 - 1
    own_refs, mate_refs = refs[:far], refs[far : 2 * far]
    out_hbm, got_ref, out_ref, sems = refs[2 * far :]
    pair, samp = lax.axis_index("pair"), lax.axis_index("samp")
    other = samps - 1 - samp

    def place(offset, core, block):
        got_ref[shifted(pair, offset, pair_count, -1) * samps + core] = block

    even, odd = offsets(pair_count, 0), offsets(pair_count, 1)
    for arrived, core in ((own_refs, samp), (mate_refs, other)):
        for i, ref in enumerate(arrived):
            offset = jnp.where(core == 0, even[i], odd[i])
            place(offset, core, ref[:BLOCK, :])
            place(offset, samps - 1 - core, ref[BLOCK : 2 * BLOCK, :])
    place(even[far], samp, near_ref[:BLOCK, :])
    place(even[far], other, near_ref[BLOCK : 2 * BLOCK, :])
    itself = (far + 1) * BLOCK
    place(0, samp, keep_ref[itself : itself + BLOCK, :])
    place(0, other, mate_self_ref[...])

    sources = got_ref.shape[0]
    s_dev = TILE * LANES // PANEL
    samples = sources * s_dev

    def by_samples(tiles):
        groups = tiles.shape[1] // s_dev
        if groups * s_dev != 8 or groups != 2:
            return [tiles[:, g * s_dev : (g + 1) * s_dev, :].reshape(samples, LANES) for g in range(groups)]
        couples = tiles.reshape(sources // 2, 2, 8, LANES)
        one, two = couples[:, 0], couples[:, 1]
        upper = lax.broadcasted_iota(jnp.int32, one.shape, 1) < s_dev
        first = jnp.where(upper, one, pltpu.roll(two, s_dev, 1))
        second = jnp.where(upper, pltpu.roll(one, s_dev, 1), two)
        return [x.reshape(samples, LANES) for x in (first, second)]

    panel_a = got_ref[:, 0:TILE, :].astype(jnp.float32)
    panel_b = got_ref[:, TILE:BLOCK, :].astype(jnp.float32)
    tile_b = jnp.where(samp == 0, panel_b[:, : TILE // 2], panel_b[:, TILE // 2 :])

    count = jnp.float32(samples)
    geno_b = jnp.concatenate(by_samples(tile_b), axis=1)
    marg_b = jnp.sum(geno_b, axis=0, keepdims=True)
    centred = (geno_b - marg_b / count) * (samples**-0.5)
    wave = wave_ref[...].astype(jnp.float32)
    for ref in (*own_refs, *mate_refs, near_ref):
        wave = wave + ref[2 * BLOCK :, :].astype(jnp.float32)
    tiles = 2 * samples // LANES
    stats = out_ref.shape[0]
    yrows = [
        jnp.concatenate([wave[k * tiles + t : k * tiles + t + 1] for t in range(tiles)], axis=1) for k in range(stats)
    ]
    yrows.append(jnp.zeros((8 * -(-stats // 8) - stats, 2 * samples), jnp.float32))
    ycolumns = jnp.concatenate(yrows, axis=0).T
    rights = []
    for k in range(stats):
        products = ycolumns[:samples, k : k + 1] * centred
        products = products - jnp.sum(products, axis=0, keepdims=True) / count
        high = products.astype(jnp.bfloat16)
        low = (products - high.astype(jnp.float32)).astype(jnp.bfloat16)
        rights.append(jnp.concatenate([high, low], axis=0))
    rows = []
    for geno_a in by_samples(panel_a[:, : TILE // 2]) + by_samples(panel_a[:, TILE // 2 :]):
        rows.append(jnp.concatenate([geno_a, geno_a], axis=0).astype(jnp.bfloat16).T)
    left = jnp.concatenate(rows, axis=0)
    half = out_ref.shape[2]
    copies = []
    for k in range(0, stats, 2):
        right = jnp.concatenate(rights[k : k + 2], axis=1)
        both = jnp.dot(left, right, preferred_element_type=jnp.float32).astype(out_ref.dtype)
        for j in range(len(rights[k : k + 2])):
            out_ref[k + j] = both[:, j * half : (j + 1) * half]
            copies.append(pltpu.make_async_copy(out_ref.at[k + j], out_hbm.at[0, k + j], sems.at[k + j]))
            copies[-1].start()
    for copy in copies:
        copy.wait()


def on_device(dosage, phenotype, perms, pairs):
    s_dev, snps = dosage.shape
    genes = phenotype.shape[0]
    samples = perms.shape[1]
    pair_count, samps = (lax.axis_size(axis) for axis in AXES)
    rounds = pair_count // 2 + 1
    stats = genes * perms.shape[0]
    rows = wave_rows(stats, samples)
    grid = dosage.reshape(s_dev, snps // LANES, LANES).transpose(1, 0, 2).reshape(-1, LANES)
    vmem = pl.BlockSpec(memory_space=pltpu.VMEM)
    hbm = pl.BlockSpec(memory_space=pltpu.HBM)

    def array(*shape):
        return jax.ShapeDtypeStruct(shape, dosage.dtype)

    swap = [(i, samps - 1 - i) for i in range(samps)]
    mate_dosage = lax.ppermute(dosage, "samp", swap)
    mate_pheno = lax.ppermute(phenotype, "samp", swap)
    params = pltpu.CompilerParams(vmem_limit_bytes=24 * 1024 * 1024)
    blocks = rounds * BLOCK
    keep, pick, wave, perms_near = pl.pallas_call(
        functools.partial(pick_kernel, pair_count, samps),
        out_shape=[
            array(blocks, LANES),
            array(blocks, grid.shape[0]),
            array(rows, LANES),
            jax.ShapeDtypeStruct(perms.shape, perms.dtype),
        ],
        in_specs=[hbm] * 4,
        out_specs=[vmem] * 4,
        scratch_shapes=[
            pltpu.SMEM(pairs.shape[::-1], pairs.dtype),
            pltpu.VMEM(grid.shape, grid.dtype),
            pltpu.VMEM(phenotype.shape, phenotype.dtype),
            pltpu.SemaphoreType.DMA((4,)),
        ],
        compiler_params=params,
        cost_estimate=pl.CostEstimate(flops=0, bytes_accessed=4 * blocks * LANES * 2, transcendentals=0),
        name="pick",
    )(*[pltpu.with_memory_space_constraint(x, pltpu.HBM) for x in (pairs.T, grid, phenotype, perms)])

    mate_grid = mate_dosage.reshape(s_dev, snps // LANES, LANES).transpose(1, 0, 2).reshape(-1, LANES)
    mate_self, wave, *messages = pl.pallas_call(
        functools.partial(join_kernel, pair_count, samps),
        out_shape=[array(BLOCK, LANES), array(rows, LANES)] + [array(2 * BLOCK + rows, LANES)] * (rounds - 1),
        in_specs=[vmem] * 6,
        out_specs=[vmem] * (rounds + 1),
        compiler_params=params,
        name="join",
    )(keep, pick, wave, perms_near, mate_grid, mate_pheno)

    arrived = []
    for i, message in enumerate(messages):
        route = [
            (p * samps + c, shifted(p, offsets(pair_count, c)[i], pair_count) * samps + c)
            for p in range(pair_count)
            for c in range(samps)
        ]
        arrived.append(lax.ppermute(message, AXES, route))
    *far, near = arrived
    mates = [lax.ppermute(a, "samp", swap) for a in far]
    half = PANEL // samps
    return pl.pallas_call(
        functools.partial(stat_kernel, pair_count, samps),
        out_shape=jax.ShapeDtypeStruct((1, stats, PANEL, half), jnp.bfloat16),
        in_specs=[vmem] * (4 + 2 * len(far)),
        out_specs=hbm,
        scratch_shapes=[
            pltpu.VMEM((pair_count * samps, BLOCK, LANES), dosage.dtype),
            pltpu.VMEM((stats, PANEL, half), jnp.bfloat16),
            pltpu.SemaphoreType.DMA((stats,)),
        ],
        compiler_params=pltpu.CompilerParams(vmem_limit_bytes=48 * 1024 * 1024),
        name="stat",
    )(wave, keep, mate_self, near, *far, *mates)


def solution(mesh):
    placed = (P(("rep", "pair", "samp"), None), P(None, ("rep", "pair", "samp")), P(), P())
    return jax.shard_map(
        on_device,
        mesh=mesh,
        in_specs=placed,
        out_specs=P(("rep", "pair"), None, None, "samp"),
        check_vma=False,
    )
```

```python
import functools

import jax
import jax.numpy as jnp
from jax import lax
from jax.experimental import pallas as pl
from jax.experimental.pallas import tpu as pltpu
from jax.sharding import PartitionSpec as P

PANEL = 512
LANES = 128
TILE = 16
BLOCK = 2 * TILE
AXES = ("pair", "samp")


def offsets(pair_count, core):
    shared = pair_count - 2
    rest = [e for e in range(1, pair_count) if e != shared]
    mine = rest[: len(rest) // 2] if core == 0 else rest[len(rest) // 2 :]
    if core == 0:
        mine = mine[1:] + mine[:1]
    return mine + [shared, 0]


def shifted(pair, offset, pair_count, sign=1):
    turn = pair_count // 2
    high = (pair >> 1) + sign * (offset >> 1)
    high = high - turn * (high >= turn) + turn * (high < 0)
    return high * 2 + ((pair ^ offset) & 1)


def wave_rows(stats, samples):
    return -(-stats * 2 * samples // LANES // 8) * 8


def spread(pheno, perms, first, rows):
    genes, s_dev = pheno.shape
    samples = perms.shape[1]
    pheno = pheno.astype(jnp.float32)
    perms = perms - first
    perms = jnp.concatenate([perms, perms], axis=1)
    tiles = []
    for g in range(genes):
        drawn = jnp.zeros(perms.shape, jnp.float32)
        for s in range(s_dev):
            drawn = jnp.where(perms == s, pheno[g : g + 1, s : s + 1], drawn)
        tiles += [drawn[r : r + 1, t : t + LANES] for r in range(perms.shape[0]) for t in range(0, 2 * samples, LANES)]
    if rows > len(tiles):
        tiles.append(jnp.zeros((rows - len(tiles), LANES), jnp.float32))
    return jnp.concatenate(tiles, axis=0)


def pick_kernel(
    pair_count, samps, pairs_hbm, grid_hbm, pheno_hbm, perms_hbm, keep_ref, pick_ref, wave_ref, perms_ref, pairs_ref, grid_ref, pheno_ref, sems
):
    fetched = ((pairs_hbm, pairs_ref), (grid_hbm, grid_ref), (pheno_hbm, pheno_ref), (perms_hbm, perms_ref))
    copies = [pltpu.make_async_copy(source, target, sems.at[i]) for i, (source, target) in enumerate(fetched)]
    for copy in copies:
        copy.start()
    pair, samp = lax.axis_index("pair"), lax.axis_index("samp")
    shape = (TILE, pick_ref.shape[1])
    ahead = lax.broadcasted_iota(jnp.int32, shape, 1) - lax.broadcasted_iota(jnp.int32, shape, 0)
    for copy in copies:
        copy.wait()
    wave = spread(pheno_ref[...], perms_ref[...], (pair * samps + samp) * pheno_ref.shape[1], wave_ref.shape[0])
    wave_ref[...] = wave.astype(wave_ref.dtype)
    for i, (even, odd) in enumerate(zip(offsets(pair_count, 0), offsets(pair_count, 1))):
        n = shifted(pair, jnp.where(samp == 0, even, odd), pair_count)
        for j in range(2):
            start = pl.multiple_of(pairs_ref[j, n] * TILE, TILE)
            rows = slice(i * BLOCK + j * TILE, i * BLOCK + (j + 1) * TILE)
            keep_ref[rows, :] = grid_ref[pl.ds(start, TILE), :]
            pick_ref[rows, :] = jnp.where(ahead == start, 1.0, 0.0).astype(pick_ref.dtype)


def join_kernel(pair_count, samps, keep_ref, pick_ref, wave_ref, perms_ref, grid_ref, pheno_ref, mate_ref, both_ref, *out_refs):
    pair, samp = lax.axis_index("pair"), lax.axis_index("samp")
    first = (pair * samps + samps - 1 - samp) * pheno_ref.shape[1]
    wave = spread(pheno_ref[...], perms_ref[...], first, wave_ref.shape[0])
    wave = (wave_ref[...].astype(jnp.float32) + wave).astype(wave_ref.dtype)
    both_ref[...] = wave
    picked = jnp.dot(pick_ref[...], grid_ref[...], preferred_element_type=jnp.float32).astype(mate_ref.dtype)
    for i, ref in enumerate(out_refs):
        rows = slice(i * BLOCK, (i + 1) * BLOCK)
        ref[:BLOCK, :] = keep_ref[rows, :]
        ref[BLOCK : 2 * BLOCK, :] = picked[rows]
        ref[2 * BLOCK :, :] = wave
    mate_ref[...] = picked[len(out_refs) * BLOCK :]


def stat_kernel(pair_count, samps, wave_ref, keep_ref, mate_self_ref, near_ref, *refs):
    far = pair_count // 2 - 1
    own_refs, mate_refs = refs[:far], refs[far : 2 * far]
    out_hbm, got_ref, out_ref, sems = refs[2 * far :]
    pair, samp = lax.axis_index("pair"), lax.axis_index("samp")
    other = samps - 1 - samp

    def place(offset, core, block):
        got_ref[shifted(pair, offset, pair_count, -1) * samps + core] = block

    even, odd = offsets(pair_count, 0), offsets(pair_count, 1)
    for arrived, core in ((own_refs, samp), (mate_refs, other)):
        for i, ref in enumerate(arrived):
            offset = jnp.where(core == 0, even[i], odd[i])
            place(offset, core, ref[:BLOCK, :])
            place(offset, samps - 1 - core, ref[BLOCK : 2 * BLOCK, :])
    place(even[far], samp, near_ref[:BLOCK, :])
    place(even[far], other, near_ref[BLOCK : 2 * BLOCK, :])
    itself = (far + 1) * BLOCK
    place(0, samp, keep_ref[itself : itself + BLOCK, :])
    place(0, other, mate_self_ref[...])

    sources = got_ref.shape[0]
    s_dev = TILE * LANES // PANEL
    samples = sources * s_dev

    def by_samples(tiles):
        groups = tiles.shape[1] // s_dev
        if groups * s_dev != 8 or groups != 2:
            return [tiles[:, g * s_dev : (g + 1) * s_dev, :].reshape(samples, LANES) for g in range(groups)]
        couples = tiles.reshape(sources // 2, 2, 8, LANES)
        one, two = couples[:, 0], couples[:, 1]
        upper = lax.broadcasted_iota(jnp.int32, one.shape, 1) < s_dev
        first = jnp.where(upper, one, pltpu.roll(two, s_dev, 1))
        second = jnp.where(upper, pltpu.roll(one, s_dev, 1), two)
        return [x.reshape(samples, LANES) for x in (first, second)]

    panel_a = got_ref[:, 0:TILE, :].astype(jnp.float32)
    panel_b = got_ref[:, TILE:BLOCK, :].astype(jnp.float32)
    tile_b = jnp.where(samp == 0, panel_b[:, : TILE // 2], panel_b[:, TILE // 2 :])

    count = jnp.float32(samples)
    geno_b = jnp.concatenate(by_samples(tile_b), axis=1)
    marg_b = jnp.sum(geno_b, axis=0, keepdims=True)
    centred = (geno_b - marg_b / count) * (samples**-0.5)
    wave = wave_ref[...].astype(jnp.float32)
    for ref in (*own_refs, *mate_refs, near_ref):
        wave = wave + ref[2 * BLOCK :, :].astype(jnp.float32)
    tiles = 2 * samples // LANES
    stats = out_ref.shape[0]
    yrows = [
        jnp.concatenate([wave[k * tiles + t : k * tiles + t + 1] for t in range(tiles)], axis=1) for k in range(stats)
    ]
    yrows.append(jnp.zeros((8 * -(-stats // 8) - stats, 2 * samples), jnp.float32))
    ycolumns = jnp.concatenate(yrows, axis=0).T
    rights = []
    for k in range(stats):
        products = ycolumns[:samples, k : k + 1] * centred
        products = products - jnp.sum(products, axis=0, keepdims=True) / count
        high = products.astype(jnp.bfloat16)
        low = (products - high.astype(jnp.float32)).astype(jnp.bfloat16)
        rights.append(jnp.concatenate([high, low], axis=0))
    right = jnp.concatenate(rights, axis=1)
    half = out_ref.shape[2]
    copies = []
    for q, geno_a in enumerate(by_samples(panel_a[:, : TILE // 2]) + by_samples(panel_a[:, TILE // 2 :])):
        left = jnp.concatenate([geno_a, geno_a], axis=0).astype(jnp.bfloat16).T
        piece = slice(q * LANES, (q + 1) * LANES)
        for k in range(stats):
            part = jnp.dot(left, right[:, k * half : (k + 1) * half], preferred_element_type=jnp.float32)
            out_ref[k, piece, :] = part.astype(out_ref.dtype)
        copies.append(pltpu.make_async_copy(out_ref.at[:, piece], out_hbm.at[0, :, piece], sems.at[q]))
        copies[-1].start()
    for copy in copies:
        copy.wait()


def on_device(dosage, phenotype, perms, pairs):
    s_dev, snps = dosage.shape
    genes = phenotype.shape[0]
    samples = perms.shape[1]
    pair_count, samps = (lax.axis_size(axis) for axis in AXES)
    rounds = pair_count // 2 + 1
    stats = genes * perms.shape[0]
    rows = wave_rows(stats, samples)
    grid = dosage.reshape(s_dev, snps // LANES, LANES).transpose(1, 0, 2).reshape(-1, LANES)
    vmem = pl.BlockSpec(memory_space=pltpu.VMEM)
    hbm = pl.BlockSpec(memory_space=pltpu.HBM)

    def array(*shape):
        return jax.ShapeDtypeStruct(shape, dosage.dtype)

    swap = [(i, samps - 1 - i) for i in range(samps)]
    mate_dosage = lax.ppermute(dosage, "samp", swap)
    mate_pheno = lax.ppermute(phenotype, "samp", swap)
    params = pltpu.CompilerParams(vmem_limit_bytes=24 * 1024 * 1024)
    blocks = rounds * BLOCK
    keep, pick, wave, perms_near = pl.pallas_call(
        functools.partial(pick_kernel, pair_count, samps),
        out_shape=[
            array(blocks, LANES),
            array(blocks, grid.shape[0]),
            array(rows, LANES),
            jax.ShapeDtypeStruct(perms.shape, perms.dtype),
        ],
        in_specs=[hbm] * 4,
        out_specs=[vmem] * 4,
        scratch_shapes=[
            pltpu.SMEM(pairs.shape[::-1], pairs.dtype),
            pltpu.VMEM(grid.shape, grid.dtype),
            pltpu.VMEM(phenotype.shape, phenotype.dtype),
            pltpu.SemaphoreType.DMA((4,)),
        ],
        compiler_params=params,
        cost_estimate=pl.CostEstimate(flops=0, bytes_accessed=4 * blocks * LANES * 2, transcendentals=0),
        name="pick",
    )(*[pltpu.with_memory_space_constraint(x, pltpu.HBM) for x in (pairs.T, grid, phenotype, perms)])

    mate_grid = mate_dosage.reshape(s_dev, snps // LANES, LANES).transpose(1, 0, 2).reshape(-1, LANES)
    mate_self, wave, *messages = pl.pallas_call(
        functools.partial(join_kernel, pair_count, samps),
        out_shape=[array(BLOCK, LANES), array(rows, LANES)] + [array(2 * BLOCK + rows, LANES)] * (rounds - 1),
        in_specs=[vmem] * 6,
        out_specs=[vmem] * (rounds + 1),
        compiler_params=params,
        name="join",
    )(keep, pick, wave, perms_near, mate_grid, mate_pheno)

    arrived = []
    for i, message in enumerate(messages):
        route = [
            (p * samps + c, shifted(p, offsets(pair_count, c)[i], pair_count) * samps + c)
            for p in range(pair_count)
            for c in range(samps)
        ]
        arrived.append(lax.ppermute(message, AXES, route))
    *far, near = arrived
    mates = [lax.ppermute(a, "samp", swap) for a in far]
    half = PANEL // samps
    return pl.pallas_call(
        functools.partial(stat_kernel, pair_count, samps),
        out_shape=jax.ShapeDtypeStruct((1, stats, PANEL, half), jnp.bfloat16),
        in_specs=[vmem] * (4 + 2 * len(far)),
        out_specs=hbm,
        scratch_shapes=[
            pltpu.VMEM((pair_count * samps, BLOCK, LANES), dosage.dtype),
            pltpu.VMEM((stats, PANEL, half), jnp.bfloat16),
            pltpu.SemaphoreType.DMA((PANEL // LANES,)),
        ],
        compiler_params=pltpu.CompilerParams(vmem_limit_bytes=48 * 1024 * 1024),
        name="stat",
    )(wave, keep, mate_self, near, *far, *mates)


def solution(mesh):
    placed = (P(("rep", "pair", "samp"), None), P(None, ("rep", "pair", "samp")), P(), P())
    return jax.shard_map(
        on_device,
        mesh=mesh,
        in_specs=placed,
        out_specs=P(("rep", "pair"), None, None, "samp"),
        check_vma=False,
    )
```

```python
import functools

import jax
import jax.numpy as jnp
from jax import lax
from jax.experimental import pallas as pl
from jax.experimental.pallas import tpu as pltpu
from jax.sharding import PartitionSpec as P

PANEL = 512
LANES = 128
TILE = 16
BLOCK = 2 * TILE
AXES = ("pair", "samp")


def offsets(pair_count, core):
    shared = pair_count - 2
    rest = [e for e in range(1, pair_count) if e != shared]
    mine = rest[: len(rest) // 2] if core == 0 else rest[len(rest) // 2 :]
    return mine[1:] + mine[:1] + [shared, 0]


def shifted(pair, offset, pair_count, sign=1):
    turn = pair_count // 2
    high = (pair >> 1) + sign * (offset >> 1)
    high = high - turn * (high >= turn) + turn * (high < 0)
    return high * 2 + ((pair ^ offset) & 1)


def wave_rows(stats, samples):
    return -(-stats * 2 * samples // LANES // 8) * 8


def spread(pheno, perms, first, rows):
    genes, s_dev = pheno.shape
    samples = perms.shape[1]
    pheno = pheno.astype(jnp.float32)
    perms = perms - first
    perms = jnp.concatenate([perms, perms], axis=1)
    tiles = []
    for g in range(genes):
        drawn = jnp.zeros(perms.shape, jnp.float32)
        for s in range(s_dev):
            drawn = jnp.where(perms == s, pheno[g : g + 1, s : s + 1], drawn)
        tiles += [drawn[r : r + 1, t : t + LANES] for r in range(perms.shape[0]) for t in range(0, 2 * samples, LANES)]
    if rows > len(tiles):
        tiles.append(jnp.zeros((rows - len(tiles), LANES), jnp.float32))
    return jnp.concatenate(tiles, axis=0)


def pick_kernel(
    pair_count, samps, pairs_hbm, grid_hbm, pheno_hbm, perms_hbm, keep_ref, pick_ref, wave_ref, perms_ref, pairs_ref, grid_ref, pheno_ref, sems
):
    fetched = ((pairs_hbm, pairs_ref), (grid_hbm, grid_ref), (pheno_hbm, pheno_ref), (perms_hbm, perms_ref))
    copies = [pltpu.make_async_copy(source, target, sems.at[i]) for i, (source, target) in enumerate(fetched)]
    for copy in copies:
        copy.start()
    pair, samp = lax.axis_index("pair"), lax.axis_index("samp")
    shape = (TILE, pick_ref.shape[1])
    ahead = lax.broadcasted_iota(jnp.int32, shape, 1) - lax.broadcasted_iota(jnp.int32, shape, 0)
    for copy in copies:
        copy.wait()
    wave = spread(pheno_ref[...], perms_ref[...], (pair * samps + samp) * pheno_ref.shape[1], wave_ref.shape[0])
    wave_ref[...] = wave.astype(wave_ref.dtype)
    for i, (even, odd) in enumerate(zip(offsets(pair_count, 0), offsets(pair_count, 1))):
        n = shifted(pair, jnp.where(samp == 0, even, odd), pair_count)
        for j in range(2):
            start = pl.multiple_of(pairs_ref[j, n] * TILE, TILE)
            rows = slice(i * BLOCK + j * TILE, i * BLOCK + (j + 1) * TILE)
            keep_ref[rows, :] = grid_ref[pl.ds(start, TILE), :]
            pick_ref[rows, :] = jnp.where(ahead == start, 1.0, 0.0).astype(pick_ref.dtype)


def join_kernel(pair_count, samps, keep_ref, pick_ref, wave_ref, perms_ref, grid_ref, pheno_ref, mate_ref, both_ref, *out_refs):
    pair, samp = lax.axis_index("pair"), lax.axis_index("samp")
    first = (pair * samps + samps - 1 - samp) * pheno_ref.shape[1]
    wave = spread(pheno_ref[...], perms_ref[...], first, wave_ref.shape[0])
    wave = (wave_ref[...].astype(jnp.float32) + wave).astype(wave_ref.dtype)
    both_ref[...] = wave
    picked = jnp.dot(pick_ref[...], grid_ref[...], preferred_element_type=jnp.float32).astype(mate_ref.dtype)
    for i, ref in enumerate(out_refs):
        rows = slice(i * BLOCK, (i + 1) * BLOCK)
        ref[:BLOCK, :] = keep_ref[rows, :]
        ref[BLOCK : 2 * BLOCK, :] = picked[rows]
        ref[2 * BLOCK :, :] = wave
    mate_ref[...] = picked[len(out_refs) * BLOCK :]


def stat_kernel(pair_count, samps, wave_ref, keep_ref, mate_self_ref, near_ref, *refs):
    far = pair_count // 2 - 1
    own_refs, mate_refs = refs[:far], refs[far : 2 * far]
    out_hbm, got_ref, out_ref, sems = refs[2 * far :]
    pair, samp = lax.axis_index("pair"), lax.axis_index("samp")
    other = samps - 1 - samp

    def place(offset, core, block):
        got_ref[shifted(pair, offset, pair_count, -1) * samps + core] = block

    even, odd = offsets(pair_count, 0), offsets(pair_count, 1)
    for arrived, core in ((own_refs, samp), (mate_refs, other)):
        for i, ref in enumerate(arrived):
            offset = jnp.where(core == 0, even[i], odd[i])
            place(offset, core, ref[:BLOCK, :])
            place(offset, samps - 1 - core, ref[BLOCK : 2 * BLOCK, :])
    place(even[far], samp, near_ref[:BLOCK, :])
    place(even[far], other, near_ref[BLOCK : 2 * BLOCK, :])
    itself = (far + 1) * BLOCK
    place(0, samp, keep_ref[itself : itself + BLOCK, :])
    place(0, other, mate_self_ref[...])

    sources = got_ref.shape[0]
    s_dev = TILE * LANES // PANEL
    samples = sources * s_dev

    def by_samples(tiles):
        groups = tiles.shape[1] // s_dev
        if groups * s_dev != 8 or groups != 2:
            return [tiles[:, g * s_dev : (g + 1) * s_dev, :].reshape(samples, LANES) for g in range(groups)]
        couples = tiles.reshape(sources // 2, 2, 8, LANES)
        one, two = couples[:, 0], couples[:, 1]
        upper = lax.broadcasted_iota(jnp.int32, one.shape, 1) < s_dev
        first = jnp.where(upper, one, pltpu.roll(two, s_dev, 1))
        second = jnp.where(upper, pltpu.roll(one, s_dev, 1), two)
        return [x.reshape(samples, LANES) for x in (first, second)]

    panel_a = got_ref[:, 0:TILE, :].astype(jnp.float32)
    panel_b = got_ref[:, TILE:BLOCK, :].astype(jnp.float32)
    tile_b = jnp.where(samp == 0, panel_b[:, : TILE // 2], panel_b[:, TILE // 2 :])

    count = jnp.float32(samples)
    geno_b = jnp.concatenate(by_samples(tile_b), axis=1)
    marg_b = jnp.sum(geno_b, axis=0, keepdims=True)
    centred = (geno_b - marg_b / count) * (samples**-0.5)
    wave = wave_ref[...].astype(jnp.float32)
    for ref in (*own_refs, *mate_refs, near_ref):
        wave = wave + ref[2 * BLOCK :, :].astype(jnp.float32)
    tiles = 2 * samples // LANES
    stats = out_ref.shape[0]
    yrows = [
        jnp.concatenate([wave[k * tiles + t : k * tiles + t + 1] for t in range(tiles)], axis=1) for k in range(stats)
    ]
    yrows.append(jnp.zeros((8 * -(-stats // 8) - stats, 2 * samples), jnp.float32))
    ycolumns = jnp.concatenate(yrows, axis=0).T
    rights = []
    for k in range(stats):
        products = ycolumns[:samples, k : k + 1] * centred
        products = products - jnp.sum(products, axis=0, keepdims=True) / count
        high = products.astype(jnp.bfloat16)
        low = (products - high.astype(jnp.float32)).astype(jnp.bfloat16)
        rights.append(jnp.concatenate([high, low], axis=0))
    right = jnp.concatenate(rights, axis=1)
    half = out_ref.shape[2]
    copies = []
    for q, geno_a in enumerate(by_samples(panel_a[:, : TILE // 2]) + by_samples(panel_a[:, TILE // 2 :])):
        left = jnp.concatenate([geno_a, geno_a], axis=0).astype(jnp.bfloat16).T
        piece = slice(q * LANES, (q + 1) * LANES)
        for k in range(stats):
            part = jnp.dot(left, right[:, k * half : (k + 1) * half], preferred_element_type=jnp.float32)
            out_ref[k, piece, :] = part.astype(out_ref.dtype)
        copies.append(pltpu.make_async_copy(out_ref.at[:, piece], out_hbm.at[0, :, piece], sems.at[q]))
        copies[-1].start()
    for copy in copies:
        copy.wait()


def on_device(dosage, phenotype, perms, pairs):
    s_dev, snps = dosage.shape
    genes = phenotype.shape[0]
    samples = perms.shape[1]
    pair_count, samps = (lax.axis_size(axis) for axis in AXES)
    rounds = pair_count // 2 + 1
    stats = genes * perms.shape[0]
    rows = wave_rows(stats, samples)
    grid = dosage.reshape(s_dev, snps // LANES, LANES).transpose(1, 0, 2).reshape(-1, LANES)
    vmem = pl.BlockSpec(memory_space=pltpu.VMEM)
    hbm = pl.BlockSpec(memory_space=pltpu.HBM)

    def array(*shape):
        return jax.ShapeDtypeStruct(shape, dosage.dtype)

    swap = [(i, samps - 1 - i) for i in range(samps)]
    mate_dosage = lax.ppermute(dosage, "samp", swap)
    mate_pheno = lax.ppermute(phenotype, "samp", swap)
    params = pltpu.CompilerParams(vmem_limit_bytes=24 * 1024 * 1024)
    blocks = rounds * BLOCK
    keep, pick, wave, perms_near = pl.pallas_call(
        functools.partial(pick_kernel, pair_count, samps),
        out_shape=[
            array(blocks, LANES),
            array(blocks, grid.shape[0]),
            array(rows, LANES),
            jax.ShapeDtypeStruct(perms.shape, perms.dtype),
        ],
        in_specs=[hbm] * 4,
        out_specs=[vmem] * 4,
        scratch_shapes=[
            pltpu.SMEM(pairs.shape[::-1], pairs.dtype),
            pltpu.VMEM(grid.shape, grid.dtype),
            pltpu.VMEM(phenotype.shape, phenotype.dtype),
            pltpu.SemaphoreType.DMA((4,)),
        ],
        compiler_params=params,
        cost_estimate=pl.CostEstimate(flops=0, bytes_accessed=4 * blocks * LANES * 2, transcendentals=0),
        name="pick",
    )(*[pltpu.with_memory_space_constraint(x, pltpu.HBM) for x in (pairs.T, grid, phenotype, perms)])

    mate_grid = mate_dosage.reshape(s_dev, snps // LANES, LANES).transpose(1, 0, 2).reshape(-1, LANES)
    mate_self, wave, *messages = pl.pallas_call(
        functools.partial(join_kernel, pair_count, samps),
        out_shape=[array(BLOCK, LANES), array(rows, LANES)] + [array(2 * BLOCK + rows, LANES)] * (rounds - 1),
        in_specs=[vmem] * 6,
        out_specs=[vmem] * (rounds + 1),
        compiler_params=params,
        name="join",
    )(keep, pick, wave, perms_near, mate_grid, mate_pheno)

    arrived = []
    for i, message in enumerate(messages):
        route = [
            (p * samps + c, shifted(p, offsets(pair_count, c)[i], pair_count) * samps + c)
            for p in range(pair_count)
            for c in range(samps)
        ]
        arrived.append(lax.ppermute(message, AXES, route))
    *far, near = arrived
    mates = [lax.ppermute(a, "samp", swap) for a in far]
    half = PANEL // samps
    return pl.pallas_call(
        functools.partial(stat_kernel, pair_count, samps),
        out_shape=jax.ShapeDtypeStruct((1, stats, PANEL, half), jnp.bfloat16),
        in_specs=[vmem] * (4 + 2 * len(far)),
        out_specs=hbm,
        scratch_shapes=[
            pltpu.VMEM((pair_count * samps, BLOCK, LANES), dosage.dtype),
            pltpu.VMEM((stats, PANEL, half), jnp.bfloat16),
            pltpu.SemaphoreType.DMA((PANEL // LANES,)),
        ],
        compiler_params=pltpu.CompilerParams(vmem_limit_bytes=48 * 1024 * 1024),
        name="stat",
    )(wave, keep, mate_self, near, *far, *mates)


def solution(mesh):
    placed = (P(("rep", "pair", "samp"), None), P(None, ("rep", "pair", "samp")), P(), P())
    return jax.shard_map(
        on_device,
        mesh=mesh,
        in_specs=placed,
        out_specs=P(("rep", "pair"), None, None, "samp"),
        check_vma=False,
    )
```

```python
import functools

import jax
import jax.numpy as jnp
from jax import lax
from jax.experimental import pallas as pl
from jax.experimental.pallas import tpu as pltpu
from jax.sharding import PartitionSpec as P

PANEL = 512
LANES = 128
TILE = 16
BLOCK = 2 * TILE
AXES = ("pair", "samp")


def offsets(pair_count, core):
    return [e for e in range(2, pair_count) if e % 2 == core] + [1, 0]


def shifted(pair, offset, pair_count, sign=1):
    turn = pair_count // 2
    high = (pair >> 1) + sign * (offset >> 1)
    high = high - turn * (high >= turn) + turn * (high < 0)
    return high * 2 + ((pair ^ offset) & 1)


def wave_rows(stats, samples):
    return -(-stats * 2 * samples // LANES // 8) * 8


def spread(pheno, perms, first, rows):
    genes, s_dev = pheno.shape
    samples = perms.shape[1]
    pheno = pheno.astype(jnp.float32)
    perms = perms - first
    perms = jnp.concatenate([perms, perms], axis=1)
    tiles = []
    for g in range(genes):
        drawn = jnp.zeros(perms.shape, jnp.float32)
        for s in range(s_dev):
            drawn = jnp.where(perms == s, pheno[g : g + 1, s : s + 1], drawn)
        tiles += [drawn[r : r + 1, t : t + LANES] for r in range(perms.shape[0]) for t in range(0, 2 * samples, LANES)]
    if rows > len(tiles):
        tiles.append(jnp.zeros((rows - len(tiles), LANES), jnp.float32))
    return jnp.concatenate(tiles, axis=0)


def pick_kernel(
    pair_count, samps, pairs_hbm, grid_hbm, pheno_hbm, perms_hbm, keep_ref, pick_ref, wave_ref, perms_ref, pairs_ref, grid_ref, pheno_ref, sems
):
    fetched = ((pairs_hbm, pairs_ref), (grid_hbm, grid_ref), (pheno_hbm, pheno_ref), (perms_hbm, perms_ref))
    copies = [pltpu.make_async_copy(source, target, sems.at[i]) for i, (source, target) in enumerate(fetched)]
    for copy in copies:
        copy.start()
    pair, samp = lax.axis_index("pair"), lax.axis_index("samp")
    shape = (TILE, pick_ref.shape[1])
    ahead = lax.broadcasted_iota(jnp.int32, shape, 1) - lax.broadcasted_iota(jnp.int32, shape, 0)
    for copy in copies:
        copy.wait()
    wave = spread(pheno_ref[...], perms_ref[...], (pair * samps + samp) * pheno_ref.shape[1], wave_ref.shape[0])
    wave_ref[...] = wave.astype(wave_ref.dtype)
    for i, (even, odd) in enumerate(zip(offsets(pair_count, 0), offsets(pair_count, 1))):
        n = shifted(pair, jnp.where(samp == 0, even, odd), pair_count)
        for j in range(2):
            start = pl.multiple_of(pairs_ref[j, n] * TILE, TILE)
            rows = slice(i * BLOCK + j * TILE, i * BLOCK + (j + 1) * TILE)
            keep_ref[rows, :] = grid_ref[pl.ds(start, TILE), :]
            pick_ref[rows, :] = jnp.where(ahead == start, 1.0, 0.0).astype(pick_ref.dtype)


def join_kernel(pair_count, samps, keep_ref, pick_ref, wave_ref, perms_ref, grid_ref, pheno_ref, mate_ref, both_ref, *out_refs):
    pair, samp = lax.axis_index("pair"), lax.axis_index("samp")
    first = (pair * samps + samps - 1 - samp) * pheno_ref.shape[1]
    wave = spread(pheno_ref[...], perms_ref[...], first, wave_ref.shape[0])
    wave = (wave_ref[...].astype(jnp.float32) + wave).astype(wave_ref.dtype)
    both_ref[...] = wave
    picked = jnp.dot(pick_ref[...], grid_ref[...], preferred_element_type=jnp.float32).astype(mate_ref.dtype)
    for i, ref in enumerate(out_refs):
        rows = slice(i * BLOCK, (i + 1) * BLOCK)
        ref[:BLOCK, :] = keep_ref[rows, :]
        ref[BLOCK : 2 * BLOCK, :] = picked[rows]
        ref[2 * BLOCK :, :] = wave
    mate_ref[...] = picked[len(out_refs) * BLOCK :]


def stat_kernel(pair_count, samps, wave_ref, keep_ref, mate_self_ref, near_ref, *refs):
    far = pair_count // 2 - 1
    own_refs, mate_refs = refs[:far], refs[far : 2 * far]
    out_hbm, got_ref, out_ref, sems = refs[2 * far :]
    pair, samp = lax.axis_index("pair"), lax.axis_index("samp")
    other = samps - 1 - samp

    def place(offset, core, block):
        got_ref[shifted(pair, offset, pair_count, -1) * samps + core] = block

    even, odd = offsets(pair_count, 0), offsets(pair_count, 1)
    for arrived, core in ((own_refs, samp), (mate_refs, other)):
        for i, ref in enumerate(arrived):
            offset = jnp.where(core == 0, even[i], odd[i])
            place(offset, core, ref[:BLOCK, :])
            place(offset, samps - 1 - core, ref[BLOCK : 2 * BLOCK, :])
    place(even[far], samp, near_ref[:BLOCK, :])
    place(even[far], other, near_ref[BLOCK : 2 * BLOCK, :])
    itself = (far + 1) * BLOCK
    place(0, samp, keep_ref[itself : itself + BLOCK, :])
    place(0, other, mate_self_ref[...])

    sources = got_ref.shape[0]
    s_dev = TILE * LANES // PANEL
    samples = sources * s_dev

    def by_samples(tiles):
        groups = tiles.shape[1] // s_dev
        if groups * s_dev != 8 or groups != 2:
            return [tiles[:, g * s_dev : (g + 1) * s_dev, :].reshape(samples, LANES) for g in range(groups)]
        couples = tiles.reshape(sources // 2, 2, 8, LANES)
        one, two = couples[:, 0], couples[:, 1]
        upper = lax.broadcasted_iota(jnp.int32, one.shape, 1) < s_dev
        first = jnp.where(upper, one, pltpu.roll(two, s_dev, 1))
        second = jnp.where(upper, pltpu.roll(one, s_dev, 1), two)
        return [x.reshape(samples, LANES) for x in (first, second)]

    panel_a = got_ref[:, 0:TILE, :].astype(jnp.float32)
    panel_b = got_ref[:, TILE:BLOCK, :].astype(jnp.float32)
    tile_b = jnp.where(samp == 0, panel_b[:, : TILE // 2], panel_b[:, TILE // 2 :])

    count = jnp.float32(samples)
    geno_b = jnp.concatenate(by_samples(tile_b), axis=1)
    marg_b = jnp.sum(geno_b, axis=0, keepdims=True)
    centred = (geno_b - marg_b / count) * (samples**-0.5)
    wave = wave_ref[...].astype(jnp.float32)
    for ref in (*own_refs, *mate_refs, near_ref):
        wave = wave + ref[2 * BLOCK :, :].astype(jnp.float32)
    tiles = 2 * samples // LANES
    stats = out_ref.shape[0]
    yrows = [
        jnp.concatenate([wave[k * tiles + t : k * tiles + t + 1] for t in range(tiles)], axis=1) for k in range(stats)
    ]
    yrows.append(jnp.zeros((8 * -(-stats // 8) - stats, 2 * samples), jnp.float32))
    ycolumns = jnp.concatenate(yrows, axis=0).T
    rights = []
    for k in range(stats):
        products = ycolumns[:samples, k : k + 1] * centred
        products = products - jnp.sum(products, axis=0, keepdims=True) / count
        high = products.astype(jnp.bfloat16)
        low = (products - high.astype(jnp.float32)).astype(jnp.bfloat16)
        rights.append(jnp.concatenate([high, low], axis=0))
    right = jnp.concatenate(rights, axis=1)
    half = out_ref.shape[2]
    copies = []
    for q, geno_a in enumerate(by_samples(panel_a[:, : TILE // 2]) + by_samples(panel_a[:, TILE // 2 :])):
        left = jnp.concatenate([geno_a, geno_a], axis=0).astype(jnp.bfloat16).T
        piece = slice(q * LANES, (q + 1) * LANES)
        for k in range(stats):
            part = jnp.dot(left, right[:, k * half : (k + 1) * half], preferred_element_type=jnp.float32)
            out_ref[k, piece, :] = part.astype(out_ref.dtype)
        copies.append(pltpu.make_async_copy(out_ref.at[:, piece], out_hbm.at[0, :, piece], sems.at[q]))
        copies[-1].start()
    for copy in copies:
        copy.wait()


def on_device(dosage, phenotype, perms, pairs):
    s_dev, snps = dosage.shape
    genes = phenotype.shape[0]
    samples = perms.shape[1]
    pair_count, samps = (lax.axis_size(axis) for axis in AXES)
    rounds = pair_count // 2 + 1
    stats = genes * perms.shape[0]
    rows = wave_rows(stats, samples)
    grid = dosage.reshape(s_dev, snps // LANES, LANES).transpose(1, 0, 2).reshape(-1, LANES)
    vmem = pl.BlockSpec(memory_space=pltpu.VMEM)
    hbm = pl.BlockSpec(memory_space=pltpu.HBM)

    def array(*shape):
        return jax.ShapeDtypeStruct(shape, dosage.dtype)

    swap = [(i, samps - 1 - i) for i in range(samps)]
    mate_dosage = lax.ppermute(dosage, "samp", swap)
    mate_pheno = lax.ppermute(phenotype, "samp", swap)
    params = pltpu.CompilerParams(vmem_limit_bytes=24 * 1024 * 1024)
    blocks = rounds * BLOCK
    keep, pick, wave, perms_near = pl.pallas_call(
        functools.partial(pick_kernel, pair_count, samps),
        out_shape=[
            array(blocks, LANES),
            array(blocks, grid.shape[0]),
            array(rows, LANES),
            jax.ShapeDtypeStruct(perms.shape, perms.dtype),
        ],
        in_specs=[hbm] * 4,
        out_specs=[vmem] * 4,
        scratch_shapes=[
            pltpu.SMEM(pairs.shape[::-1], pairs.dtype),
            pltpu.VMEM(grid.shape, grid.dtype),
            pltpu.VMEM(phenotype.shape, phenotype.dtype),
            pltpu.SemaphoreType.DMA((4,)),
        ],
        compiler_params=params,
        cost_estimate=pl.CostEstimate(flops=0, bytes_accessed=4 * blocks * LANES * 2, transcendentals=0),
        name="pick",
    )(*[pltpu.with_memory_space_constraint(x, pltpu.HBM) for x in (pairs.T, grid, phenotype, perms)])

    mate_grid = mate_dosage.reshape(s_dev, snps // LANES, LANES).transpose(1, 0, 2).reshape(-1, LANES)
    mate_self, wave, *messages = pl.pallas_call(
        functools.partial(join_kernel, pair_count, samps),
        out_shape=[array(BLOCK, LANES), array(rows, LANES)] + [array(2 * BLOCK + rows, LANES)] * (rounds - 1),
        in_specs=[vmem] * 6,
        out_specs=[vmem] * (rounds + 1),
        compiler_params=params,
        name="join",
    )(keep, pick, wave, perms_near, mate_grid, mate_pheno)

    arrived = []
    for i, message in enumerate(messages):
        route = [
            (p * samps + c, shifted(p, offsets(pair_count, c)[i], pair_count) * samps + c)
            for p in range(pair_count)
            for c in range(samps)
        ]
        arrived.append(lax.ppermute(message, AXES, route))
    *far, near = arrived
    mates = [lax.ppermute(a, "samp", swap) for a in far]
    half = PANEL // samps
    return pl.pallas_call(
        functools.partial(stat_kernel, pair_count, samps),
        out_shape=jax.ShapeDtypeStruct((1, stats, PANEL, half), jnp.bfloat16),
        in_specs=[vmem] * (4 + 2 * len(far)),
        out_specs=hbm,
        scratch_shapes=[
            pltpu.VMEM((pair_count * samps, BLOCK, LANES), dosage.dtype),
            pltpu.VMEM((stats, PANEL, half), jnp.bfloat16),
            pltpu.SemaphoreType.DMA((PANEL // LANES,)),
        ],
        compiler_params=pltpu.CompilerParams(vmem_limit_bytes=48 * 1024 * 1024),
        name="stat",
    )(wave, keep, mate_self, near, *far, *mates)


def solution(mesh):
    placed = (P(("rep", "pair", "samp"), None), P(None, ("rep", "pair", "samp")), P(), P())
    return jax.shard_map(
        on_device,
        mesh=mesh,
        in_specs=placed,
        out_specs=P(("rep", "pair"), None, None, "samp"),
        check_vma=False,
    )
```

```python
import functools

import jax
import jax.numpy as jnp
from jax import lax
from jax.experimental import pallas as pl
from jax.experimental.pallas import tpu as pltpu
from jax.sharding import PartitionSpec as P

PANEL = 512
LANES = 128
TILE = 16
BLOCK = 2 * TILE
AXES = ("pair", "samp")


def offsets(pair_count, core):
    return [e for e in range(2, pair_count) if e % 2 == core] + [1, 0]


def shifted(pair, offset, pair_count, sign=1):
    turn = pair_count // 2
    high = (pair >> 1) + sign * (offset >> 1)
    high = high - turn * (high >= turn) + turn * (high < 0)
    return high * 2 + ((pair ^ offset) & 1)


def wave_rows(stats, samples):
    return -(-stats * 2 * samples // LANES // 8) * 8


def spread(pheno, perms, first, rows):
    genes, s_dev = pheno.shape
    samples = perms.shape[1]
    pheno = pheno.astype(jnp.float32)
    perms = perms - first
    perms = jnp.concatenate([perms, perms], axis=1)
    tiles = []
    for g in range(genes):
        drawn = jnp.zeros(perms.shape, jnp.float32)
        for s in range(s_dev):
            drawn = jnp.where(perms == s, pheno[g : g + 1, s : s + 1], drawn)
        tiles += [drawn[r : r + 1, t : t + LANES] for r in range(perms.shape[0]) for t in range(0, 2 * samples, LANES)]
    if rows > len(tiles):
        tiles.append(jnp.zeros((rows - len(tiles), LANES), jnp.float32))
    return jnp.concatenate(tiles, axis=0)


def pick_kernel(
    pair_count, samps, pairs_hbm, grid_hbm, pheno_hbm, perms_hbm, keep_ref, pick_ref, wave_ref, perms_ref, pairs_ref, grid_ref, pheno_ref, sems
):
    fetched = ((pairs_hbm, pairs_ref), (grid_hbm, grid_ref), (pheno_hbm, pheno_ref), (perms_hbm, perms_ref))
    copies = [pltpu.make_async_copy(source, target, sems.at[i]) for i, (source, target) in enumerate(fetched)]
    for copy in copies:
        copy.start()
    pair, samp = lax.axis_index("pair"), lax.axis_index("samp")
    shape = (TILE, pick_ref.shape[1])
    ahead = lax.broadcasted_iota(jnp.int32, shape, 1) - lax.broadcasted_iota(jnp.int32, shape, 0)
    for copy in copies:
        copy.wait()
    wave = spread(pheno_ref[...], perms_ref[...], (pair * samps + samp) * pheno_ref.shape[1], wave_ref.shape[0])
    wave_ref[...] = wave.astype(wave_ref.dtype)
    for i, (even, odd) in enumerate(zip(offsets(pair_count, 0), offsets(pair_count, 1))):
        n = shifted(pair, jnp.where(samp == 0, even, odd), pair_count)
        for j in range(2):
            start = pl.multiple_of(pairs_ref[j, n] * TILE, TILE)
            rows = slice(i * BLOCK + j * TILE, i * BLOCK + (j + 1) * TILE)
            keep_ref[rows, :] = grid_ref[pl.ds(start, TILE), :]
            pick_ref[rows, :] = jnp.where(ahead == start, 1.0, 0.0).astype(pick_ref.dtype)


def join_kernel(pair_count, samps, keep_ref, pick_ref, wave_ref, perms_ref, grid_ref, pheno_ref, mate_ref, both_ref, *out_refs):
    pair, samp = lax.axis_index("pair"), lax.axis_index("samp")
    first = (pair * samps + samps - 1 - samp) * pheno_ref.shape[1]
    wave = spread(pheno_ref[...], perms_ref[...], first, wave_ref.shape[0])
    wave = (wave_ref[...].astype(jnp.float32) + wave).astype(wave_ref.dtype)
    both_ref[...] = wave
    picked = jnp.dot(pick_ref[...], grid_ref[...], preferred_element_type=jnp.float32).astype(mate_ref.dtype)
    for i, ref in enumerate(out_refs):
        rows = slice(i * BLOCK, (i + 1) * BLOCK)
        ref[:BLOCK, :] = keep_ref[rows, :]
        ref[BLOCK : 2 * BLOCK, :] = picked[rows]
        ref[2 * BLOCK :, :] = wave
    mate_ref[...] = picked[len(out_refs) * BLOCK :]


def stat_kernel(pair_count, samps, wave_ref, keep_ref, mate_self_ref, near_ref, *refs):
    far = pair_count // 2 - 1
    own_refs, mate_refs = refs[:far], refs[far : 2 * far]
    out_hbm, got_ref, out_ref, sems = refs[2 * far :]
    pair, samp = lax.axis_index("pair"), lax.axis_index("samp")
    other = samps - 1 - samp

    def place(offset, core, block):
        got_ref[shifted(pair, offset, pair_count, -1) * samps + core] = block

    even, odd = offsets(pair_count, 0), offsets(pair_count, 1)
    for arrived, core in ((own_refs, samp), (mate_refs, other)):
        for i, ref in enumerate(arrived):
            offset = jnp.where(core == 0, even[i], odd[i])
            place(offset, core, ref[:BLOCK, :])
            place(offset, samps - 1 - core, ref[BLOCK : 2 * BLOCK, :])
    place(even[far], samp, near_ref[:BLOCK, :])
    place(even[far], other, near_ref[BLOCK : 2 * BLOCK, :])
    itself = (far + 1) * BLOCK
    place(0, samp, keep_ref[itself : itself + BLOCK, :])
    place(0, other, mate_self_ref[...])

    sources = got_ref.shape[0]
    s_dev = TILE * LANES // PANEL
    samples = sources * s_dev

    def by_samples(tiles):
        groups = tiles.shape[1] // s_dev
        if groups * s_dev != 8 or groups != 2:
            return [tiles[:, g * s_dev : (g + 1) * s_dev, :].reshape(samples, LANES) for g in range(groups)]
        couples = tiles.reshape(sources // 2, 2, 8, LANES)
        one, two = couples[:, 0], couples[:, 1]
        upper = lax.broadcasted_iota(jnp.int32, one.shape, 1) < s_dev
        first = jnp.where(upper, one, pltpu.roll(two, s_dev, 1))
        second = jnp.where(upper, pltpu.roll(one, s_dev, 1), two)
        return [x.reshape(samples, LANES) for x in (first, second)]

    panel_a = got_ref[:, 0:TILE, :].astype(jnp.float32)
    panel_b = got_ref[:, TILE:BLOCK, :].astype(jnp.float32)
    tile_b = jnp.where(samp == 0, panel_b[:, : TILE // 2], panel_b[:, TILE // 2 :])

    count = jnp.float32(samples)
    geno_b = jnp.concatenate(by_samples(tile_b), axis=1)
    marg_b = jnp.sum(geno_b, axis=0, keepdims=True)
    centred = (geno_b - marg_b / count) * (samples**-0.5)
    wave = wave_ref[...].astype(jnp.float32)
    for ref in (*own_refs, *mate_refs, near_ref):
        wave = wave + ref[2 * BLOCK :, :].astype(jnp.float32)
    tiles = 2 * samples // LANES
    stats = out_ref.shape[0]
    yrows = [
        jnp.concatenate([wave[k * tiles + t : k * tiles + t + 1] for t in range(tiles)], axis=1) for k in range(stats)
    ]
    yrows.append(jnp.zeros((8 * -(-stats // 8) - stats, 2 * samples), jnp.float32))
    ycolumns = jnp.concatenate(yrows, axis=0).T
    rights = []
    for k in range(stats):
        products = ycolumns[:samples, k : k + 1] * centred
        products = products - jnp.sum(products, axis=0, keepdims=True) / count
        high = products.astype(jnp.bfloat16)
        low = (products - high.astype(jnp.float32)).astype(jnp.bfloat16)
        rights.append(jnp.concatenate([high, low], axis=0))
    right = jnp.concatenate(rights, axis=1)
    half = out_ref.shape[2]
    copies = []
    for q, geno_a in enumerate(by_samples(panel_a[:, : TILE // 2]) + by_samples(panel_a[:, TILE // 2 :])):
        left = jnp.concatenate([geno_a, geno_a], axis=0).astype(jnp.bfloat16).T
        piece = slice(q * LANES, (q + 1) * LANES)
        for k in range(stats):
            part = jnp.dot(left, right[:, k * half : (k + 1) * half], preferred_element_type=jnp.float32)
            out_ref[k, piece, :] = part.astype(out_ref.dtype)
            copies.append(pltpu.make_async_copy(out_ref.at[k, piece], out_hbm.at[0, k, piece], sems.at[q, k]))
            copies[-1].start()
    for copy in copies:
        copy.wait()


def on_device(dosage, phenotype, perms, pairs):
    s_dev, snps = dosage.shape
    genes = phenotype.shape[0]
    samples = perms.shape[1]
    pair_count, samps = (lax.axis_size(axis) for axis in AXES)
    rounds = pair_count // 2 + 1
    stats = genes * perms.shape[0]
    rows = wave_rows(stats, samples)
    grid = dosage.reshape(s_dev, snps // LANES, LANES).transpose(1, 0, 2).reshape(-1, LANES)
    vmem = pl.BlockSpec(memory_space=pltpu.VMEM)
    hbm = pl.BlockSpec(memory_space=pltpu.HBM)

    def array(*shape):
        return jax.ShapeDtypeStruct(shape, dosage.dtype)

    swap = [(i, samps - 1 - i) for i in range(samps)]
    mate_dosage = lax.ppermute(dosage, "samp", swap)
    mate_pheno = lax.ppermute(phenotype, "samp", swap)
    params = pltpu.CompilerParams(vmem_limit_bytes=24 * 1024 * 1024)
    blocks = rounds * BLOCK
    keep, pick, wave, perms_near = pl.pallas_call(
        functools.partial(pick_kernel, pair_count, samps),
        out_shape=[
            array(blocks, LANES),
            array(blocks, grid.shape[0]),
            array(rows, LANES),
            jax.ShapeDtypeStruct(perms.shape, perms.dtype),
        ],
        in_specs=[hbm] * 4,
        out_specs=[vmem] * 4,
        scratch_shapes=[
            pltpu.SMEM(pairs.shape[::-1], pairs.dtype),
            pltpu.VMEM(grid.shape, grid.dtype),
            pltpu.VMEM(phenotype.shape, phenotype.dtype),
            pltpu.SemaphoreType.DMA((4,)),
        ],
        compiler_params=params,
        cost_estimate=pl.CostEstimate(flops=0, bytes_accessed=4 * blocks * LANES * 2, transcendentals=0),
        name="pick",
    )(*[pltpu.with_memory_space_constraint(x, pltpu.HBM) for x in (pairs.T, grid, phenotype, perms)])

    mate_grid = mate_dosage.reshape(s_dev, snps // LANES, LANES).transpose(1, 0, 2).reshape(-1, LANES)
    mate_self, wave, *messages = pl.pallas_call(
        functools.partial(join_kernel, pair_count, samps),
        out_shape=[array(BLOCK, LANES), array(rows, LANES)] + [array(2 * BLOCK + rows, LANES)] * (rounds - 1),
        in_specs=[vmem] * 6,
        out_specs=[vmem] * (rounds + 1),
        compiler_params=params,
        name="join",
    )(keep, pick, wave, perms_near, mate_grid, mate_pheno)

    arrived = []
    for i, message in enumerate(messages):
        route = [
            (p * samps + c, shifted(p, offsets(pair_count, c)[i], pair_count) * samps + c)
            for p in range(pair_count)
            for c in range(samps)
        ]
        arrived.append(lax.ppermute(message, AXES, route))
    *far, near = arrived
    mates = [lax.ppermute(a, "samp", swap) for a in far]
    half = PANEL // samps
    return pl.pallas_call(
        functools.partial(stat_kernel, pair_count, samps),
        out_shape=jax.ShapeDtypeStruct((1, stats, PANEL, half), jnp.bfloat16),
        in_specs=[vmem] * (4 + 2 * len(far)),
        out_specs=hbm,
        scratch_shapes=[
            pltpu.VMEM((pair_count * samps, BLOCK, LANES), dosage.dtype),
            pltpu.VMEM((stats, PANEL, half), jnp.bfloat16),
            pltpu.SemaphoreType.DMA((PANEL // LANES, stats)),
        ],
        compiler_params=pltpu.CompilerParams(vmem_limit_bytes=48 * 1024 * 1024),
        name="stat",
    )(wave, keep, mate_self, near, *far, *mates)


def solution(mesh):
    placed = (P(("rep", "pair", "samp"), None), P(None, ("rep", "pair", "samp")), P(), P())
    return jax.shard_map(
        on_device,
        mesh=mesh,
        in_specs=placed,
        out_specs=P(("rep", "pair"), None, None, "samp"),
        check_vma=False,
    )
```

```python
import functools

import jax
import jax.numpy as jnp
from jax import lax
from jax.experimental import pallas as pl
from jax.experimental.pallas import tpu as pltpu
from jax.sharding import PartitionSpec as P

PANEL = 512
LANES = 128
TILE = 16
BLOCK = 2 * TILE
AXES = ("pair", "samp")


def offsets(pair_count, core):
    return [e for e in range(2, pair_count) if e % 2 == core] + [1, 0]


def shifted(pair, offset, pair_count, sign=1):
    turn = pair_count // 2
    high = (pair >> 1) + sign * (offset >> 1)
    high = high - turn * (high >= turn) + turn * (high < 0)
    return high * 2 + ((pair ^ offset) & 1)


def wave_rows(stats, samples):
    return -(-stats * 2 * samples // LANES // 8) * 8


def spread(pheno, perms, first, rows):
    genes, s_dev = pheno.shape
    samples = perms.shape[1]
    pheno = pheno.astype(jnp.float32)
    perms = perms - first
    perms = jnp.concatenate([perms, perms], axis=1)
    tiles = []
    for g in range(genes):
        drawn = jnp.zeros(perms.shape, jnp.float32)
        for s in range(s_dev):
            drawn = jnp.where(perms == s, pheno[g : g + 1, s : s + 1], drawn)
        tiles += [drawn[r : r + 1, t : t + LANES] for r in range(perms.shape[0]) for t in range(0, 2 * samples, LANES)]
    if rows > len(tiles):
        tiles.append(jnp.zeros((rows - len(tiles), LANES), jnp.float32))
    return jnp.concatenate(tiles, axis=0)


def pick_kernel(
    pair_count, samps, pairs_hbm, grid_hbm, pheno_hbm, perms_hbm, keep_ref, pick_ref, wave_ref, perms_ref, pairs_ref, grid_ref, pheno_ref, sems
):
    fetched = ((pairs_hbm, pairs_ref), (grid_hbm, grid_ref), (pheno_hbm, pheno_ref), (perms_hbm, perms_ref))
    copies = [pltpu.make_async_copy(source, target, sems.at[i]) for i, (source, target) in enumerate(fetched)]
    for copy in copies:
        copy.start()
    pair, samp = lax.axis_index("pair"), lax.axis_index("samp")
    shape = (TILE, pick_ref.shape[1])
    ahead = lax.broadcasted_iota(jnp.int32, shape, 1) - lax.broadcasted_iota(jnp.int32, shape, 0)
    for copy in copies:
        copy.wait()
    wave = spread(pheno_ref[...], perms_ref[...], (pair * samps + samp) * pheno_ref.shape[1], wave_ref.shape[0])
    wave_ref[...] = wave.astype(wave_ref.dtype)
    for i, (even, odd) in enumerate(zip(offsets(pair_count, 0), offsets(pair_count, 1))):
        n = shifted(pair, jnp.where(samp == 0, even, odd), pair_count)
        for j in range(2):
            start = pl.multiple_of(pairs_ref[j, n] * TILE, TILE)
            rows = slice(i * BLOCK + j * TILE, i * BLOCK + (j + 1) * TILE)
            keep_ref[rows, :] = grid_ref[pl.ds(start, TILE), :]
            pick_ref[rows, :] = jnp.where(ahead == start, 1.0, 0.0).astype(pick_ref.dtype)


def join_kernel(pair_count, samps, keep_ref, pick_ref, wave_ref, perms_ref, grid_ref, pheno_ref, mate_ref, both_ref, *out_refs):
    pair, samp = lax.axis_index("pair"), lax.axis_index("samp")
    first = (pair * samps + samps - 1 - samp) * pheno_ref.shape[1]
    wave = spread(pheno_ref[...], perms_ref[...], first, wave_ref.shape[0])
    wave = (wave_ref[...].astype(jnp.float32) + wave).astype(wave_ref.dtype)
    both_ref[...] = wave
    picked = jnp.dot(pick_ref[...], grid_ref[...], preferred_element_type=jnp.float32).astype(mate_ref.dtype)
    for i, ref in enumerate(out_refs):
        rows = slice(i * BLOCK, (i + 1) * BLOCK)
        ref[:BLOCK, :] = keep_ref[rows, :]
        ref[BLOCK : 2 * BLOCK, :] = picked[rows]
        ref[2 * BLOCK :, :] = wave
    mate_ref[...] = picked[len(out_refs) * BLOCK :]


def stat_kernel(pair_count, samps, wave_ref, keep_ref, mate_self_ref, near_ref, *refs):
    far = pair_count // 2 - 1
    own_refs, mate_refs = refs[:far], refs[far : 2 * far]
    out_hbm, got_ref, out_ref, sems = refs[2 * far :]
    pair, samp = lax.axis_index("pair"), lax.axis_index("samp")
    other = samps - 1 - samp

    def place(offset, core, block):
        got_ref[shifted(pair, offset, pair_count, -1) * samps + core] = block

    even, odd = offsets(pair_count, 0), offsets(pair_count, 1)
    for arrived, core in ((own_refs, samp), (mate_refs, other)):
        for i, ref in enumerate(arrived):
            offset = jnp.where(core == 0, even[i], odd[i])
            place(offset, core, ref[:BLOCK, :])
            place(offset, samps - 1 - core, ref[BLOCK : 2 * BLOCK, :])
    place(even[far], samp, near_ref[:BLOCK, :])
    place(even[far], other, near_ref[BLOCK : 2 * BLOCK, :])
    itself = (far + 1) * BLOCK
    place(0, samp, keep_ref[itself : itself + BLOCK, :])
    place(0, other, mate_self_ref[...])

    sources = got_ref.shape[0]
    s_dev = TILE * LANES // PANEL
    samples = sources * s_dev

    def by_samples(tiles):
        groups = tiles.shape[1] // s_dev
        if groups * s_dev != 8 or groups != 2:
            return [tiles[:, g * s_dev : (g + 1) * s_dev, :].reshape(samples, LANES) for g in range(groups)]
        couples = tiles.reshape(sources // 2, 2, 8, LANES)
        one, two = couples[:, 0], couples[:, 1]
        upper = lax.broadcasted_iota(jnp.int32, one.shape, 1) < s_dev
        first = jnp.where(upper, one, pltpu.roll(two, s_dev, 1))
        second = jnp.where(upper, pltpu.roll(one, s_dev, 1), two)
        return [x.reshape(samples, LANES) for x in (first, second)]

    panel_a = got_ref[:, 0:TILE, :].astype(jnp.float32)
    panel_b = got_ref[:, TILE:BLOCK, :].astype(jnp.float32)
    tile_b = jnp.where(samp == 0, panel_b[:, : TILE // 2], panel_b[:, TILE // 2 :])

    count = jnp.float32(samples)
    geno_b = jnp.concatenate(by_samples(tile_b), axis=1)
    marg_b = jnp.sum(geno_b, axis=0, keepdims=True)
    centred = (geno_b - marg_b / count) * (samples**-0.5)
    wave = wave_ref[...].astype(jnp.float32)
    for ref in (*own_refs, *mate_refs, near_ref):
        wave = wave + ref[2 * BLOCK :, :].astype(jnp.float32)
    tiles = 2 * samples // LANES
    stats = out_ref.shape[0]
    yrows = [
        jnp.concatenate([wave[k * tiles + t : k * tiles + t + 1] for t in range(tiles)], axis=1) for k in range(stats)
    ]
    yrows.append(jnp.zeros((8 * -(-stats // 8) - stats, 2 * samples), jnp.float32))
    ycolumns = jnp.concatenate(yrows, axis=0).T
    rights = []
    for k in range(stats):
        products = ycolumns[:samples, k : k + 1] * centred
        products = products - jnp.sum(products, axis=0, keepdims=True) / count
        high = products.astype(jnp.bfloat16)
        low = (products - high.astype(jnp.float32)).astype(jnp.bfloat16)
        rights.append(jnp.concatenate([high, low], axis=0))
    right = jnp.concatenate(rights, axis=1)
    half = out_ref.shape[2]
    copies = []
    for q, geno_a in enumerate(by_samples(panel_a[:, : TILE // 2]) + by_samples(panel_a[:, TILE // 2 :])):
        left = jnp.concatenate([geno_a, geno_a], axis=0).astype(jnp.bfloat16).T
        piece = slice(q * LANES, (q + 1) * LANES)
        for k in range(stats):
            part = jnp.dot(left, right[:, k * half : (k + 1) * half], preferred_element_type=jnp.float32)
            out_ref[k, piece, :] = part.astype(out_ref.dtype)
        if q % 2 == 1:
            done = slice((q - 1) * LANES, (q + 1) * LANES)
            copies.append(pltpu.make_async_copy(out_ref.at[:, done], out_hbm.at[0, :, done], sems.at[q // 2]))
            copies[-1].start()
    for copy in copies:
        copy.wait()


def on_device(dosage, phenotype, perms, pairs):
    s_dev, snps = dosage.shape
    genes = phenotype.shape[0]
    samples = perms.shape[1]
    pair_count, samps = (lax.axis_size(axis) for axis in AXES)
    rounds = pair_count // 2 + 1
    stats = genes * perms.shape[0]
    rows = wave_rows(stats, samples)
    grid = dosage.reshape(s_dev, snps // LANES, LANES).transpose(1, 0, 2).reshape(-1, LANES)
    vmem = pl.BlockSpec(memory_space=pltpu.VMEM)
    hbm = pl.BlockSpec(memory_space=pltpu.HBM)

    def array(*shape):
        return jax.ShapeDtypeStruct(shape, dosage.dtype)

    swap = [(i, samps - 1 - i) for i in range(samps)]
    mate_dosage = lax.ppermute(dosage, "samp", swap)
    mate_pheno = lax.ppermute(phenotype, "samp", swap)
    params = pltpu.CompilerParams(vmem_limit_bytes=24 * 1024 * 1024)
    blocks = rounds * BLOCK
    keep, pick, wave, perms_near = pl.pallas_call(
        functools.partial(pick_kernel, pair_count, samps),
        out_shape=[
            array(blocks, LANES),
            array(blocks, grid.shape[0]),
            array(rows, LANES),
            jax.ShapeDtypeStruct(perms.shape, perms.dtype),
        ],
        in_specs=[hbm] * 4,
        out_specs=[vmem] * 4,
        scratch_shapes=[
            pltpu.SMEM(pairs.shape[::-1], pairs.dtype),
            pltpu.VMEM(grid.shape, grid.dtype),
            pltpu.VMEM(phenotype.shape, phenotype.dtype),
            pltpu.SemaphoreType.DMA((4,)),
        ],
        compiler_params=params,
        cost_estimate=pl.CostEstimate(flops=0, bytes_accessed=4 * blocks * LANES * 2, transcendentals=0),
        name="pick",
    )(*[pltpu.with_memory_space_constraint(x, pltpu.HBM) for x in (pairs.T, grid, phenotype, perms)])

    mate_grid = mate_dosage.reshape(s_dev, snps // LANES, LANES).transpose(1, 0, 2).reshape(-1, LANES)
    mate_self, wave, *messages = pl.pallas_call(
        functools.partial(join_kernel, pair_count, samps),
        out_shape=[array(BLOCK, LANES), array(rows, LANES)] + [array(2 * BLOCK + rows, LANES)] * (rounds - 1),
        in_specs=[vmem] * 6,
        out_specs=[vmem] * (rounds + 1),
        compiler_params=params,
        name="join",
    )(keep, pick, wave, perms_near, mate_grid, mate_pheno)

    arrived = []
    for i, message in enumerate(messages):
        route = [
            (p * samps + c, shifted(p, offsets(pair_count, c)[i], pair_count) * samps + c)
            for p in range(pair_count)
            for c in range(samps)
        ]
        arrived.append(lax.ppermute(message, AXES, route))
    *far, near = arrived
    mates = [lax.ppermute(a, "samp", swap) for a in far]
    half = PANEL // samps
    return pl.pallas_call(
        functools.partial(stat_kernel, pair_count, samps),
        out_shape=jax.ShapeDtypeStruct((1, stats, PANEL, half), jnp.bfloat16),
        in_specs=[vmem] * (4 + 2 * len(far)),
        out_specs=hbm,
        scratch_shapes=[
            pltpu.VMEM((pair_count * samps, BLOCK, LANES), dosage.dtype),
            pltpu.VMEM((stats, PANEL, half), jnp.bfloat16),
            pltpu.SemaphoreType.DMA((PANEL // LANES // 2,)),
        ],
        compiler_params=pltpu.CompilerParams(vmem_limit_bytes=48 * 1024 * 1024),
        name="stat",
    )(wave, keep, mate_self, near, *far, *mates)


def solution(mesh):
    placed = (P(("rep", "pair", "samp"), None), P(None, ("rep", "pair", "samp")), P(), P())
    return jax.shard_map(
        on_device,
        mesh=mesh,
        in_specs=placed,
        out_specs=P(("rep", "pair"), None, None, "samp"),
        check_vma=False,
    )
```

```python
import functools

import jax
import jax.numpy as jnp
from jax import lax
from jax.experimental import pallas as pl
from jax.experimental.pallas import tpu as pltpu
from jax.sharding import PartitionSpec as P

PANEL = 512
LANES = 128
TILE = 16
BLOCK = 2 * TILE
AXES = ("pair", "samp")


def offsets(pair_count, core):
    return [e for e in range(2, pair_count) if e % 2 == core] + [1, 0]


def shifted(pair, offset, pair_count, sign=1):
    turn = pair_count // 2
    high = (pair >> 1) + sign * (offset >> 1)
    high = high - turn * (high >= turn) + turn * (high < 0)
    return high * 2 + ((pair ^ offset) & 1)


def wave_rows(stats, samples):
    return -(-stats * 2 * samples // LANES // 8) * 8


def spread(pheno, perms, first, rows):
    genes, s_dev = pheno.shape
    samples = perms.shape[1]
    pheno = pheno.astype(jnp.float32)
    perms = perms - first
    perms = jnp.concatenate([perms, perms], axis=1)
    tiles = []
    for g in range(genes):
        drawn = jnp.zeros(perms.shape, jnp.float32)
        for s in range(s_dev):
            drawn = jnp.where(perms == s, pheno[g : g + 1, s : s + 1], drawn)
        tiles += [drawn[r : r + 1, t : t + LANES] for r in range(perms.shape[0]) for t in range(0, 2 * samples, LANES)]
    if rows > len(tiles):
        tiles.append(jnp.zeros((rows - len(tiles), LANES), jnp.float32))
    return jnp.concatenate(tiles, axis=0)


def pick_kernel(
    pair_count, samps, pairs_hbm, grid_hbm, pheno_hbm, perms_hbm, keep_ref, pick_ref, wave_ref, perms_ref, pairs_ref, grid_ref, pheno_ref, sems
):
    fetched = ((grid_hbm, grid_ref), (pairs_hbm, pairs_ref), (pheno_hbm, pheno_ref), (perms_hbm, perms_ref))
    copies = [pltpu.make_async_copy(source, target, sems.at[i]) for i, (source, target) in enumerate(fetched)]
    for copy in copies:
        copy.start()
    pair, samp = lax.axis_index("pair"), lax.axis_index("samp")
    shape = (TILE, pick_ref.shape[1])
    ahead = lax.broadcasted_iota(jnp.int32, shape, 1) - lax.broadcasted_iota(jnp.int32, shape, 0)
    for copy in copies:
        copy.wait()
    wave = spread(pheno_ref[...], perms_ref[...], (pair * samps + samp) * pheno_ref.shape[1], wave_ref.shape[0])
    wave_ref[...] = wave.astype(wave_ref.dtype)
    for i, (even, odd) in enumerate(zip(offsets(pair_count, 0), offsets(pair_count, 1))):
        n = shifted(pair, jnp.where(samp == 0, even, odd), pair_count)
        for j in range(2):
            start = pl.multiple_of(pairs_ref[j, n] * TILE, TILE)
            rows = slice(i * BLOCK + j * TILE, i * BLOCK + (j + 1) * TILE)
            keep_ref[rows, :] = grid_ref[pl.ds(start, TILE), :]
            pick_ref[rows, :] = jnp.where(ahead == start, 1.0, 0.0).astype(pick_ref.dtype)


def join_kernel(pair_count, samps, keep_ref, pick_ref, wave_ref, perms_ref, grid_ref, pheno_ref, mate_ref, both_ref, *out_refs):
    pair, samp = lax.axis_index("pair"), lax.axis_index("samp")
    first = (pair * samps + samps - 1 - samp) * pheno_ref.shape[1]
    wave = spread(pheno_ref[...], perms_ref[...], first, wave_ref.shape[0])
    wave = (wave_ref[...].astype(jnp.float32) + wave).astype(wave_ref.dtype)
    both_ref[...] = wave
    picked = jnp.dot(pick_ref[...], grid_ref[...], preferred_element_type=jnp.float32).astype(mate_ref.dtype)
    for i, ref in enumerate(out_refs):
        rows = slice(i * BLOCK, (i + 1) * BLOCK)
        ref[:BLOCK, :] = keep_ref[rows, :]
        ref[BLOCK : 2 * BLOCK, :] = picked[rows]
        ref[2 * BLOCK :, :] = wave
    mate_ref[...] = picked[len(out_refs) * BLOCK :]


def stat_kernel(pair_count, samps, wave_ref, keep_ref, mate_self_ref, near_ref, *refs):
    far = pair_count // 2 - 1
    own_refs, mate_refs = refs[:far], refs[far : 2 * far]
    out_hbm, got_ref, out_ref, sems = refs[2 * far :]
    pair, samp = lax.axis_index("pair"), lax.axis_index("samp")
    other = samps - 1 - samp

    def place(offset, core, block):
        got_ref[shifted(pair, offset, pair_count, -1) * samps + core] = block

    even, odd = offsets(pair_count, 0), offsets(pair_count, 1)
    for arrived, core in ((own_refs, samp), (mate_refs, other)):
        for i, ref in enumerate(arrived):
            offset = jnp.where(core == 0, even[i], odd[i])
            place(offset, core, ref[:BLOCK, :])
            place(offset, samps - 1 - core, ref[BLOCK : 2 * BLOCK, :])
    place(even[far], samp, near_ref[:BLOCK, :])
    place(even[far], other, near_ref[BLOCK : 2 * BLOCK, :])
    itself = (far + 1) * BLOCK
    place(0, samp, keep_ref[itself : itself + BLOCK, :])
    place(0, other, mate_self_ref[...])

    sources = got_ref.shape[0]
    s_dev = TILE * LANES // PANEL
    samples = sources * s_dev

    def by_samples(tiles):
        groups = tiles.shape[1] // s_dev
        if groups * s_dev != 8 or groups != 2:
            return [tiles[:, g * s_dev : (g + 1) * s_dev, :].reshape(samples, LANES) for g in range(groups)]
        couples = tiles.reshape(sources // 2, 2, 8, LANES)
        one, two = couples[:, 0], couples[:, 1]
        upper = lax.broadcasted_iota(jnp.int32, one.shape, 1) < s_dev
        first = jnp.where(upper, one, pltpu.roll(two, s_dev, 1))
        second = jnp.where(upper, pltpu.roll(one, s_dev, 1), two)
        return [x.reshape(samples, LANES) for x in (first, second)]

    panel_a = got_ref[:, 0:TILE, :].astype(jnp.float32)
    panel_b = got_ref[:, TILE:BLOCK, :].astype(jnp.float32)
    tile_b = jnp.where(samp == 0, panel_b[:, : TILE // 2], panel_b[:, TILE // 2 :])

    count = jnp.float32(samples)
    geno_b = jnp.concatenate(by_samples(tile_b), axis=1)
    marg_b = jnp.sum(geno_b, axis=0, keepdims=True)
    centred = (geno_b - marg_b / count) * (samples**-0.5)
    wave = wave_ref[...].astype(jnp.float32)
    for ref in (*own_refs, *mate_refs, near_ref):
        wave = wave + ref[2 * BLOCK :, :].astype(jnp.float32)
    tiles = 2 * samples // LANES
    stats = out_ref.shape[0]
    yrows = [
        jnp.concatenate([wave[k * tiles + t : k * tiles + t + 1] for t in range(tiles)], axis=1) for k in range(stats)
    ]
    yrows.append(jnp.zeros((8 * -(-stats // 8) - stats, 2 * samples), jnp.float32))
    ycolumns = jnp.concatenate(yrows, axis=0).T
    rights = []
    for k in range(stats):
        products = ycolumns[:samples, k : k + 1] * centred
        products = products - jnp.sum(products, axis=0, keepdims=True) / count
        high = products.astype(jnp.bfloat16)
        low = (products - high.astype(jnp.float32)).astype(jnp.bfloat16)
        rights.append(jnp.concatenate([high, low], axis=0))
    right = jnp.concatenate(rights, axis=1)
    half = out_ref.shape[2]
    copies = []
    for q, geno_a in enumerate(by_samples(panel_a[:, : TILE // 2]) + by_samples(panel_a[:, TILE // 2 :])):
        left = jnp.concatenate([geno_a, geno_a], axis=0).astype(jnp.bfloat16).T
        piece = slice(q * LANES, (q + 1) * LANES)
        for k in range(stats):
            part = jnp.dot(left, right[:, k * half : (k + 1) * half], preferred_element_type=jnp.float32)
            out_ref[k, piece, :] = part.astype(out_ref.dtype)
        copies.append(pltpu.make_async_copy(out_ref.at[:, piece], out_hbm.at[0, :, piece], sems.at[q]))
        copies[-1].start()
    for copy in copies:
        copy.wait()


def on_device(dosage, phenotype, perms, pairs):
    s_dev, snps = dosage.shape
    genes = phenotype.shape[0]
    samples = perms.shape[1]
    pair_count, samps = (lax.axis_size(axis) for axis in AXES)
    rounds = pair_count // 2 + 1
    stats = genes * perms.shape[0]
    rows = wave_rows(stats, samples)
    grid = dosage.reshape(s_dev, snps // LANES, LANES).transpose(1, 0, 2).reshape(-1, LANES)
    vmem = pl.BlockSpec(memory_space=pltpu.VMEM)
    hbm = pl.BlockSpec(memory_space=pltpu.HBM)

    def array(*shape):
        return jax.ShapeDtypeStruct(shape, dosage.dtype)

    swap = [(i, samps - 1 - i) for i in range(samps)]
    mate_dosage = lax.ppermute(dosage, "samp", swap)
    mate_pheno = lax.ppermute(phenotype, "samp", swap)
    params = pltpu.CompilerParams(vmem_limit_bytes=24 * 1024 * 1024)
    blocks = rounds * BLOCK
    keep, pick, wave, perms_near = pl.pallas_call(
        functools.partial(pick_kernel, pair_count, samps),
        out_shape=[
            array(blocks, LANES),
            array(blocks, grid.shape[0]),
            array(rows, LANES),
            jax.ShapeDtypeStruct(perms.shape, perms.dtype),
        ],
        in_specs=[hbm] * 4,
        out_specs=[vmem] * 4,
        scratch_shapes=[
            pltpu.SMEM(pairs.shape[::-1], pairs.dtype),
            pltpu.VMEM(grid.shape, grid.dtype),
            pltpu.VMEM(phenotype.shape, phenotype.dtype),
            pltpu.SemaphoreType.DMA((4,)),
        ],
        compiler_params=params,
        cost_estimate=pl.CostEstimate(flops=0, bytes_accessed=4 * blocks * LANES * 2, transcendentals=0),
        name="pick",
    )(*[pltpu.with_memory_space_constraint(x, pltpu.HBM) for x in (pairs.T, grid, phenotype, perms)])

    mate_grid = mate_dosage.reshape(s_dev, snps // LANES, LANES).transpose(1, 0, 2).reshape(-1, LANES)
    mate_self, wave, *messages = pl.pallas_call(
        functools.partial(join_kernel, pair_count, samps),
        out_shape=[array(BLOCK, LANES), array(rows, LANES)] + [array(2 * BLOCK + rows, LANES)] * (rounds - 1),
        in_specs=[vmem] * 6,
        out_specs=[vmem] * (rounds + 1),
        compiler_params=params,
        name="join",
    )(keep, pick, wave, perms_near, mate_grid, mate_pheno)

    arrived = []
    for i, message in enumerate(messages):
        route = [
            (p * samps + c, shifted(p, offsets(pair_count, c)[i], pair_count) * samps + c)
            for p in range(pair_count)
            for c in range(samps)
        ]
        arrived.append(lax.ppermute(message, AXES, route))
    *far, near = arrived
    mates = [lax.ppermute(a, "samp", swap) for a in far]
    half = PANEL // samps
    return pl.pallas_call(
        functools.partial(stat_kernel, pair_count, samps),
        out_shape=jax.ShapeDtypeStruct((1, stats, PANEL, half), jnp.bfloat16),
        in_specs=[vmem] * (4 + 2 * len(far)),
        out_specs=hbm,
        scratch_shapes=[
            pltpu.VMEM((pair_count * samps, BLOCK, LANES), dosage.dtype),
            pltpu.VMEM((stats, PANEL, half), jnp.bfloat16),
            pltpu.SemaphoreType.DMA((PANEL // LANES,)),
        ],
        compiler_params=pltpu.CompilerParams(vmem_limit_bytes=48 * 1024 * 1024),
        name="stat",
    )(wave, keep, mate_self, near, *far, *mates)


def solution(mesh):
    placed = (P(("rep", "pair", "samp"), None), P(None, ("rep", "pair", "samp")), P(), P())
    return jax.shard_map(
        on_device,
        mesh=mesh,
        in_specs=placed,
        out_specs=P(("rep", "pair"), None, None, "samp"),
        check_vma=False,
    )
```
